128 devices in a mesh: rows: 64 (over z, x, y), sub: 2 (over core).
Axes of the slice: x: 4, y: 4, z: 4, core: 2. Of those that a mesh axis runs over, the one named last changes fastest.
Arguments:
- points: bfloat16 [49152, 128], P('rows'), may hold values from -5 to 5, as said below
- old_factor: float32 [49152, 512], P('rows', 'sub'), may hold values from -0.039774756 to 0.039774756
- targets: float32 [49152], P('rows'), may hold values from -6 to 6
- pivots: int32 [512], replicated, may hold values from 0 to 49151, as said below
Outputs:
- new_factor: float32 [49152, 512], P('rows', 'sub')
- solution: float32 [49152], P('rows')
- residual: float32 [49152], P('rows')
- preconditioned: float32 [49152], P('rows')
The draws below stay inside these ranges and needn't reach their ends.
Inputs may be any that keep to these rules, and one draw needn't show every extreme that they name: `points`: cluster centres plus small per-point offsets. `pivots`: 512 distinct point indices.
All inputs are finite; a program needn't handle non-finite values.
Results may differ from the reference program's by a relative error of at most 0.0018.
Values may be sent and summed in bfloat16 or wider, within the bound.
No kernel may reach another device: no remote copies, remote signals or barrier semaphores. Data moves between devices by JAX's collectives and lax.ppermute only.
A program may use at most 128 MiB of HBM per device.

```python
import jax
import jax.numpy as jnp
from jax import lax

DIM = 128
ROWS_DEV = 768
PIV = 512
PREV = 512
CLUSTER = 256
RANK = 1024
NPTS = 49152


def draw_points(key, part):
    key = jax.random.fold_in(key, 11)
    center_key, label_key, noise_key = jax.random.split(key, 3)
    centers = jax.random.truncated_normal(center_key, -4.0, 4.0, (NPTS // CLUSTER, DIM), jnp.float32)
    labels = jax.random.randint(label_key, (NPTS,), 0, NPTS // CLUSTER)
    noise = 0.25 * jax.random.truncated_normal(noise_key, -4.0, 4.0, (NPTS, DIM), jnp.float32)
    return (centers[labels] + noise).astype(jnp.bfloat16)


def draw_old_factor(key, part):
    key = jax.random.fold_in(key, 31)
    entry_key = jax.random.fold_in(key, 0)
    factor_scale = 0.45 / (PIV ** 0.5 + PREV ** 0.5)
    entries = jax.random.truncated_normal(entry_key, -4.0, 4.0, (NPTS, PREV), jnp.float32)
    return (entries * factor_scale).astype(jnp.float32)


def draw_pivots(key, part):
    key = jax.random.fold_in(key, 23)
    inner_key, order_key = jax.random.split(key, 2)
    middle = jax.random.permutation(inner_key, NPTS - 2)[:PIV - 2].astype(jnp.int32) + 1
    ends = jnp.array([0, NPTS - 1], dtype=jnp.int32)
    chosen = jnp.concatenate([middle, ends])
    return jax.random.permutation(order_key, chosen).astype(jnp.int32)


def steps_of(key, shape, pieces, least, high):
    def one(dim, shards_of):
        steps = jax.random.uniform(jax.random.fold_in(jax.random.fold_in(key, 6), dim), (shards_of,), jnp.float32, least / len(pieces), high / len(pieces))
        return jnp.repeat(jnp.exp(steps), shape[dim] // shards_of).reshape((-1,) + (1,) * (len(shape) - dim - 1))

    factor_of = one(*pieces[0])
    for cut in pieces[1:]:
        factor_of = factor_of * one(*cut)
    return factor_of


def centred(key, shape, scale, limit, cuts=(), kind=jnp.bfloat16):
    loudness = steps_of(key, shape, cuts, -0.22, 0.18) if cuts else 1.0
    values = jax.random.normal(key, shape, jnp.float32) * scale * loudness
    return jnp.minimum(jnp.maximum(values, -limit), limit).astype(kind)


def setup_inputs(seed: int = 0) -> dict:
    key_of = jax.random.split(jax.random.key(seed), 5)
    points = draw_points(jax.random.fold_in(key_of[4], 71), 0)
    old_factor = draw_old_factor(jax.random.fold_in(key_of[4], 71), 0)
    targets = centred(key_of[2], (NPTS,), 1.0, 6.0, ((0, 64),), jnp.float32)
    pivots = draw_pivots(jax.random.fold_in(key_of[4], 71), 0)
    return dict(points=points, old_factor=old_factor, targets=targets, pivots=pivots)


ridge_shift = 0.5
precise = lax.Precision.HIGHEST

def kernel_block(left, left_norms, right, right_norms):
    inner = jnp.dot(left, right.T, precision=precise)
    dist = jnp.maximum(left_norms[:, None] + right_norms[None, :] - 2.0 * inner, 0.0)
    return jnp.exp(-(2.0 / left.shape[1]) * dist)

def precondition(vector, factor, core_lower, projection):
    coef = jax.scipy.linalg.cho_solve((core_lower, True), projection)
    return (vector - jnp.dot(factor, coef, precision=precise)) / ridge_shift

def reference(points, old_factor, targets, pivots):
    wide = points.astype(jnp.float32)
    norms = jnp.sum(wide * wide, axis=1)
    pivot_points = wide[pivots]
    pivot_norms = norms[pivots]
    pivot_old = old_factor[pivots]
    columns = kernel_block(wide, norms, pivot_points, pivot_norms) - jnp.dot(old_factor, pivot_old.T, precision=precise)
    block = columns[pivots] + ridge_shift * jnp.eye(PIV, dtype=jnp.float32)
    lower = jnp.linalg.cholesky(block)
    inverse = jax.scipy.linalg.solve_triangular(lower, jnp.eye(PIV, dtype=jnp.float32), lower=True)
    new_factor = jnp.dot(columns, inverse.T, precision=precise)
    factor = jnp.concatenate([old_factor, new_factor], axis=1)
    core = ridge_shift * jnp.eye(RANK, dtype=jnp.float32) + jnp.dot(factor.T, factor, precision=precise)
    core_lower = jnp.linalg.cholesky(core)
    direction = precondition(targets, factor, core_lower, jnp.dot(targets, factor, precision=precise))
    blocks = wide.reshape(NPTS // ROWS_DEV, ROWS_DEV, DIM)
    norm_blocks = norms.reshape(NPTS // ROWS_DEV, ROWS_DEV)

    def apply_rows(pair):
        return jnp.dot(kernel_block(pair[0], pair[1], wide, norms), direction, precision=precise)
    image = lax.map(apply_rows, (blocks, norm_blocks)).reshape(NPTS) + ridge_shift * direction
    alpha = jnp.sum(direction * targets) / jnp.sum(direction * image)
    solution = alpha * direction
    residual = targets - alpha * image
    preconditioned = precondition(residual, factor, core_lower, jnp.dot(residual, factor, precision=precise))
    return (new_factor, solution, residual, preconditioned)
```

```python
import math

import jax
import jax.numpy as jnp
from jax import lax
from jax.experimental import pallas as pl
from jax.experimental.pallas import tpu as pltpu
from jax.sharding import PartitionSpec as P

ridge_shift = 0.5
precise = lax.Precision.HIGHEST
everyone = ("rows", "sub")
f32, bf16 = jnp.float32, jnp.bfloat16


def factor_blocks(mats):
    lane = lax.broadcasted_iota(jnp.int32, (8, 128), 1)
    sub = lax.broadcasted_iota(jnp.int32, (8, 128), 0)
    outs = [[] for _ in mats]
    state = list(mats)
    for panel in range(16):
        lo = 8 * panel
        inside = (lane >= lo) & (lane < lo + 8)
        unit = (lane == lo + sub).astype(jnp.float32)
        cols = [[jnp.broadcast_to(a[:, lo + j:lo + j + 1], a.shape) for j in range(8)] for a in state]
        heads = [jnp.where(inside, unit, a[:8]) for a in state]
        scales = [jnp.zeros((8, 128), jnp.float32) for a in state]
        tails = [[] for _ in state]
        for j in range(8):
            for m in range(len(state)):
                col = cols[m][j]
                pivot = jnp.broadcast_to(col[j:j + 1], (8, 128))
                recip = 1.0 / pivot
                scales[m] = jnp.where(sub == j, lax.rsqrt(pivot), scales[m])
                top = jnp.where(sub > j, col[:8] * recip, 0.0)
                rest = col[8:] * recip[:1] if col.shape[0] > 8 else None
                for later in range(j + 1, 8):
                    row = cols[m][later][j:j + 1]
                    new = cols[m][later][:8] - top * row
                    if rest is not None:
                        new = jnp.concatenate([new, cols[m][later][8:] - rest * row], 0)
                    cols[m][later] = new
                heads[m] = heads[m] - top * heads[m][j:j + 1]
                tails[m].append(rest)
        for m in range(len(state)):
            outs[m].append(heads[m] * scales[m])
            if panel < 15:
                a = state[m][8:]
                inside_all = jnp.broadcast_to(inside[:1], a.shape)
                a = jnp.where(inside_all, 0.0, a)
                for j in range(8):
                    a = a - tails[m][j] * heads[m][j:j + 1]
                state[m] = a
    low = lax.broadcasted_iota(jnp.int32, (128, 128), 0) >= lax.broadcasted_iota(jnp.int32, (128, 128), 1)
    return [jnp.where(low, jnp.concatenate(o, 0), 0.0) for o in outs]

def chol_inverse(refs, size):
    rows = lax.broadcasted_iota(jnp.int32, (size, size), 0)
    colid = lax.broadcasted_iota(jnp.int32, (size, size), 1)
    crow = lax.broadcasted_iota(jnp.int32, (128, size), 1)
    def step(k, carry):
        off = pl.multiple_of(k * 128, 128)
        here = pl.ds(off, 128)
        invs = factor_blocks([r[here, here] for r in refs])
        inside = (crow >= off) & (crow < off + 128)
        inside_all = (colid >= off) & (colid < off + 128)
        for r, inv in zip(refs, invs):
            left = lax.dot_general(r[:, here], inv, (((1,), (1,)), ((), ())), precision=precise, preferred_element_type=jnp.float32)
            r[here, here] = inv
            head = jnp.dot(inv, jnp.where(inside, 0.0, r[here, :]), precision=precise, preferred_element_type=jnp.float32)
            r[here, :] = head
            r[here, here] = inv
            upd = jnp.dot(left, r[here, :], precision=precise, preferred_element_type=jnp.float32)
            old = r[...]
            r[...] = jnp.where(rows >= off + 128, jnp.where(inside_all, 0.0, old) - upd, old)
        return carry
    lax.fori_loop(0, size // 128, step, 0)
    for r in refs:
        r[...] = jnp.where(rows >= colid, r[...], 0.0)


def pair_kernel(first_in, second_in, first_out, second_out):
    first_out[...] = first_in[...]
    second_out[...] = second_in[...]
    chol_inverse([first_out, second_out], first_in.shape[0])


def single_kernel(matrix, out):
    out[...] = matrix[...]
    chol_inverse([out], matrix.shape[0])


def factor_pair(first, second):
    shape = jax.ShapeDtypeStruct(first.shape, f32)
    return pl.pallas_call(
        pair_kernel,
        out_shape=(shape, shape),
        compiler_params=pltpu.CompilerParams(vmem_limit_bytes=40 << 20),
        name="factor_pair",
    )(first, second)


def factor_single(matrix):
    return pl.pallas_call(
        single_kernel,
        out_shape=jax.ShapeDtypeStruct(matrix.shape, f32),
        compiler_params=pltpu.CompilerParams(vmem_limit_bytes=40 << 20),
        name="factor_single",
    )(matrix)


def rows_kernel(scale, left, points, shifts, weights, out, acc):
    @pl.when(pl.program_id(0) == 0)
    def _():
        acc[...] = jnp.zeros_like(acc)

    lane = lax.broadcasted_iota(jnp.int32, (256, 128), 1)
    ones = jnp.where(lane < 3, 1.0, 0.0).astype(bf16)
    total = acc[...]
    for tile in range(points.shape[0] // 256):
        here = slice(256 * tile, 256 * tile + 256)
        right = jnp.concatenate([points[here], ones], axis=1)
        inner = lax.dot_general(left[...], right, (((1,), (1,)), ((), ())), preferred_element_type=f32)
        value = jnp.exp2(jnp.minimum(inner * scale + shifts[:, here], 0.0)) * weights[:, here]
        total = total + (value[:, :128] + value[:, 128:])
    acc[...] = total

    @pl.when(pl.program_id(0) == pl.num_programs(0) - 1)
    def _():
        ones_row = jnp.ones((8, 128), f32)
        out[...] = lax.dot_general(
            ones_row, acc[...], (((1,), (1,)), ((), ())), precision=precise, preferred_element_type=f32
        )


def kernel_rows(points, norms, others, other_norms, weights):
    count, dim = points.shape
    scale = 2.0 * (2.0 / dim) * math.log2(math.e)
    half_norms = -0.5 * norms
    pieces = []
    for _ in range(3):
        piece = lax.reduce_precision(half_norms, 8, 7)
        pieces.append(piece.astype(bf16))
        half_norms = half_norms - piece
    extra = jnp.pad(jnp.stack(pieces, axis=1), ((0, 0), (0, dim - 3)))
    left = jnp.concatenate([points, extra], axis=1)
    shifts = (-0.5 * scale) * other_norms
    total = others.shape[0]
    steps = 8
    size = total // steps
    out = pl.pallas_call(
        lambda *refs: rows_kernel(scale, *refs),
        grid=(steps,),
        in_specs=[
            pl.BlockSpec((count, 2 * dim), lambda i: (0, 0)),
            pl.BlockSpec((size, dim), lambda i: (i, 0)),
            pl.BlockSpec((1, size), lambda i: (0, i)),
            pl.BlockSpec((1, size), lambda i: (0, i)),
        ],
        out_specs=pl.BlockSpec((8, count), lambda i: (0, 0)),
        out_shape=jax.ShapeDtypeStruct((8, count), f32),
        scratch_shapes=[pltpu.VMEM((count, 128), f32)],
        compiler_params=pltpu.CompilerParams(vmem_limit_bytes=40 << 20),
        name="kernel_rows",
    )(left, others, shifts[None], weights[None])
    return out[0]


def kernel_values(left, left_norms, right, right_norms):
    inner = lax.dot_general(left, right, (((1,), (1,)), ((), ())), preferred_element_type=f32)
    dist = jnp.maximum(left_norms[:, None] + right_norms[None, :] - 2.0 * inner, 0.0)
    return jnp.exp(-(2.0 / left.shape[1]) * dist)


def point_norms(rows):
    wide = rows.astype(f32)
    return jnp.sum(wide * wide, axis=1)


def dot(left, right, contract):
    return lax.dot_general(left, right, (contract, ((), ())), precision=precise, preferred_element_type=f32)


def exchange(pieces):
    return lax.all_to_all(pieces, everyone, 0, 0, tiled=True)


def spread(piece, parts):
    return exchange(jnp.broadcast_to(piece.reshape(1, -1), (parts, piece.size)))


def swap(value):
    return lax.ppermute(value, "sub", [(0, 1), (1, 0)])


def both(mine, part, axis):
    other = swap(mine)
    first = jnp.where(part == 0, mine, other)
    second = jnp.where(part == 0, other, mine)
    return jnp.concatenate([first, second], axis=axis)


def split(value):
    high = lax.reduce_precision(value, 8, 7)
    return high.astype(bf16), (value - high).astype(bf16)


def local(points, old_factor, targets, pivots):
    count, dim = points.shape
    pivot_count = pivots.shape[0]
    prev = 2 * old_factor.shape[1]
    part = lax.axis_index("sub")
    chips = lax.axis_size("rows")
    parts = 2 * chips
    half = count // 2
    each = pivot_count // parts
    first = lax.axis_index("rows") * count
    norms = point_norms(points)
    others = lax.all_gather(
        lax.dynamic_slice_in_dim(points, part * half, half, 0), "rows", axis=0, tiled=True
    )

    picks = (pivots[:, None] == (first + lax.iota(jnp.int32, count))[None, :]).astype(bf16)
    high, low = split(old_factor)
    my_points = lax.dynamic_slice_in_dim(points, part * (dim // 2), dim // 2, 1)
    wanted = jnp.concatenate([my_points, high, low], axis=1)
    picked = lax.dot_general(picks, wanted, (((1,), (0,)), ((), ())), preferred_element_type=f32)
    width = wanted.shape[1]
    came = exchange(picked.astype(bf16).reshape(parts, each * width))
    came = jnp.sum(came.reshape(chips, 2, each, width).astype(f32), axis=0).astype(bf16)
    kept = jnp.concatenate([came[0], came[1]], axis=1)
    pivot_rows = spread(kept, parts).reshape(pivot_count, 2 * width)
    cols = old_factor.shape[1]
    pivot_points = jnp.concatenate(
        [pivot_rows[:, : dim // 2], pivot_rows[:, width : width + dim // 2]], axis=1
    )

    def pivot_half(start):
        start = start + dim // 2
        return pivot_rows[:, start : start + cols].astype(f32) + pivot_rows[
            :, start + cols : start + 2 * cols
        ].astype(f32)

    pivot_old = jnp.concatenate([pivot_half(0), pivot_half(width)], axis=1)
    pivot_norms = point_norms(pivot_points)

    old_full = both(old_factor, part, 1)
    old_gram = dot(old_full, old_factor, ((0,), (0,)))
    old_gram = exchange(old_gram.reshape(parts, -1))
    old_gram = jnp.sum(old_gram.reshape(chips, 2, -1), axis=0)
    old_gram = spread(old_gram, parts).reshape(parts, 2, prev // parts, cols)
    old_gram = jnp.concatenate(
        [old_gram[:, 0].reshape(prev, cols), old_gram[:, 1].reshape(prev, cols)], axis=1
    )
    old_core = old_gram + ridge_shift * jnp.eye(prev, dtype=f32)

    columns = kernel_values(points, norms, pivot_points, pivot_norms) - dot(
        old_full, pivot_old, ((1,), (1,))
    )
    block = kernel_values(pivot_points, pivot_norms, pivot_points, pivot_norms) - dot(
        pivot_old, pivot_old, ((1,), (1,))
    )
    block = block + ridge_shift * jnp.eye(pivot_count, dtype=f32)

    side = jnp.where(part == 0, old_full, columns)
    gram = dot(side, columns, ((0,), (0,)))
    proj = jnp.sum(side * targets[:, None], axis=0)
    pad = 128 - prev // parts
    sent = jnp.concatenate(
        [gram.reshape(parts, -1), jnp.pad(proj.reshape(parts, -1), ((0, 0), (0, pad)))], axis=1
    )
    size = sent.shape[1]
    came = jnp.sum(exchange(sent).reshape(chips, 2, size), axis=0)
    came = exchange(jnp.broadcast_to(came[None], (chips, 2, size)).reshape(parts, size))
    came = both(came[None], part, 0)
    grams = came[:, :, : size - 128].reshape(2, prev, pivot_count)
    projs = came[:, :, size - 128 : size - pad].reshape(2, prev)
    cross, square = grams[0], grams[1]
    old_proj, new_proj = projs[0], projs[1]

    old_inverse, block_inverse = factor_pair(old_core, block)
    cross_low = dot(old_inverse, cross, ((1,), (0,)))
    schur = ridge_shift * block + square - dot(cross_low, cross_low, ((0,), (0,)))
    schur_inverse = factor_single(schur)

    def solve(old_side, new_side):
        up = dot(old_inverse, old_side, ((1,), (0,)))
        down = dot(schur_inverse, new_side - dot(cross_low, up, ((0,), (0,))), ((1,), (0,)))
        new_coef = dot(schur_inverse, down, ((0,), (0,)))
        old_coef = dot(old_inverse, up - dot(cross_low, new_coef, ((1,), (0,))), ((0,), (0,)))
        return old_coef, new_coef

    def apply(vector, coefs):
        fitted = dot(old_full, coefs[0], ((1,), (0,))) + dot(columns, coefs[1], ((1,), (0,)))
        return (vector - fitted) / ridge_shift

    direction = apply(targets, solve(old_proj, new_proj))
    weights = spread(lax.dynamic_slice_in_dim(direction, part * half, half, 0), parts)
    weights = lax.dynamic_index_in_dim(weights.reshape(chips, 2, half), part, 1, False)
    rows_part = kernel_rows(points, norms, others, point_norms(others), weights.reshape(-1))

    image_part = rows_part + (0.5 * ridge_shift) * direction
    sums = jnp.concatenate(
        [
            dot(image_part, old_full, ((0,), (0,))),
            dot(image_part, columns, ((0,), (0,))),
            jnp.sum(direction * image_part)[None],
            0.5 * jnp.sum(direction * targets)[None],
            jnp.zeros((126,), f32),
        ]
    )
    sums = jnp.sum(spread(sums, parts), axis=0)
    image = rows_part + swap(rows_part) + ridge_shift * direction
    alpha = sums[prev + pivot_count + 1] / sums[prev + pivot_count]
    residual = targets - alpha * image
    coefs = solve(old_proj - alpha * sums[:prev], new_proj - alpha * sums[prev : prev + pivot_count])
    preconditioned = apply(residual, coefs)
    mine = lax.dynamic_slice_in_dim(block_inverse, part * cols, cols, 0)
    new_part = dot(columns, mine, ((1,), (1,)))
    return new_part, alpha * direction, residual, preconditioned


def solution(mesh):
    in_specs = (P("rows", None), P("rows", "sub"), P("rows"), P())
    out_specs = (P("rows", "sub"), P("rows"), P("rows"), P("rows"))
    return jax.shard_map(local, mesh=mesh, in_specs=in_specs, out_specs=out_specs, check_vma=False)
```

```python
import math

import jax
import jax.numpy as jnp
from jax import lax
from jax.experimental import pallas as pl
from jax.experimental.pallas import tpu as pltpu
from jax.sharding import PartitionSpec as P

ridge_shift = 0.5
precise = lax.Precision.HIGHEST
everyone = ("rows", "sub")
f32, bf16 = jnp.float32, jnp.bfloat16
whole = pl.BlockSpec(memory_space=pltpu.VMEM)
scalar = pl.BlockSpec(memory_space=pltpu.SMEM)
params = pltpu.CompilerParams(vmem_limit_bytes=48 << 20)


def dot(left, right, contract):
    return lax.dot_general(left, right, (contract, ((), ())), precision=precise, preferred_element_type=f32)


def narrow_dot(left, right):
    return lax.dot_general(left, right, (((1,), (1,)), ((), ())), preferred_element_type=f32)


def factor_blocks(mats):
    lane = lax.broadcasted_iota(jnp.int32, (8, 128), 1)
    sub = lax.broadcasted_iota(jnp.int32, (8, 128), 0)
    outs = [[] for _ in mats]
    state = list(mats)
    for panel in range(16):
        lo = 8 * panel
        inside = (lane >= lo) & (lane < lo + 8)
        unit = (lane == lo + sub).astype(jnp.float32)
        cols = [[jnp.broadcast_to(a[:, lo + j:lo + j + 1], a.shape) for j in range(8)] for a in state]
        heads = [jnp.where(inside, unit, a[:8]) for a in state]
        scales = [jnp.zeros((8, 128), jnp.float32) for a in state]
        tails = [[] for _ in state]
        for j in range(8):
            for m in range(len(state)):
                col = cols[m][j]
                pivot = jnp.broadcast_to(col[j:j + 1], (8, 128))
                recip = 1.0 / pivot
                scales[m] = jnp.where(sub == j, lax.rsqrt(pivot), scales[m])
                top = jnp.where(sub > j, col[:8] * recip, 0.0)
                rest = col[8:] * recip[:1] if col.shape[0] > 8 else None
                for later in range(j + 1, 8):
                    row = cols[m][later][j:j + 1]
                    new = cols[m][later][:8] - top * row
                    if rest is not None:
                        new = jnp.concatenate([new, cols[m][later][8:] - rest * row], 0)
                    cols[m][later] = new
                heads[m] = heads[m] - top * heads[m][j:j + 1]
                tails[m].append(rest)
        for m in range(len(state)):
            outs[m].append(heads[m] * scales[m])
            if panel < 15:
                a = state[m][8:]
                inside_all = jnp.broadcast_to(inside[:1], a.shape)
                a = jnp.where(inside_all, 0.0, a)
                for j in range(8):
                    a = a - tails[m][j] * heads[m][j:j + 1]
                state[m] = a
    low = lax.broadcasted_iota(jnp.int32, (128, 128), 0) >= lax.broadcasted_iota(jnp.int32, (128, 128), 1)
    return [jnp.where(low, jnp.concatenate(o, 0), 0.0) for o in outs]

def chol_inverse(refs, size):
    rows = lax.broadcasted_iota(jnp.int32, (size, size), 0)
    colid = lax.broadcasted_iota(jnp.int32, (size, size), 1)
    crow = lax.broadcasted_iota(jnp.int32, (128, size), 1)
    def step(k, carry):
        off = pl.multiple_of(k * 128, 128)
        here = pl.ds(off, 128)
        invs = factor_blocks([r[here, here] for r in refs])
        inside = (crow >= off) & (crow < off + 128)
        inside_all = (colid >= off) & (colid < off + 128)
        for r, inv in zip(refs, invs):
            left = lax.dot_general(r[:, here], inv, (((1,), (1,)), ((), ())), precision=precise, preferred_element_type=jnp.float32)
            r[here, here] = inv
            head = jnp.dot(inv, jnp.where(inside, 0.0, r[here, :]), precision=precise, preferred_element_type=jnp.float32)
            r[here, :] = head
            r[here, here] = inv
            upd = jnp.dot(left, r[here, :], precision=precise, preferred_element_type=jnp.float32)
            old = r[...]
            r[...] = jnp.where(rows >= off + 128, jnp.where(inside_all, 0.0, old) - upd, old)
        return carry
    lax.fori_loop(0, size // 128, step, 0)
    for r in refs:
        r[...] = jnp.where(rows >= colid, r[...], 0.0)


def factor_kernel(matrix, out):
    out[...] = matrix[...]
    chol_inverse([out], matrix.shape[0])


def factor(matrix):
    size = matrix.shape[0]
    return pl.pallas_call(
        factor_kernel,
        out_shape=jax.ShapeDtypeStruct(matrix.shape, f32),
        in_specs=[whole],
        out_specs=whole,
        compiler_params=params,
        cost_estimate=pl.CostEstimate(flops=120 * size**3, bytes_accessed=8 * size**2, transcendentals=0),
        name="factor",
    )(matrix)


def columns_kernel(part, points, pivot_points, old_full, pivot_old, targets, columns, block, gram):
    rate = -2.0 / points.shape[1]
    wide = points[...].astype(f32)
    pivot_wide = pivot_points[...].astype(f32)
    squares = pivot_wide * pivot_wide
    norms = jnp.sum(wide * wide, axis=1, keepdims=True)
    pivot_column = jnp.sum(squares, axis=1, keepdims=True)
    pivot_row = dot(jnp.ones((8, points.shape[1]), f32), squares, ((1,), (1,)))[:1]
    inner = narrow_dot(points[...], pivot_points[...])
    values = jnp.exp(rate * jnp.maximum(norms + pivot_row - 2.0 * inner, 0.0))
    high = old_full[...].astype(bf16)
    low = (old_full[...] - high.astype(f32)).astype(bf16)
    values = values - (narrow_dot(high, pivot_old[...]) + narrow_dot(low, pivot_old[...]))
    columns[...] = values
    inner = narrow_dot(pivot_points[...], pivot_points[...])
    square = jnp.exp(rate * jnp.maximum(pivot_column + pivot_row - 2.0 * inner, 0.0))
    square = square - narrow_dot(pivot_old[...], pivot_old[...])
    size = square.shape[0]
    eye = lax.broadcasted_iota(jnp.int32, (size, size), 0) == lax.broadcasted_iota(jnp.int32, (size, size), 1)
    block[...] = square + jnp.where(eye, ridge_shift, 0.0)

    @pl.when(part[0] == 0)
    def _():
        gram[...] = dot(old_full[...], columns[...], ((0,), (0,)))

    @pl.when(part[0] == 1)
    def _():
        gram[...] = dot(columns[...], columns[...], ((0,), (0,)))
        proj = dot(jnp.broadcast_to(targets[...], (8, targets.shape[1])), columns[...], ((1,), (0,)))
        gram[size - 2 : size - 1, : size // 2] = proj[:1, : size // 2]
        gram[size - 1 : size, : size // 2] = proj[:1, size // 2 :]


def pivot_columns(part, points, pivot_points, old_full, pivot_old, targets):
    count, size = points.shape[0], pivot_points.shape[0]
    return pl.pallas_call(
        columns_kernel,
        out_shape=(
            jax.ShapeDtypeStruct((count, size), f32),
            jax.ShapeDtypeStruct((size, size), f32),
            jax.ShapeDtypeStruct((size, size), f32),
        ),
        in_specs=[scalar] + [whole] * 5,
        out_specs=(whole,) * 3,
        compiler_params=params,
        name="pivot_columns",
    )(part, points, pivot_points, old_full, pivot_old, targets)


def solve(old_inverse, cross_low, schur_inverse, old_side, new_side):
    up = dot(old_side, old_inverse, ((1,), (1,)))
    down = dot(new_side - dot(up, cross_low, ((1,), (0,))), schur_inverse, ((1,), (1,)))
    new_coef = dot(down, schur_inverse, ((1,), (0,)))
    old_coef = dot(up - dot(new_coef, cross_low, ((1,), (1,))), old_inverse, ((1,), (0,)))
    return old_coef, new_coef


def apply(vector, coefs, old_full, columns):
    fitted = dot(coefs[0], old_full, ((1,), (1,))) + dot(coefs[1], columns, ((1,), (1,)))
    return (vector - fitted[:1]) * (1.0 / ridge_shift)


def core_kernel(
    part, old_inverse, block, mine, other, old_proj, old_full, columns, targets,
    cross_low, schur_inverse, new_proj, direction, weights,
):
    size = block.shape[0]
    mid = size // 2
    first = part[0] == 0
    cross = jnp.where(first, mine[...], other[...])
    schur_inverse[...] = jnp.where(first, other[...], mine[...])
    new_proj[:, :mid] = schur_inverse[size - 2 : size - 1, :mid]
    new_proj[:, mid:] = schur_inverse[size - 1 : size, :mid]
    for start in range(0, mid, 128):
        turned = jnp.transpose(schur_inverse[start : start + 128, size - 128 :])
        schur_inverse[size - 2 :, start : start + 128] = turned[126:]
    cross_low[...] = dot(old_inverse[...], cross, ((1,), (0,)))
    schur_inverse[...] = (
        ridge_shift * block[...]
        + schur_inverse[...]
        - dot(cross_low[...], cross_low[...], ((0,), (0,)))
    )
    chol_inverse([schur_inverse], size)
    coefs = solve(
        old_inverse[...], cross_low[...], schur_inverse[...],
        jnp.broadcast_to(old_proj[...], (8, size)), jnp.broadcast_to(new_proj[...], (8, size)),
    )
    value = apply(targets[...], coefs, old_full[...], columns[...])
    direction[...] = value
    half = value.shape[1] // 2
    mine_half = jnp.where(first, value[:, :half], value[:, half:])
    weights[...] = jnp.broadcast_to(mine_half[None], weights.shape)


def core_solve(part, old_inverse, block, mine, other, old_proj, old_full, columns, targets, parts):
    size, count = block.shape[0], columns.shape[0]
    return pl.pallas_call(
        core_kernel,
        out_shape=(
            jax.ShapeDtypeStruct((size, size), f32),
            jax.ShapeDtypeStruct((size, size), f32),
            jax.ShapeDtypeStruct((1, size), f32),
            jax.ShapeDtypeStruct((1, count), f32),
            jax.ShapeDtypeStruct((parts, 1, count // 2), f32),
        ),
        in_specs=[scalar] + [whole] * 8,
        out_specs=(whole,) * 5,
        compiler_params=params,
        name="core_solve",
    )(part, old_inverse, block, mine, other, old_proj, old_full, columns, targets)


def rows_kernel(
    scale, stride, half, part, points, others, weights, old_full, columns, direction, targets,
    rows, sums, left, acc,
):
    count, dim = points.shape
    step = pl.program_id(0)

    @pl.when(step == 0)
    def _():
        acc[...] = jnp.zeros_like(acc)
        wide = points[...].astype(f32)
        rest = -0.5 * jnp.sum(wide * wide, axis=1, keepdims=True)
        lane = lax.broadcasted_iota(jnp.int32, (count, dim), 1)
        extra = jnp.zeros((count, dim), f32)
        for k in range(3):
            piece = rest.astype(bf16).astype(f32)
            extra = jnp.where(lane == k, piece, extra)
            rest = rest - piece
        left[:, :dim] = points[...]
        left[:, dim:] = extra.astype(bf16)

    lane = lax.broadcasted_iota(jnp.int32, (256, dim), 1)
    ones = jnp.where(lane < 3, 1.0, 0.0).astype(bf16)
    groups = half // 128
    chips = others.shape[0] // stride
    total = acc[...]
    for pair in range(chips // 2):
        tiles = []
        for chip in (2 * pair, 2 * pair + 1):
            base = chip * stride
            pieces = others[base + half : base + half + 16, :].astype(f32)
            shift = scale * (pieces[:groups] + pieces[groups : 2 * groups] + pieces[2 * groups : 3 * groups])
            weight = weights[2 * chip + part[0]]
            for g in range(groups):
                tiles.append(
                    (
                        others[base + 128 * g : base + 128 * g + 128, :],
                        shift[g : g + 1],
                        weight[:, 128 * g : 128 * g + 128],
                    )
                )
        for k in range(0, len(tiles), 2):
            one, two = tiles[k], tiles[k + 1]
            right = jnp.concatenate([jnp.concatenate([one[0], two[0]], axis=0), ones], axis=1)
            inner = narrow_dot(left[...], right) * scale
            one_value = jnp.exp2(jnp.minimum(inner[:, :128] + one[1], 0.0)) * one[2]
            two_value = jnp.exp2(jnp.minimum(inner[:, 128:] + two[1], 0.0)) * two[2]
            total = total + (one_value + two_value)
    acc[...] = total

    @pl.when(step == pl.num_programs(0) - 1)
    def _():
        mine = dot(jnp.ones((8, 128), f32), acc[...], ((1,), (1,)))
        rows[...] = mine[:1]
        image = mine + (0.5 * ridge_shift) * direction[...]
        size = old_full.shape[1]
        flat = (sums.shape[0], 1)
        sums[:, :, :size] = jnp.broadcast_to(
            dot(image, old_full[...], ((1,), (0,)))[:1][None], flat + (size,)
        )
        sums[:, :, size : 2 * size] = jnp.broadcast_to(
            dot(image, columns[...], ((1,), (0,)))[:1][None], flat + (size,)
        )
        along_image = jnp.sum(image[:1] * direction[...], axis=1, keepdims=True)
        along_targets = 0.5 * jnp.sum(targets[...] * direction[...], axis=1, keepdims=True)
        place = lax.broadcasted_iota(jnp.int32, (1, 128), 1)
        last = jnp.where(place == 0, along_image, jnp.where(place == 1, along_targets, 0.0))
        sums[:, :, 2 * size :] = jnp.broadcast_to(last[None], flat + (128,))


def kernel_rows(part, points, others, stride, weights, old_full, columns, direction, targets):
    count, dim = points.shape
    parts = weights.shape[0]
    chips = parts // 2
    scale = 2.0 * (2.0 / dim) * math.log2(math.e)
    steps = 8
    size = others.shape[0] // steps
    width = old_full.shape[1] + columns.shape[1] + 128

    def fixed(array):
        return pl.BlockSpec(array.shape, lambda i: (0,) * array.ndim)

    return pl.pallas_call(
        lambda *refs: rows_kernel(scale, stride, weights.shape[2], *refs),
        grid=(steps,),
        in_specs=[
            scalar,
            fixed(points),
            pl.BlockSpec((size, dim), lambda i: (i, 0)),
            pl.BlockSpec((parts // steps, 1, weights.shape[2]), lambda i: (i, 0, 0)),
            fixed(old_full),
            fixed(columns),
            fixed(direction),
            fixed(targets),
        ],
        out_specs=(
            pl.BlockSpec((1, count), lambda i: (0, 0)),
            pl.BlockSpec((parts, 1, width), lambda i: (0, 0, 0)),
        ),
        out_shape=(
            jax.ShapeDtypeStruct((1, count), f32),
            jax.ShapeDtypeStruct((parts, 1, width), f32),
        ),
        scratch_shapes=[pltpu.VMEM((count, 2 * dim), bf16), pltpu.VMEM((count, 128), f32)],
        compiler_params=params,
        name="kernel_rows",
    )(part, points, others, weights, old_full, columns, direction, targets)


def tail_kernel(
    sums, mine, other, old_inverse, cross_low, schur_inverse, old_proj, new_proj,
    old_full, columns, direction, targets, answer, residual, preconditioned,
):
    size = old_proj.shape[1]
    total = jnp.sum(sums[...], axis=0)
    alpha = total[:, 2 * size + 1 : 2 * size + 2] / total[:, 2 * size : 2 * size + 1]
    step = alpha * direction[...]
    answer[...] = step
    left = targets[...] - alpha * (mine[...] + other[...]) - ridge_shift * step
    residual[...] = left
    coefs = solve(
        old_inverse[...], cross_low[...], schur_inverse[...],
        jnp.broadcast_to(old_proj[...] - alpha * total[:, :size], (8, size)),
        jnp.broadcast_to(new_proj[...] - alpha * total[:, size : 2 * size], (8, size)),
    )
    preconditioned[...] = apply(left, coefs, old_full[...], columns[...])


def tail(*args):
    row = jax.ShapeDtypeStruct(args[1].shape, f32)
    return pl.pallas_call(
        tail_kernel,
        out_shape=(row,) * 3,
        in_specs=[whole] * len(args),
        out_specs=(whole,) * 3,
        compiler_params=params,
        name="tail",
    )(*args)


def exchange(pieces, axes):
    return lax.all_to_all(pieces, axes, 0, 0, tiled=True)


def spread(piece, count, axes):
    return exchange(jnp.broadcast_to(piece[None], (count,) + piece.shape), axes)


def swap(value):
    return lax.ppermute(value, "sub", [(0, 1), (1, 0)])


def both(mine, part):
    other = swap(mine)
    first = jnp.where(part == 0, mine, other)
    second = jnp.where(part == 0, other, mine)
    return jnp.concatenate([first, second], axis=1)


def local(points, old_factor, targets, pivots):
    count, dim = points.shape
    size = pivots.shape[0]
    part = lax.axis_index("sub")
    chips = lax.axis_size("rows")
    parts = 2 * chips
    half = count // 2
    each = size // chips
    prev = 2 * old_factor.shape[1]
    first = lax.axis_index("rows") * count
    part_ref = part.astype(jnp.int32).reshape(1)
    row = targets.reshape(1, count)

    picks = (pivots[:, None] == (first + lax.iota(jnp.int32, count))[None, :]).astype(bf16)
    wanted = jnp.concatenate([points, old_factor.astype(bf16)], axis=1)
    width = wanted.shape[1]
    picked = lax.dot_general(picks, wanted, (((1,), (0,)), ((), ())), preferred_element_type=f32)
    came = exchange(picked.astype(bf16).reshape(chips, each, width), "rows")
    kept = jnp.sum(came.astype(f32), axis=0).astype(bf16)
    came = spread(kept, parts, everyone).reshape(chips, 2, each, width)
    pivot_points = came[:, 0, :, :dim].reshape(size, dim)
    pivot_old = jnp.concatenate(
        [came[:, 0, :, dim:].reshape(size, -1), came[:, 1, :, dim:].reshape(size, -1)], axis=1
    )

    near = lax.dynamic_slice_in_dim(points, part * half, half, 0)
    wide = near.astype(f32)
    rest = -0.5 * jnp.sum(wide * wide, axis=1)
    pieces = []
    for _ in range(3):
        piece = lax.reduce_precision(rest, 8, 7)
        pieces.append(piece.astype(bf16).reshape(-1, dim))
        rest = rest - piece
    pieces = jnp.concatenate(pieces, axis=0)
    pieces = jnp.pad(pieces, ((0, 16 - pieces.shape[0]), (0, 0)))
    near = jnp.concatenate([near, pieces], axis=0)
    others = lax.all_gather(near, "rows", axis=0, tiled=True)

    old_full = both(old_factor, part)
    old_gram = jnp.concatenate(
        [
            dot(old_full, old_factor, ((0,), (0,))),
            jnp.pad(jnp.sum(old_factor * targets[:, None], axis=0)[None], ((0, 7), (0, 0))),
        ],
        axis=0,
    )
    old_gram = both(lax.psum(old_gram, "rows"), part)
    old_proj = old_gram[prev : prev + 1]
    old_core = old_gram[:prev] + ridge_shift * jnp.eye(prev, dtype=f32)

    columns, block, gram = pivot_columns(part_ref, points, pivot_points, old_full, pivot_old, row)
    came = exchange(gram.reshape(chips, each, size), "rows")
    block_inverse = factor(block)
    kept = jnp.sum(came, axis=0)
    mine = spread(kept, chips, "rows").reshape(size, size)
    old_inverse = factor(old_core)
    other = swap(mine)

    cross_low, schur_inverse, new_proj, direction, weights = core_solve(
        part_ref, old_inverse, block, mine, other, old_proj, old_full, columns, row, parts
    )
    weights = exchange(weights, everyone)
    rows, sums = kernel_rows(
        part_ref, points, others, near.shape[0], weights, old_full, columns, direction, row
    )
    sums = exchange(sums, everyone)
    answer, residual, preconditioned = tail(
        sums, rows, swap(rows), old_inverse, cross_low, schur_inverse, old_proj, new_proj,
        old_full, columns, direction, row,
    )
    cols = size // 2
    chosen = lax.dynamic_slice_in_dim(block_inverse, part * cols, cols, 0)
    new_part = dot(columns, chosen, ((1,), (1,)))
    return new_part, answer.reshape(count), residual.reshape(count), preconditioned.reshape(count)


def solution(mesh):
    in_specs = (P("rows", None), P("rows", "sub"), P("rows"), P())
    out_specs = (P("rows", "sub"), P("rows"), P("rows"), P("rows"))
    return jax.shard_map(local, mesh=mesh, in_specs=in_specs, out_specs=out_specs, check_vma=False)
```

```python
import math

import jax
import jax.numpy as jnp
from jax import lax
from jax.experimental import pallas as pl
from jax.experimental.pallas import tpu as pltpu
from jax.sharding import PartitionSpec as P

ridge_shift = 0.5
precise = lax.Precision.HIGHEST
everyone = ("rows", "sub")
f32, bf16 = jnp.float32, jnp.bfloat16
whole = pl.BlockSpec(memory_space=pltpu.VMEM)
scalar = pl.BlockSpec(memory_space=pltpu.SMEM)
params = pltpu.CompilerParams(vmem_limit_bytes=24 << 20)


def dot(left, right, contract):
    return lax.dot_general(left, right, (contract, ((), ())), precision=precise, preferred_element_type=f32)


def narrow_dot(left, right):
    return lax.dot_general(left, right, (((1,), (1,)), ((), ())), preferred_element_type=f32)


def factor_blocks(mats):
    lane = lax.broadcasted_iota(jnp.int32, (8, 128), 1)
    sub = lax.broadcasted_iota(jnp.int32, (8, 128), 0)
    outs = [[] for _ in mats]
    state = list(mats)
    for panel in range(16):
        lo = 8 * panel
        inside = (lane >= lo) & (lane < lo + 8)
        unit = (lane == lo + sub).astype(jnp.float32)
        cols = [[jnp.broadcast_to(a[:, lo + j:lo + j + 1], a.shape) for j in range(8)] for a in state]
        heads = [jnp.where(inside, unit, a[:8]) for a in state]
        scales = [jnp.zeros((8, 128), jnp.float32) for a in state]
        tails = [[] for _ in state]
        for j in range(8):
            for m in range(len(state)):
                col = cols[m][j]
                pivot = jnp.broadcast_to(col[j:j + 1], (8, 128))
                recip = 1.0 / pivot
                scales[m] = jnp.where(sub == j, lax.rsqrt(pivot), scales[m])
                top = jnp.where(sub > j, col[:8] * recip, 0.0)
                rest = col[8:] * recip[:1] if col.shape[0] > 8 else None
                for later in range(j + 1, 8):
                    row = cols[m][later][j:j + 1]
                    new = cols[m][later][:8] - top * row
                    if rest is not None:
                        new = jnp.concatenate([new, cols[m][later][8:] - rest * row], 0)
                    cols[m][later] = new
                heads[m] = heads[m] - top * heads[m][j:j + 1]
                tails[m].append(rest)
        for m in range(len(state)):
            outs[m].append(heads[m] * scales[m])
            if panel < 15:
                a = state[m][8:]
                inside_all = jnp.broadcast_to(inside[:1], a.shape)
                a = jnp.where(inside_all, 0.0, a)
                for j in range(8):
                    a = a - tails[m][j] * heads[m][j:j + 1]
                state[m] = a
    low = lax.broadcasted_iota(jnp.int32, (128, 128), 0) >= lax.broadcasted_iota(jnp.int32, (128, 128), 1)
    return [jnp.where(low, jnp.concatenate(o, 0), 0.0) for o in outs]

def chol_inverse(refs, size):
    rows = lax.broadcasted_iota(jnp.int32, (size, size), 0)
    colid = lax.broadcasted_iota(jnp.int32, (size, size), 1)
    crow = lax.broadcasted_iota(jnp.int32, (128, size), 1)
    def step(k, carry):
        off = pl.multiple_of(k * 128, 128)
        here = pl.ds(off, 128)
        invs = factor_blocks([r[here, here] for r in refs])
        inside = (crow >= off) & (crow < off + 128)
        inside_all = (colid >= off) & (colid < off + 128)
        for r, inv in zip(refs, invs):
            left = lax.dot_general(r[:, here], inv, (((1,), (1,)), ((), ())), precision=precise, preferred_element_type=jnp.float32)
            r[here, here] = inv
            head = jnp.dot(inv, jnp.where(inside, 0.0, r[here, :]), precision=precise, preferred_element_type=jnp.float32)
            r[here, :] = head
            r[here, here] = inv
            upd = jnp.dot(left, r[here, :], precision=precise, preferred_element_type=jnp.float32)
            old = r[...]
            r[...] = jnp.where(rows >= off + 128, jnp.where(inside_all, 0.0, old) - upd, old)
        return carry
    lax.fori_loop(0, size // 128, step, 0)
    for r in refs:
        r[...] = jnp.where(rows >= colid, r[...], 0.0)


def factor_kernel(matrix, out):
    out[...] = matrix[...]
    chol_inverse([out], matrix.shape[0])


def factor(matrix):
    size = matrix.shape[0]
    return pl.pallas_call(
        factor_kernel,
        out_shape=jax.ShapeDtypeStruct(matrix.shape, f32),
        in_specs=[whole],
        out_specs=whole,
        compiler_params=params,
        cost_estimate=pl.CostEstimate(flops=120 * size**3, bytes_accessed=8 * size**2, transcendentals=0),
        name="factor",
    )(matrix)


def prepare_kernel(ids, pivots, points, mine, other, targets, sent, old_full):
    size, count = pivots.shape[0], points.shape[0]
    dim, cols = points.shape[1], mine.shape[1]
    first = ids[1] == 0
    old_full[:, :cols] = jnp.where(first, mine[...], other[...])
    old_full[:, cols:] = jnp.where(first, other[...], mine[...])
    places = ids[0] + lax.broadcasted_iota(jnp.int32, (size, count), 1)
    picks = jnp.where(pivots[...] == places, 1.0, 0.0).astype(bf16)
    wanted = jnp.concatenate([points[...], mine[...].astype(bf16)], axis=1)
    picked = lax.dot_general(picks, wanted, (((1,), (0,)), ((), ())), preferred_element_type=f32)
    sent[:, : dim + cols] = picked.astype(bf16)
    wide = jnp.concatenate([mine[...], jnp.broadcast_to(targets[...], (count, 128))], axis=1)
    gram = dot(old_full[...], wide, ((0,), (0,)))
    rest = gram[:, :cols]
    for k in range(2):
        piece = rest.astype(bf16)
        start = dim + cols + k * cols
        sent[:, start : start + cols] = piece
        rest = rest - piece.astype(f32)
    rest = gram[:, cols:]
    lane = lax.broadcasted_iota(jnp.int32, (size, 128), 1)
    proj = jnp.zeros((size, 128), f32)
    for k in range(3):
        piece = rest.astype(bf16).astype(f32)
        proj = jnp.where(lane == k, piece, proj)
        rest = rest - piece
    sent[:, dim + 3 * cols :] = proj.astype(bf16)


def prepare(ids, pivots, points, mine, other, targets):
    size, count = pivots.shape[0], points.shape[0]
    width = points.shape[1] + 3 * mine.shape[1] + 128
    return pl.pallas_call(
        prepare_kernel,
        out_shape=(
            jax.ShapeDtypeStruct((size, width), bf16),
            jax.ShapeDtypeStruct((count, 2 * mine.shape[1]), f32),
        ),
        in_specs=[scalar] + [whole] * 5,
        out_specs=(whole,) * 2,
        compiler_params=params,
        name="prepare",
    )(ids, pivots, points, mine, other, targets)


def to_row(column):
    blocks = [
        jnp.transpose(jnp.broadcast_to(column[k : k + 128], (128, 128)))[:1]
        for k in range(0, column.shape[0], 128)
    ]
    return jnp.concatenate(blocks, axis=1)


def columns_kernel(
    ids, points, came, swapped, old_full, targets, columns, block, gram, old_core, old_proj
):
    first = ids[1] == 0
    dim = points.shape[1]
    size = came.shape[0]
    cols = size // 2
    rate = -2.0 / dim
    pivot_points = came[:, :dim]
    wide = points[...].astype(f32)
    pivot_wide = pivot_points.astype(f32)
    squares = pivot_wide * pivot_wide
    norms = jnp.sum(wide * wide, axis=1, keepdims=True)
    pivot_column = jnp.sum(squares, axis=1, keepdims=True)
    pivot_row = dot(jnp.ones((8, dim), f32), squares, ((1,), (1,)))[:1]
    inner = narrow_dot(points[...], pivot_points)
    values = jnp.exp(rate * jnp.maximum(norms + pivot_row - 2.0 * inner, 0.0))
    mine, other = came[:, dim : dim + cols], swapped[:, dim : dim + cols]
    pivot_old = jnp.concatenate(
        [jnp.where(first, mine, other), jnp.where(first, other, mine)], axis=1
    )
    high = old_full[...].astype(bf16)
    low = (old_full[...] - high.astype(f32)).astype(bf16)
    values = values - (narrow_dot(high, pivot_old) + narrow_dot(low, pivot_old))
    columns[...] = values
    inner = narrow_dot(pivot_points, pivot_points)
    square = jnp.exp(rate * jnp.maximum(pivot_column + pivot_row - 2.0 * inner, 0.0))
    square = square - narrow_dot(pivot_old, pivot_old)
    eye = lax.broadcasted_iota(jnp.int32, (size, size), 0) == lax.broadcasted_iota(jnp.int32, (size, size), 1)
    shift = jnp.where(eye, ridge_shift, 0.0)
    block[...] = square + shift

    @pl.when(first)
    def _():
        gram[...] = dot(old_full[...], columns[...], ((0,), (0,)))

    @pl.when(ids[1] == 1)
    def _():
        gram[...] = dot(columns[...], columns[...], ((0,), (0,)))
        proj = dot(jnp.broadcast_to(targets[...], (8, targets.shape[1])), columns[...], ((1,), (0,)))
        gram[size - 2 : size - 1, :cols] = proj[:1, :cols]
        gram[size - 1 : size, :cols] = proj[:1, cols:]

    def old_half(ref):
        start = dim + cols
        return ref[:, start : start + cols].astype(f32) + ref[:, start + cols : start + 2 * cols].astype(f32)

    mine, other = old_half(came), old_half(swapped)
    old_core[:, :cols] = jnp.where(first, mine, other) + shift[:, :cols]
    old_core[:, cols:] = jnp.where(first, other, mine) + shift[:, cols:]
    pieces = came[:, dim + 3 * cols :].astype(f32)
    old_proj[...] = to_row(pieces[:, 0:1] + pieces[:, 1:2] + pieces[:, 2:3])


def pivot_columns(ids, points, came, swapped, old_full, targets):
    count, size = points.shape[0], came.shape[0]
    square = jax.ShapeDtypeStruct((size, size), f32)
    return pl.pallas_call(
        columns_kernel,
        out_shape=(
            jax.ShapeDtypeStruct((count, size), f32), square, square, square,
            jax.ShapeDtypeStruct((1, size), f32),
        ),
        in_specs=[scalar] + [whole] * 5,
        out_specs=(whole,) * 5,
        compiler_params=params,
        name="pivot_columns",
    )(ids, points, came, swapped, old_full, targets)


def across(matrix, row):
    return jnp.sum(matrix * row, axis=1, keepdims=True)


def down(matrix, column):
    return jnp.sum(matrix * column, axis=0, keepdims=True)


def solve(old_inverse, cross_low, schur_inverse, old_side, new_side):
    up = across(old_inverse[...], old_side)
    middle = across(schur_inverse[...], new_side - down(cross_low[...], up))
    new_coef = down(schur_inverse[...], middle)
    old_coef = down(old_inverse[...], up - across(cross_low[...], new_coef))
    return old_coef, new_coef


def fit(coefs, old_full, columns):
    return across(old_full[...], coefs[0]) + across(columns[...], coefs[1])


def core_kernel(
    ids, old_inverse, block, mine, other, old_proj, old_full, columns, targets,
    cross_low, schur_inverse, new_proj, direction, upright, weights,
):
    size = block.shape[0]
    mid = size // 2
    first = ids[1] == 0
    cross = jnp.where(first, mine[...], other[...])
    schur_inverse[...] = jnp.where(first, other[...], mine[...])
    new_proj[:, :mid] = schur_inverse[size - 2 : size - 1, :mid]
    new_proj[:, mid:] = schur_inverse[size - 1 : size, :mid]
    for start in range(0, mid, 128):
        turned = jnp.transpose(schur_inverse[start : start + 128, size - 128 :])
        schur_inverse[size - 2 :, start : start + 128] = turned[126:]
    cross_low[...] = dot(old_inverse[...], cross, ((1,), (0,)))
    schur_inverse[...] = (
        ridge_shift * block[...]
        + schur_inverse[...]
        - dot(cross_low[...], cross_low[...], ((0,), (0,)))
    )
    chol_inverse([schur_inverse], size)
    coefs = solve(old_inverse, cross_low, schur_inverse, old_proj[...], new_proj[...])
    upright[...] = (targets[...] - fit(coefs, old_full, columns)) * (1.0 / ridge_shift)
    value = to_row(upright[...])
    direction[...] = value
    half = value.shape[1] // 2
    mine_half = jnp.where(first, value[:, :half], value[:, half:])
    weights[...] = jnp.broadcast_to(mine_half[None], weights.shape)


def core_solve(ids, old_inverse, block, mine, other, old_proj, old_full, columns, targets, parts):
    size, count = block.shape[0], columns.shape[0]
    return pl.pallas_call(
        core_kernel,
        out_shape=(
            jax.ShapeDtypeStruct((size, size), f32),
            jax.ShapeDtypeStruct((size, size), f32),
            jax.ShapeDtypeStruct((1, size), f32),
            jax.ShapeDtypeStruct((1, count), f32),
            jax.ShapeDtypeStruct((count, 1), f32),
            jax.ShapeDtypeStruct((parts, 1, count // 2), f32),
        ),
        in_specs=[scalar] + [whole] * 8,
        out_specs=(whole,) * 6,
        compiler_params=params,
        name="core_solve",
    )(ids, old_inverse, block, mine, other, old_proj, old_full, columns, targets)


def rows_kernel(
    scale, stride, half, ids, points, others, weights, old_full, columns, direction, targets,
    rows, sums, left, acc,
):
    count, dim = points.shape
    step = pl.program_id(0)

    @pl.when(step == 0)
    def _():
        acc[...] = jnp.zeros_like(acc)
        wide = points[...].astype(f32)
        rest = -0.5 * jnp.sum(wide * wide, axis=1, keepdims=True)
        lane = lax.broadcasted_iota(jnp.int32, (count, dim), 1)
        extra = jnp.zeros((count, dim), f32)
        for k in range(3):
            piece = rest.astype(bf16).astype(f32)
            extra = jnp.where(lane == k, piece, extra)
            rest = rest - piece
        left[:, :dim] = points[...]
        left[:, dim:] = extra.astype(bf16)

    lane = lax.broadcasted_iota(jnp.int32, (256, dim), 1)
    ones = jnp.where(lane < 3, 1.0, 0.0).astype(bf16)
    groups = half // 128
    chips = others.shape[0] // stride
    total = acc[...]
    for pair in range(chips // 2):
        tiles = []
        for chip in (2 * pair, 2 * pair + 1):
            base = chip * stride
            pieces = others[base + half : base + half + 16, :].astype(f32)
            shift = scale * (pieces[:groups] + pieces[groups : 2 * groups] + pieces[2 * groups : 3 * groups])
            weight = weights[2 * chip + ids[1]]
            for g in range(groups):
                tiles.append(
                    (
                        others[base + 128 * g : base + 128 * g + 128, :],
                        shift[g : g + 1],
                        weight[:, 128 * g : 128 * g + 128],
                    )
                )
        for k in range(0, len(tiles), 2):
            one, two = tiles[k], tiles[k + 1]
            right = jnp.concatenate([jnp.concatenate([one[0], two[0]], axis=0), ones], axis=1)
            inner = narrow_dot(left[...], right) * scale
            one_value = jnp.exp2(jnp.minimum(inner[:, :128] + one[1], 0.0)) * one[2]
            two_value = jnp.exp2(jnp.minimum(inner[:, 128:] + two[1], 0.0)) * two[2]
            total = total + (one_value + two_value)
    acc[...] = total

    @pl.when(step == pl.num_programs(0) - 1)
    def _():
        mine = jnp.sum(acc[...], axis=1, keepdims=True)
        rows[...] = to_row(mine)
        image = mine + (0.5 * ridge_shift) * direction[...]
        size = old_full.shape[1]
        flat = (sums.shape[0], 1)
        sums[:, :, :size] = jnp.broadcast_to(down(old_full[...], image)[None], flat + (size,))
        sums[:, :, size : 2 * size] = jnp.broadcast_to(down(columns[...], image)[None], flat + (size,))
        along_image = jnp.sum(image * direction[...], axis=0, keepdims=True)
        along_targets = 0.5 * jnp.sum(targets[...] * direction[...], axis=0, keepdims=True)
        place = lax.broadcasted_iota(jnp.int32, (1, 128), 1)
        last = jnp.where(place == 0, along_image, jnp.where(place == 1, along_targets, 0.0))
        sums[:, :, 2 * size :] = jnp.broadcast_to(last[None], flat + (128,))


def kernel_rows(ids, points, others, stride, weights, old_full, columns, direction, targets):
    count, dim = points.shape
    parts = weights.shape[0]
    chips = parts // 2
    scale = 2.0 * (2.0 / dim) * math.log2(math.e)
    steps = 8
    size = others.shape[0] // steps
    width = old_full.shape[1] + columns.shape[1] + 128

    def fixed(array):
        return pl.BlockSpec(array.shape, lambda i: (0,) * array.ndim)

    return pl.pallas_call(
        lambda *refs: rows_kernel(scale, stride, weights.shape[2], *refs),
        grid=(steps,),
        in_specs=[
            scalar,
            fixed(points),
            pl.BlockSpec((size, dim), lambda i: (i, 0)),
            pl.BlockSpec((parts // steps, 1, weights.shape[2]), lambda i: (i, 0, 0)),
            fixed(old_full),
            fixed(columns),
            fixed(direction),
            fixed(targets),
        ],
        out_specs=(
            pl.BlockSpec((1, count), lambda i: (0, 0)),
            pl.BlockSpec((parts, 1, width), lambda i: (0, 0, 0)),
        ),
        out_shape=(
            jax.ShapeDtypeStruct((1, count), f32),
            jax.ShapeDtypeStruct((parts, 1, width), f32),
        ),
        scratch_shapes=[pltpu.VMEM((count, 2 * dim), bf16), pltpu.VMEM((count, 128), f32)],
        compiler_params=params,
        name="kernel_rows",
    )(ids, points, others, weights, old_full, columns, direction, targets)


def tail_kernel(
    sums, mine, other, old_inverse, cross_low, schur_inverse, old_proj, new_proj,
    old_full, columns, direction, targets, answer, residual, preconditioned,
):
    size = old_proj.shape[1]
    total = jnp.sum(sums[...], axis=0)
    alpha = total[:, 2 * size + 1 : 2 * size + 2] / total[:, 2 * size : 2 * size + 1]
    step = alpha * direction[...]
    answer[...] = step
    left = targets[...] - alpha * (mine[...] + other[...]) - ridge_shift * step
    residual[...] = left
    coefs = solve(
        old_inverse, cross_low, schur_inverse,
        old_proj[...] - alpha * total[:, :size], new_proj[...] - alpha * total[:, size : 2 * size],
    )
    preconditioned[...] = (left - to_row(fit(coefs, old_full, columns))) * (1.0 / ridge_shift)


def tail(*args):
    row = jax.ShapeDtypeStruct(args[1].shape, f32)
    return pl.pallas_call(
        tail_kernel,
        out_shape=(row,) * 3,
        in_specs=[whole] * len(args),
        out_specs=(whole,) * 3,
        compiler_params=params,
        name="tail",
    )(*args)


def exchange(pieces, axes):
    return lax.all_to_all(pieces, axes, 0, 0, tiled=True)


def spread(piece, count, axes):
    return exchange(jnp.broadcast_to(piece[None], (count,) + piece.shape), axes)


def split(rest, count):
    pieces = []
    for _ in range(count):
        piece = lax.reduce_precision(rest, 8, 7)
        pieces.append(piece.astype(bf16))
        rest = rest - piece
    return pieces


def swap(value):
    return lax.ppermute(value, "sub", [(0, 1), (1, 0)])


def local(points, old_factor, targets, pivots):
    count, dim = points.shape
    size = pivots.shape[0]
    part = lax.axis_index("sub")
    chips = lax.axis_size("rows")
    parts = 2 * chips
    half = count // 2
    each = size // chips
    cols = old_factor.shape[1]
    first = lax.axis_index("rows") * count
    ids = jnp.stack([first, part]).astype(jnp.int32)
    row, upright = targets.reshape(1, count), targets.reshape(count, 1)

    sent, old_full = prepare(ids, pivots.reshape(size, 1), points, old_factor, swap(old_factor), upright)
    width = sent.shape[1]
    came = exchange(sent.reshape(chips, each, width), "rows")
    kept = jnp.sum(came.astype(f32), axis=0)
    start = dim + cols
    gram = kept[:, start : start + cols] + kept[:, start + cols : start + 2 * cols]
    proj = jnp.sum(kept[:, start + 2 * cols : start + 2 * cols + 3], axis=1, keepdims=True)
    kept = jnp.concatenate(
        [kept[:, :start].astype(bf16)]
        + split(gram, 2)
        + [jnp.pad(jnp.concatenate(split(proj, 3), axis=1), ((0, 0), (0, 125)))],
        axis=1,
    )
    came = spread(kept, chips, "rows").reshape(size, width)
    swapped = swap(came)

    near = lax.dynamic_slice_in_dim(points, part * half, half, 0)
    wide = near.astype(f32)
    pieces = split(-0.5 * jnp.sum(wide * wide, axis=1), 3)
    pieces = jnp.concatenate([piece.reshape(-1, dim) for piece in pieces], axis=0)
    pieces = jnp.pad(pieces, ((0, 16 - pieces.shape[0]), (0, 0)))
    near = jnp.concatenate([near, pieces], axis=0)
    others = lax.all_gather(near, "rows", axis=0, tiled=True)

    columns, block, gram, old_core, old_proj = pivot_columns(
        ids, points, came, swapped, old_full, row
    )
    came = exchange(gram.reshape(chips, each, size), "rows")
    block_inverse = factor(block)
    kept = jnp.sum(came, axis=0)
    kept, block_inverse = lax.optimization_barrier((kept, block_inverse))
    mine = spread(kept, chips, "rows").reshape(size, size)
    old_inverse = factor(old_core)
    mine, old_inverse = lax.optimization_barrier((mine, old_inverse))
    other = swap(mine)

    cross_low, schur_inverse, new_proj, direction, direction_column, weights = core_solve(
        ids, old_inverse, block, mine, other, old_proj, old_full, columns, upright, parts
    )
    weights = exchange(weights, everyone)
    chosen = lax.dynamic_slice_in_dim(block_inverse, part * cols, cols, 0)
    new_part = dot(columns, chosen, ((1,), (1,)))
    rows, sums = kernel_rows(
        ids, points, others, near.shape[0], weights, old_full, columns, direction_column, upright
    )
    sums = exchange(sums, everyone)
    answer, residual, preconditioned = tail(
        sums, rows, swap(rows), old_inverse, cross_low, schur_inverse, old_proj, new_proj,
        old_full, columns, direction, row,
    )
    return new_part, answer.reshape(count), residual.reshape(count), preconditioned.reshape(count)


def solution(mesh):
    in_specs = (P("rows", None), P("rows", "sub"), P("rows"), P())
    out_specs = (P("rows", "sub"), P("rows"), P("rows"), P("rows"))
    return jax.shard_map(local, mesh=mesh, in_specs=in_specs, out_specs=out_specs, check_vma=False)
```

```python
import math

import jax
import jax.numpy as jnp
from jax import lax
from jax.experimental import pallas as pl
from jax.experimental.pallas import tpu as pltpu
from jax.sharding import PartitionSpec as P

ridge_shift = 0.5
precise = lax.Precision.HIGHEST
everyone = ("rows", "sub")
f32, bf16 = jnp.float32, jnp.bfloat16
whole = pl.BlockSpec(memory_space=pltpu.VMEM)
far = pl.BlockSpec(memory_space=pltpu.HBM)
scalar = pl.BlockSpec(memory_space=pltpu.SMEM)
params = pltpu.CompilerParams(vmem_limit_bytes=24 << 20)


def dot(left, right, contract):
    return lax.dot_general(left, right, (contract, ((), ())), precision=precise, preferred_element_type=f32)


def narrow_dot(left, right):
    return lax.dot_general(left, right, (((1,), (1,)), ((), ())), preferred_element_type=f32)


def total(terms):
    while len(terms) > 1:
        terms = [terms[i] + terms[i + 1] if i + 1 < len(terms) else terms[i] for i in range(0, len(terms), 2)]
    return terms[0]

def factor_block(a, hook):
    lane = lax.broadcasted_iota(jnp.int32, (8, 128), 1)
    sub = lax.broadcasted_iota(jnp.int32, (8, 128), 0)
    full = lambda v: jnp.broadcast_to(v, (8, 128))
    rows = [a[8 * i:8 * i + 8] for i in range(16)]
    outs, pending = [], []
    def drain(n):
        for _ in range(min(n, len(pending))):
            pending.pop(0)()
    for panel in range(16):
        lo = 8 * panel
        inside = (lane >= lo) & (lane < lo + 8)
        head = rows[panel]
        cols = [full(head[:, lo + j:lo + j + 1]) for j in range(8)]
        e = {(i, j): full(cols[j][i:i + 1]) for j in range(8) for i in range(j, 8)}
        head = jnp.where(inside, (lane == lo + sub).astype(f32), head)
        base = [full(head[j:j + 1]) for j in range(8)]
        per = -(-len(pending) // 5)
        m, pieces = {}, {}
        for j in (0, 2, 4, 6):
            p, q, s = e[j, j], e[j + 1, j], e[j + 1, j + 1]
            rdet = 1.0 / (p * s - q * q)
            pieces[j] = (p, q, s, rdet)
            g = {}
            for i in range(j + 2, 8):
                x, y = e[i, j], e[i, j + 1]
                g[i] = (x * s - y * q, y * p - x * q)
            for i in range(j + 2, 8):
                for k in range(j + 2, i + 1):
                    e[i, k] = e[i, k] - (g[i][0] * e[k, j] + g[i][1] * e[k, j + 1]) * rdet
            for i in range(j + 2, 8):
                f0, f1 = g[i][0] * rdet, g[i][1] * rdet
                for k in range(j):
                    m[i, k] = m[i, k] - (f0 * m[j, k] + f1 * m[j + 1, k])
                m[i, j], m[i, j + 1] = -f0, -f1
            drain(per)
            if j == 2:
                hook(panel)
        h = [total([base[i]] + [m[i, k] * base[k] for k in range(i - i % 2)]) for i in range(8)]
        y = []
        for j in (0, 2, 4, 6):
            p, q, s, rdet = pieces[j]
            y.append((s * h[j] - q * h[j + 1]) * rdet)
            y.append((p * h[j + 1] - q * h[j]) * rdet)
        G = [total([y[l]] + [m[i, l] * y[i] for i in range(l - l % 2 + 2, 8)]) for l in range(8)]
        drain(len(pending))
        if panel < 15:
            r = rows[panel + 1]
            c = total([full(r[:, lo + j:lo + j + 1]) * G[j] for j in range(8)])
            rows[panel + 1] = jnp.where(inside, 0.0, r) - c
        if panel < 14:
            g = G[7]
            for l in range(7):
                g = jnp.where(sub == l, G[l], g)
            parts = ([jnp.zeros((lo, 128), f32)] if panel else []) + [g, jnp.zeros((120 - lo, 128), f32)]
            upd = dot(jnp.concatenate(rows[panel + 2:], 0), jnp.concatenate(parts, 0), ((1,), (0,)))

            def use(i, upd=upd, first=panel + 2, inside=inside):
                rows[i] = jnp.where(inside, 0.0, rows[i]) - upd[8 * (i - first):8 * (i - first) + 8]

            for i in range(panel + 2, 16):
                pending.append(lambda i=i, u=use: u(i))
        out = jnp.zeros((8, 128), f32)
        for j in (0, 2, 4, 6):
            p, q, s, rdet = pieces[j]
            rp = 1.0 / p
            out = jnp.where(sub == j, h[j] * lax.rsqrt(p), out)
            out = jnp.where(sub == j + 1, (h[j + 1] - (q * rp) * h[j]) * lax.rsqrt(s - q * (q * rp)), out)
        outs.append(out)
    low = lax.broadcasted_iota(jnp.int32, (128, 128), 0) >= lax.broadcasted_iota(jnp.int32, (128, 128), 1)
    return jnp.where(low, jnp.concatenate(outs, 0), 0.0)

def chol_inverse(ref, left, block, inverse):
    size = ref.shape[0]
    blocks = size // 128
    row = lax.broadcasted_iota(jnp.int32, (size, 128), 0)
    lane = lax.broadcasted_iota(jnp.int32, (128, size), 1)
    block[...] = ref[:128, :128]
    inverse[...] = jnp.zeros_like(inverse)

    def finish(here, off):
        inside = (lane >= off) & (lane < off + 128)
        return dot(inverse[...], jnp.where(inside, 0.0, ref[here, :]), ((1,), (0,)))

    def step(k, carry):
        off = pl.multiple_of(k * 128, 128)
        prev = pl.multiple_of(jnp.maximum(off - 128, 0), 128)
        here, before = pl.ds(off, 128), pl.ds(prev, 128)

        def hook(panel):
            if panel == 0:
                value = dot(ref[:, before], inverse[...], ((1,), (1,)))
                left[...] = jnp.where((row >= off) & (off > 0), value, 0.0)
            elif panel == 2:
                ref[before, :] = jnp.where(off > 0, finish(before, prev), ref[before, :])
                ref[before, before] = jnp.where(off > 0, inverse[...], ref[before, before])
            elif panel % 3 == 1 and panel // 3 - 1 in range(blocks):
                c = panel // 3 - 1
                lanes = slice(128 * c, 128 * c + 128)
                gone = (off > 0) & (prev == 128 * c)
                old = ref[:, lanes]
                upd = dot(left[...], ref[before, lanes], ((1,), (0,)))
                ref[:, lanes] = jnp.where(row >= off, jnp.where(gone, 0.0, old) - upd, old)

        value = factor_block(block[...], hook)
        after = pl.multiple_of(jnp.minimum(off + 128, size - 128), 128)
        after = pl.ds(after, 128)
        part = dot(ref[after, here], value, ((1,), (1,)))
        block[...] = ref[after, after] - dot(part, part, ((1,), (1,)))
        inverse[...] = value
        return carry

    lax.fori_loop(0, blocks, step, 0)
    last = slice(size - 128, size)
    ref[last, :] = finish(last, size - 128)
    ref[last, last] = inverse[...]
    rows = lax.broadcasted_iota(jnp.int32, (size, size), 0)
    lanes = lax.broadcasted_iota(jnp.int32, (size, size), 1)
    ref[...] = jnp.where(rows >= lanes, ref[...], 0.0)


def factor_scratch(size):
    return [pltpu.VMEM((size, 128), f32), pltpu.VMEM((128, 128), f32), pltpu.VMEM((128, 128), f32)]


class Mover:
    def __init__(self, sems):
        self.sems, self.used = sems, 0

    def start(self, source, target, pieces=4):
        rows = source.shape[0] // pieces
        copies = []
        for k in range(pieces):
            here = pl.ds(k * rows, rows)
            copies.append(pltpu.make_async_copy(source.at[here], target.at[here], self.sems.at[self.used]))
            copies[-1].start()
            self.used += 1
        return copies


def arrive(copies):
    for copy in copies:
        copy.wait()


def factor_kernel(matrix, out, work, left, block, inverse, sems):
    mover = Mover(sems)
    arrive(mover.start(matrix, work))
    chol_inverse(work, left, block, inverse)
    arrive(mover.start(work, out))


def factor(matrix):
    size = matrix.shape[0]
    return pl.pallas_call(
        factor_kernel,
        out_shape=jax.ShapeDtypeStruct(matrix.shape, f32),
        in_specs=[far],
        out_specs=far,
        scratch_shapes=[pltpu.VMEM((size, size), f32)] + factor_scratch(size) + [pltpu.SemaphoreType.DMA((8,))],
        compiler_params=params,
        cost_estimate=pl.CostEstimate(flops=120 * size**3, bytes_accessed=8 * size**2, transcendentals=0),
        name="factor",
    )(matrix)


def sum_kernel(came, out, work, sems):
    work[...] = jnp.broadcast_to(jnp.sum(came[...], axis=0)[None], work.shape)
    arrive(Mover(sems).start(work, out))


def sum_spread(came):
    return pl.pallas_call(
        sum_kernel,
        out_shape=jax.ShapeDtypeStruct(came.shape, f32),
        in_specs=[whole],
        out_specs=far,
        scratch_shapes=[pltpu.VMEM(came.shape, f32), pltpu.SemaphoreType.DMA((4,))],
        compiler_params=params,
        name="sum_spread",
    )(came)


def prepare_kernel(ids, pivots, points, mine, other, targets, sent, old_full):
    size, count = pivots.shape[1], points.shape[0]
    dim, cols = points.shape[1], mine.shape[1]
    first = ids[1] == 0
    old_full[:, :cols] = jnp.where(first, mine[...], other[...])
    old_full[:, cols:] = jnp.where(first, other[...], mine[...])
    places = ids[0] + lax.broadcasted_iota(jnp.int32, (size, count), 1)
    wanted_ids = jnp.concatenate([to_column(pivots[...].astype(f32))] * (count // 128), axis=1)
    picks = jnp.where(wanted_ids == places.astype(f32), 1.0, 0.0).astype(bf16)
    wanted = jnp.concatenate([points[...], mine[...].astype(bf16)], axis=1)
    picked = lax.dot_general(picks, wanted, (((1,), (0,)), ((), ())), preferred_element_type=f32)
    sent[:, : dim + cols] = picked.astype(bf16)
    wide = jnp.concatenate([mine[...], to_column(targets[...])], axis=1)
    gram = dot(old_full[...], wide, ((0,), (0,)))
    rest = gram[:, :cols]
    for k in range(2):
        piece = rest.astype(bf16)
        start = dim + cols + k * cols
        sent[:, start : start + cols] = piece
        rest = rest - piece.astype(f32)
    rest = gram[:, cols:]
    lane = lax.broadcasted_iota(jnp.int32, (size, 128), 1)
    proj = jnp.zeros((size, 128), f32)
    for k in range(3):
        piece = rest.astype(bf16).astype(f32)
        proj = jnp.where(lane == k, piece, proj)
        rest = rest - piece
    sent[:, dim + 3 * cols :] = proj.astype(bf16)


def prepare(ids, pivots, points, mine, other, targets):
    size, count = pivots.shape[1], points.shape[0]
    width = points.shape[1] + 3 * mine.shape[1] + 128
    return pl.pallas_call(
        prepare_kernel,
        out_shape=(
            jax.ShapeDtypeStruct((size, width), bf16),
            jax.ShapeDtypeStruct((count, 2 * mine.shape[1]), f32),
        ),
        in_specs=[scalar] + [whole] * 5,
        out_specs=(whole,) * 2,
        compiler_params=params,
        name="prepare",
    )(ids, pivots, points, mine, other, targets)


def to_column(row):
    blocks = [
        jnp.transpose(jnp.broadcast_to(row[:, k : k + 128], (128, 128)))
        for k in range(0, row.shape[1], 128)
    ]
    return jnp.concatenate(blocks, axis=0)


def to_row(column):
    blocks = [
        jnp.transpose(jnp.broadcast_to(column[k : k + 128], (128, 128)))[:1]
        for k in range(0, column.shape[0], 128)
    ]
    return jnp.concatenate(blocks, axis=1)


def columns_kernel(
    ids, points, came, swapped, old_full, targets,
    columns, block_out, gram_out, old_core_out, old_proj, block, gram, old_core, sems,
):
    mover = Mover(sems)
    first = ids[1] == 0
    dim = points.shape[1]
    size = came.shape[0]
    cols = size // 2
    rate = -2.0 / dim
    pivot_points = came[:, :dim]
    wide = points[...].astype(f32)
    pivot_wide = pivot_points.astype(f32)
    squares = pivot_wide * pivot_wide
    norms = jnp.sum(wide * wide, axis=1, keepdims=True)
    pivot_column = jnp.sum(squares, axis=1, keepdims=True)
    pivot_row = dot(jnp.ones((8, dim), f32), squares, ((1,), (1,)))[:1]
    inner = narrow_dot(points[...], pivot_points)
    values = jnp.exp(rate * jnp.maximum(norms + pivot_row - 2.0 * inner, 0.0))
    mine, other = came[:, dim : dim + cols], swapped[:, dim : dim + cols]
    pivot_old = jnp.concatenate(
        [jnp.where(first, mine, other), jnp.where(first, other, mine)], axis=1
    )
    high = old_full[...].astype(bf16)
    low = (old_full[...] - high.astype(f32)).astype(bf16)
    values = values - (narrow_dot(high, pivot_old) + narrow_dot(low, pivot_old))
    columns[...] = values
    inner = narrow_dot(pivot_points, pivot_points)
    square = jnp.exp(rate * jnp.maximum(pivot_column + pivot_row - 2.0 * inner, 0.0))
    square = square - narrow_dot(pivot_old, pivot_old)
    eye = lax.broadcasted_iota(jnp.int32, (size, size), 0) == lax.broadcasted_iota(jnp.int32, (size, size), 1)
    shift = jnp.where(eye, ridge_shift, 0.0)
    block[...] = square + shift

    copies = mover.start(block, block_out)

    def old_half(ref):
        start = dim + cols
        return ref[:, start : start + cols].astype(f32) + ref[:, start + cols : start + 2 * cols].astype(f32)

    mine, other = old_half(came), old_half(swapped)
    old_core[:, :cols] = jnp.where(first, mine, other) + shift[:, :cols]
    old_core[:, cols:] = jnp.where(first, other, mine) + shift[:, cols:]
    pieces = came[:, dim + 3 * cols :].astype(f32)
    old_proj[...] = to_row(pieces[:, 0:1] + pieces[:, 1:2] + pieces[:, 2:3])
    copies += mover.start(old_core, old_core_out)

    @pl.when(first)
    def _():
        gram[...] = dot(old_full[...], columns[...], ((0,), (0,)))

    @pl.when(ids[1] == 1)
    def _():
        gram[...] = dot(columns[...], columns[...], ((0,), (0,)))
        proj = dot(jnp.broadcast_to(targets[...], (8, targets.shape[1])), columns[...], ((1,), (0,)))
        gram[size - 2 : size - 1, :cols] = proj[:1, :cols]
        gram[size - 1 : size, :cols] = proj[:1, cols:]

    copies += mover.start(gram, gram_out)
    arrive(copies)


def pivot_columns(ids, points, came, swapped, old_full, targets):
    count, size = points.shape[0], came.shape[0]
    square = jax.ShapeDtypeStruct((size, size), f32)
    return pl.pallas_call(
        columns_kernel,
        out_shape=(
            jax.ShapeDtypeStruct((count, size), f32), square, square, square,
            jax.ShapeDtypeStruct((1, size), f32),
        ),
        in_specs=[scalar] + [whole] * 5,
        out_specs=(whole, far, far, far, whole),
        scratch_shapes=[pltpu.VMEM((size, size), f32)] * 3 + [pltpu.SemaphoreType.DMA((12,))],
        compiler_params=params,
        name="pivot_columns",
    )(ids, points, came, swapped, old_full, targets)


def across(matrix, row):
    return jnp.sum(matrix * row, axis=1, keepdims=True)


def down(matrix, column):
    return jnp.sum(matrix * column, axis=0, keepdims=True)


def solve(old_inverse, cross_low, schur_inverse, old_side, new_side):
    up = across(old_inverse[...], old_side)
    middle = across(schur_inverse[...], new_side - down(cross_low[...], up))
    new_coef = down(schur_inverse[...], middle)
    old_coef = down(old_inverse[...], up - across(cross_low[...], new_coef))
    return old_coef, new_coef


def fit(coefs, old_full, columns):
    return across(old_full[...], coefs[0]) + across(columns[...], coefs[1])


def core_kernel(
    ids, old_inverse_in, block_in, mine, other, old_proj, old_full, columns, targets,
    cross_out, schur_out, new_proj, direction, weights,
    old_inverse, block, cross_low, schur_inverse, left, part, inverse, sems,
):
    mover = Mover(sems)
    first_copy = mover.start(old_inverse_in, old_inverse)
    second_copy = mover.start(block_in, block)
    size = block.shape[0]
    mid = size // 2
    first = ids[1] == 0
    cross = jnp.where(first, mine[...], other[...])
    schur_inverse[...] = jnp.where(first, other[...], mine[...])
    new_proj[:, :mid] = schur_inverse[size - 2 : size - 1, :mid]
    new_proj[:, mid:] = schur_inverse[size - 1 : size, :mid]
    for start in range(0, mid, 128):
        turned = jnp.transpose(schur_inverse[start : start + 128, size - 128 :])
        schur_inverse[size - 2 :, start : start + 128] = turned[126:]
    arrive(first_copy)
    cross_low[...] = dot(old_inverse[...], cross, ((1,), (0,)))
    copies = mover.start(cross_low, cross_out)
    arrive(second_copy)
    schur_inverse[...] = (
        ridge_shift * block[...]
        + schur_inverse[...]
        - dot(cross_low[...], cross_low[...], ((0,), (0,)))
    )
    chol_inverse(schur_inverse, left, part, inverse)
    copies += mover.start(schur_inverse, schur_out)
    coefs = solve(old_inverse, cross_low, schur_inverse, old_proj[...], new_proj[...])
    value = (targets[...] - to_row(fit(coefs, old_full, columns))) * (1.0 / ridge_shift)
    direction[...] = value
    half = value.shape[1] // 2
    mine_half = jnp.where(first, value[:, :half], value[:, half:])
    weights[...] = jnp.broadcast_to(mine_half[None], weights.shape)
    arrive(copies)


def core_solve(ids, old_inverse, block, mine, other, old_proj, old_full, columns, targets, parts):
    size, count = block.shape[0], columns.shape[0]
    square = jax.ShapeDtypeStruct((size, size), f32)
    return pl.pallas_call(
        core_kernel,
        out_shape=(
            square,
            square,
            jax.ShapeDtypeStruct((1, size), f32),
            jax.ShapeDtypeStruct((1, count), f32),
            jax.ShapeDtypeStruct((parts, 1, count // 2), f32),
        ),
        in_specs=[scalar, far, far] + [whole] * 6,
        out_specs=(far, far, whole, whole, whole),
        scratch_shapes=[pltpu.VMEM((size, size), f32)] * 4
        + factor_scratch(size)
        + [pltpu.SemaphoreType.DMA((16,))],
        compiler_params=params,
        name="core_solve",
    )(ids, old_inverse, block, mine, other, old_proj, old_full, columns, targets)


def rows_kernel(
    scale, stride, half, ids, points, others, weights, old_full, columns, direction, targets,
    rows, sums, left, acc,
):
    count, dim = points.shape
    step = pl.program_id(0)

    @pl.when(step == 0)
    def _():
        acc[...] = jnp.zeros_like(acc)
        wide = points[...].astype(f32)
        rest = -0.5 * jnp.sum(wide * wide, axis=1, keepdims=True)
        lane = lax.broadcasted_iota(jnp.int32, (count, dim), 1)
        extra = jnp.zeros((count, dim), f32)
        for k in range(3):
            piece = rest.astype(bf16).astype(f32)
            extra = jnp.where(lane == k, piece, extra)
            rest = rest - piece
        left[:, :dim] = points[...]
        left[:, dim:] = extra.astype(bf16)

    lane = lax.broadcasted_iota(jnp.int32, (256, dim), 1)
    ones = jnp.where(lane < 3, 1.0, 0.0).astype(bf16)
    groups = half // 128
    chips = others.shape[0] // stride
    total = acc[...]
    for pair in range(chips // 2):
        tiles = []
        for chip in (2 * pair, 2 * pair + 1):
            base = chip * stride
            pieces = others[base + half : base + half + 16, :].astype(f32)
            shift = scale * (pieces[:groups] + pieces[groups : 2 * groups] + pieces[2 * groups : 3 * groups])
            weight = weights[2 * chip + ids[1]]
            for g in range(groups):
                tiles.append(
                    (
                        others[base + 128 * g : base + 128 * g + 128, :],
                        shift[g : g + 1],
                        weight[:, 128 * g : 128 * g + 128],
                    )
                )
        for k in range(0, len(tiles), 2):
            one, two = tiles[k], tiles[k + 1]
            right = jnp.concatenate([jnp.concatenate([one[0], two[0]], axis=0), ones], axis=1)
            inner = narrow_dot(left[...], right) * scale
            one_value = jnp.exp2(jnp.minimum(inner[:, :128] + one[1], 0.0)) * one[2]
            two_value = jnp.exp2(jnp.minimum(inner[:, 128:] + two[1], 0.0)) * two[2]
            total = total + (one_value + two_value)
    acc[...] = total

    @pl.when(step == pl.num_programs(0) - 1)
    def _():
        mine = jnp.sum(acc[...], axis=1, keepdims=True)
        rows[...] = to_row(mine)
        image = mine + (0.5 * ridge_shift) * to_column(direction[...])[:, :1]
        size = old_full.shape[1]
        flat = (sums.shape[0], 1)
        sums[:, :, :size] = jnp.broadcast_to(down(old_full[...], image)[None], flat + (size,))
        sums[:, :, size : 2 * size] = jnp.broadcast_to(down(columns[...], image)[None], flat + (size,))
        along_image = jnp.sum(to_row(image) * direction[...], axis=1, keepdims=True)
        along_targets = 0.5 * jnp.sum(targets[...] * direction[...], axis=1, keepdims=True)
        place = lax.broadcasted_iota(jnp.int32, (1, 128), 1)
        last = jnp.where(place == 0, along_image, jnp.where(place == 1, along_targets, 0.0))
        sums[:, :, 2 * size :] = jnp.broadcast_to(last[None], flat + (128,))


def kernel_rows(ids, points, others, stride, weights, old_full, columns, direction, targets):
    count, dim = points.shape
    parts = weights.shape[0]
    chips = parts // 2
    scale = 2.0 * (2.0 / dim) * math.log2(math.e)
    steps = 8
    size = others.shape[0] // steps
    width = old_full.shape[1] + columns.shape[1] + 128

    def fixed(array):
        return pl.BlockSpec(array.shape, lambda i: (0,) * array.ndim)

    return pl.pallas_call(
        lambda *refs: rows_kernel(scale, stride, weights.shape[2], *refs),
        grid=(steps,),
        in_specs=[
            scalar,
            fixed(points),
            pl.BlockSpec((size, dim), lambda i: (i, 0)),
            pl.BlockSpec((parts // steps, 1, weights.shape[2]), lambda i: (i, 0, 0)),
            whole,
            whole,
            fixed(direction),
            fixed(targets),
        ],
        out_specs=(
            pl.BlockSpec((1, count), lambda i: (0, 0)),
            pl.BlockSpec((parts, 1, width), lambda i: (0, 0, 0)),
        ),
        out_shape=(
            jax.ShapeDtypeStruct((1, count), f32),
            jax.ShapeDtypeStruct((parts, 1, width), f32),
        ),
        scratch_shapes=[pltpu.VMEM((count, 2 * dim), bf16), pltpu.VMEM((count, 128), f32)],
        compiler_params=pltpu.CompilerParams(vmem_limit_bytes=52 << 20),
        name="kernel_rows",
    )(ids, points, others, weights, old_full, columns, direction, targets)


def tail_kernel(
    sums, mine, other, old_inverse_in, cross_in, schur_in, old_proj, new_proj,
    old_full, columns, direction, targets, answer, residual, preconditioned,
    old_inverse, cross_low, schur_inverse, sems,
):
    mover = Mover(sems)
    copies = mover.start(old_inverse_in, old_inverse)
    copies += mover.start(cross_in, cross_low)
    copies += mover.start(schur_in, schur_inverse)
    size = old_proj.shape[1]
    total = jnp.sum(sums[...], axis=0)
    alpha = total[:, 2 * size + 1 : 2 * size + 2] / total[:, 2 * size : 2 * size + 1]
    step = alpha * direction[...]
    answer[...] = step[0]
    left = targets[...] - alpha * (mine[...] + other[...]) - ridge_shift * step
    residual[...] = left[0]
    arrive(copies)
    coefs = solve(
        old_inverse, cross_low, schur_inverse,
        old_proj[...] - alpha * total[:, :size], new_proj[...] - alpha * total[:, size : 2 * size],
    )
    preconditioned[...] = ((left - to_row(fit(coefs, old_full, columns))) * (1.0 / ridge_shift))[0]


def tail(*args):
    row = jax.ShapeDtypeStruct(args[1].shape[1:], f32)
    size = args[3].shape[0]
    return pl.pallas_call(
        tail_kernel,
        out_shape=(row,) * 3,
        in_specs=[whole] * 3 + [far] * 3 + [whole] * (len(args) - 6),
        out_specs=(whole,) * 3,
        scratch_shapes=[pltpu.VMEM((size, size), f32)] * 3 + [pltpu.SemaphoreType.DMA((12,))],
        compiler_params=params,
        name="tail",
    )(*args)


def exchange(pieces, axes):
    return lax.all_to_all(pieces, axes, 0, 0, tiled=True)


def spread(piece, count, axes):
    return exchange(jnp.broadcast_to(piece[None], (count,) + piece.shape), axes)


def split(rest, count):
    pieces = []
    for _ in range(count):
        piece = lax.reduce_precision(rest, 8, 7)
        pieces.append(piece.astype(bf16))
        rest = rest - piece
    return pieces


def swap(value):
    return lax.ppermute(value, "sub", [(0, 1), (1, 0)])


def local(points, old_factor, targets, pivots):
    count, dim = points.shape
    size = pivots.shape[0]
    part = lax.axis_index("sub")
    chips = lax.axis_size("rows")
    parts = 2 * chips
    half = count // 2
    each = size // chips
    cols = old_factor.shape[1]
    first = lax.axis_index("rows") * count
    ids = jnp.stack([first, part]).astype(jnp.int32)
    row = targets.reshape(1, count)

    sent, old_full = prepare(ids, pivots.reshape(1, size), points, old_factor, swap(old_factor), row)
    width = sent.shape[1]
    came = exchange(sent.reshape(chips, each, width), "rows")
    kept = jnp.sum(came.astype(f32), axis=0)
    start = dim + cols
    gram = kept[:, start : start + cols] + kept[:, start + cols : start + 2 * cols]
    proj = jnp.sum(kept[:, start + 2 * cols : start + 2 * cols + 3], axis=1, keepdims=True)
    kept = jnp.concatenate(
        [kept[:, :start].astype(bf16)]
        + split(gram, 2)
        + [jnp.pad(jnp.concatenate(split(proj, 3), axis=1), ((0, 0), (0, 125)))],
        axis=1,
    )
    came = spread(kept, chips, "rows").reshape(size, width)
    swapped = swap(came)

    later_points, came = lax.optimization_barrier((points, came))
    near = lax.dynamic_slice_in_dim(later_points, part * half, half, 0)
    wide = near.astype(f32)
    pieces = split(-0.5 * jnp.sum(wide * wide, axis=1), 3)
    pieces = jnp.concatenate([piece.reshape(-1, dim) for piece in pieces], axis=0)
    pieces = jnp.pad(pieces, ((0, 16 - pieces.shape[0]), (0, 0)))
    near = jnp.concatenate([near, pieces], axis=0)
    others = lax.all_gather(near, "rows", axis=0, tiled=True)

    columns, block, gram, old_core, old_proj = pivot_columns(
        ids, points, came, swapped, old_full, row
    )
    came = exchange(gram.reshape(chips, each, size), "rows")
    block_inverse = factor(block)
    came, block_inverse = lax.optimization_barrier((came, block_inverse))
    mine = exchange(sum_spread(came), "rows").reshape(size, size)
    old_inverse = factor(old_core)
    mine, old_inverse = lax.optimization_barrier((mine, old_inverse))
    other = swap(mine)

    cross_low, schur_inverse, new_proj, direction, weights = core_solve(
        ids, old_inverse, block, mine, other, old_proj, old_full, columns, row, parts
    )
    weights = exchange(weights, everyone)
    chosen = lax.dynamic_slice_in_dim(block_inverse, part * cols, cols, 0)
    new_part = dot(columns, chosen, ((1,), (1,)))
    rows, sums = kernel_rows(
        ids, points, others, near.shape[0], weights, old_full, columns, direction, row
    )
    sums = exchange(sums, everyone)
    answer, residual, preconditioned = tail(
        sums, rows, swap(rows), old_inverse, cross_low, schur_inverse, old_proj, new_proj,
        old_full, columns, direction, row,
    )
    return new_part, answer, residual, preconditioned


def solution(mesh):
    in_specs = (P("rows", None), P("rows", "sub"), P("rows"), P())
    out_specs = (P("rows", "sub"), P("rows"), P("rows"), P("rows"))
    return jax.shard_map(local, mesh=mesh, in_specs=in_specs, out_specs=out_specs, check_vma=False)
```

```python
import math

import jax
import jax.numpy as jnp
from jax import lax
from jax.experimental import pallas as pl
from jax.experimental.pallas import tpu as pltpu
from jax.sharding import PartitionSpec as P

ridge_shift = 0.5
precise = lax.Precision.HIGHEST
everyone = ("rows", "sub")
f32, bf16 = jnp.float32, jnp.bfloat16
whole = pl.BlockSpec(memory_space=pltpu.VMEM)
far = pl.BlockSpec(memory_space=pltpu.HBM)
scalar = pl.BlockSpec(memory_space=pltpu.SMEM)
params = pltpu.CompilerParams(vmem_limit_bytes=60 << 20)


def dot(left, right, contract):
    return lax.dot_general(left, right, (contract, ((), ())), precision=precise, preferred_element_type=f32)


def narrow_dot(left, right):
    return lax.dot_general(left, right, (((1,), (1,)), ((), ())), preferred_element_type=f32)


def total(terms):
    while len(terms) > 1:
        terms = [terms[i] + terms[i + 1] if i + 1 < len(terms) else terms[i] for i in range(0, len(terms), 2)]
    return terms[0]

def factor_block(a, hook):
    lane = lax.broadcasted_iota(jnp.int32, (8, 128), 1)
    sub = lax.broadcasted_iota(jnp.int32, (8, 128), 0)
    full = lambda v: jnp.broadcast_to(v, (8, 128))
    rows = [a[8 * i:8 * i + 8] for i in range(16)]
    outs, pending = [], []
    def drain(n):
        for _ in range(min(n, len(pending))):
            pending.pop(0)()
    for panel in range(16):
        lo = 8 * panel
        inside = (lane >= lo) & (lane < lo + 8)
        head = rows[panel]
        cols = [full(head[:, lo + j:lo + j + 1]) for j in range(8)]
        e = {(i, j): full(cols[j][i:i + 1]) for j in range(8) for i in range(j, 8)}
        head = jnp.where(inside, (lane == lo + sub).astype(f32), head)
        base = [full(head[j:j + 1]) for j in range(8)]
        per = -(-len(pending) // 5)
        m, pieces = {}, {}
        for j in (0, 2, 4, 6):
            p, q, s = e[j, j], e[j + 1, j], e[j + 1, j + 1]
            rdet = 1.0 / (p * s - q * q)
            pieces[j] = (p, q, s, rdet)
            g = {}
            for i in range(j + 2, 8):
                x, y = e[i, j], e[i, j + 1]
                g[i] = (x * s - y * q, y * p - x * q)
            for i in range(j + 2, 8):
                for k in range(j + 2, i + 1):
                    e[i, k] = e[i, k] - (g[i][0] * e[k, j] + g[i][1] * e[k, j + 1]) * rdet
            for i in range(j + 2, 8):
                f0, f1 = g[i][0] * rdet, g[i][1] * rdet
                for k in range(j):
                    m[i, k] = m[i, k] - (f0 * m[j, k] + f1 * m[j + 1, k])
                m[i, j], m[i, j + 1] = -f0, -f1
            drain(per)
            if j == 2:
                hook(panel)
        h = [total([base[i]] + [m[i, k] * base[k] for k in range(i - i % 2)]) for i in range(8)]
        y = []
        for j in (0, 2, 4, 6):
            p, q, s, rdet = pieces[j]
            y.append((s * h[j] - q * h[j + 1]) * rdet)
            y.append((p * h[j + 1] - q * h[j]) * rdet)
        G = [total([y[l]] + [m[i, l] * y[i] for i in range(l - l % 2 + 2, 8)]) for l in range(8)]
        drain(len(pending))
        if panel < 15:
            r = rows[panel + 1]
            c = total([full(r[:, lo + j:lo + j + 1]) * G[j] for j in range(8)])
            rows[panel + 1] = jnp.where(inside, 0.0, r) - c
        if panel < 14:
            g = G[7]
            for l in range(7):
                g = jnp.where(sub == l, G[l], g)
            parts = ([jnp.zeros((lo, 128), f32)] if panel else []) + [g, jnp.zeros((120 - lo, 128), f32)]
            upd = dot(jnp.concatenate(rows[panel + 2:], 0), jnp.concatenate(parts, 0), ((1,), (0,)))

            def use(i, upd=upd, first=panel + 2, inside=inside):
                rows[i] = jnp.where(inside, 0.0, rows[i]) - upd[8 * (i - first):8 * (i - first) + 8]

            for i in range(panel + 2, 16):
                pending.append(lambda i=i, u=use: u(i))
        out = jnp.zeros((8, 128), f32)
        for j in (0, 2, 4, 6):
            p, q, s, rdet = pieces[j]
            rp = 1.0 / p
            out = jnp.where(sub == j, h[j] * lax.rsqrt(p), out)
            out = jnp.where(sub == j + 1, (h[j + 1] - (q * rp) * h[j]) * lax.rsqrt(s - q * (q * rp)), out)
        outs.append(out)
    low = lax.broadcasted_iota(jnp.int32, (128, 128), 0) >= lax.broadcasted_iota(jnp.int32, (128, 128), 1)
    return jnp.where(low, jnp.concatenate(outs, 0), 0.0)

def chol_inverse(ref, left, block, inverse):
    size = ref.shape[0]
    blocks = size // 128
    row = lax.broadcasted_iota(jnp.int32, (size, 128), 0)
    lane = lax.broadcasted_iota(jnp.int32, (128, size), 1)
    block[...] = ref[:128, :128]
    inverse[...] = jnp.zeros_like(inverse)

    def finish(here, off):
        inside = (lane >= off) & (lane < off + 128)
        return dot(inverse[...], jnp.where(inside, 0.0, ref[here, :]), ((1,), (0,)))

    def step(k, carry):
        off = pl.multiple_of(k * 128, 128)
        prev = pl.multiple_of(jnp.maximum(off - 128, 0), 128)
        here, before = pl.ds(off, 128), pl.ds(prev, 128)

        def hook(panel):
            if panel == 0:
                value = dot(ref[:, before], inverse[...], ((1,), (1,)))
                left[...] = jnp.where((row >= off) & (off > 0), value, 0.0)
            elif panel == 2:
                ref[before, :] = jnp.where(off > 0, finish(before, prev), ref[before, :])
                ref[before, before] = jnp.where(off > 0, inverse[...], ref[before, before])
            elif panel % 3 == 1 and panel // 3 - 1 in range(blocks):
                c = panel // 3 - 1
                lanes = slice(128 * c, 128 * c + 128)
                gone = (off > 0) & (prev == 128 * c)
                old = ref[:, lanes]
                upd = dot(left[...], ref[before, lanes], ((1,), (0,)))
                ref[:, lanes] = jnp.where(row >= off, jnp.where(gone, 0.0, old) - upd, old)

        value = factor_block(block[...], hook)
        after = pl.multiple_of(jnp.minimum(off + 128, size - 128), 128)
        after = pl.ds(after, 128)
        part = dot(ref[after, here], value, ((1,), (1,)))
        block[...] = ref[after, after] - dot(part, part, ((1,), (1,)))
        inverse[...] = value
        return carry

    lax.fori_loop(0, blocks, step, 0)
    last = slice(size - 128, size)
    ref[last, :] = finish(last, size - 128)
    ref[last, last] = inverse[...]
    rows = lax.broadcasted_iota(jnp.int32, (size, size), 0)
    lanes = lax.broadcasted_iota(jnp.int32, (size, size), 1)
    ref[...] = jnp.where(rows >= lanes, ref[...], 0.0)


def factor_scratch(size):
    return [pltpu.VMEM((size, 128), f32), pltpu.VMEM((128, 128), f32), pltpu.VMEM((128, 128), f32)]


class Mover:
    def __init__(self, sems):
        self.sems, self.used = sems, 0

    def plan(self, source, target, pieces=4):
        rows = source.shape[0] // pieces
        copies = []
        for k in range(pieces):
            here = pl.ds(k * rows, rows)
            copies.append(pltpu.make_async_copy(source.at[here], target.at[here], self.sems.at[self.used]))
            self.used += 1
        return copies

    def start(self, source, target):
        copies = self.plan(source, target)
        for copy in copies:
            copy.start()
        return copies


def arrive(copies):
    for copy in copies:
        copy.wait()


def factor_kernel(matrix, out, work, left, block, inverse, sems):
    mover = Mover(sems)
    arrive(mover.start(matrix, work))
    chol_inverse(work, left, block, inverse)
    arrive(mover.start(work, out))


def factor(matrix):
    size = matrix.shape[0]
    return pl.pallas_call(
        factor_kernel,
        out_shape=jax.ShapeDtypeStruct(matrix.shape, f32),
        in_specs=[far],
        out_specs=far,
        scratch_shapes=[pltpu.VMEM((size, size), f32)] + factor_scratch(size) + [pltpu.SemaphoreType.DMA((8,))],
        compiler_params=params,
        cost_estimate=pl.CostEstimate(flops=120 * size**3, bytes_accessed=8 * size**2, transcendentals=0),
        name="factor",
    )(matrix)


def sum_kernel(came_in, out, came, work, sems):
    mover = Mover(sems)
    copies = mover.start(came_in, came)
    count = came.shape[0] // len(copies)
    total = 0.0
    for k, copy in enumerate(copies):
        copy.wait()
        total = total + jnp.sum(came[count * k : count * k + count], axis=0)
    work[...] = jnp.broadcast_to(total[None], work.shape)
    arrive(mover.start(work, out))


def sum_spread(came):
    return pl.pallas_call(
        sum_kernel,
        out_shape=jax.ShapeDtypeStruct(came.shape, f32),
        in_specs=[far],
        out_specs=far,
        scratch_shapes=[pltpu.VMEM(came.shape, f32)] * 2 + [pltpu.SemaphoreType.DMA((8,))],
        compiler_params=params,
        name="sum_spread",
    )(came)


def prepare_kernel(
    ids, pivots, points_in, mine_in, other_in, targets, sent_out, old_out, near,
    points, mine, other, sent, old_full, sems,
):
    mover = Mover(sems)
    early = mover.start(points_in, points) + mover.start(mine_in, mine)
    late = mover.start(other_in, other)
    size, count = pivots.shape[1], points.shape[0]
    dim, cols = points.shape[1], mine.shape[1]
    first = ids[1] == 0
    places = ids[0] + lax.broadcasted_iota(jnp.int32, (size, count), 1)
    wanted_ids = jnp.concatenate([to_column(pivots[...].astype(f32))] * (count // 128), axis=1)
    picks = jnp.where(wanted_ids == places.astype(f32), 1.0, 0.0).astype(bf16)
    arrive(early)
    wanted = jnp.concatenate([points[...], mine[...].astype(bf16)], axis=1)
    picked = lax.dot_general(picks, wanted, (((1,), (0,)), ((), ())), preferred_element_type=f32)
    sent[:, : dim + cols] = picked.astype(bf16)
    arrive(late)
    old_full[:, :cols] = jnp.where(first, mine[...], other[...])
    old_full[:, cols:] = jnp.where(first, other[...], mine[...])
    copies = mover.start(old_full, old_out)
    wide = jnp.concatenate([mine[...], to_column(targets[...])], axis=1)
    gram = dot(old_full[...], wide, ((0,), (0,)))
    rest = gram[:, :cols]
    for k in range(2):
        piece = rest.astype(bf16)
        start = dim + cols + k * cols
        sent[:, start : start + cols] = piece
        rest = rest - piece.astype(f32)
    rest = gram[:, cols:]
    lane = lax.broadcasted_iota(jnp.int32, (size, 128), 1)
    proj = jnp.zeros((size, 128), f32)
    for k in range(3):
        piece = rest.astype(bf16).astype(f32)
        proj = jnp.where(lane == k, piece, proj)
        rest = rest - piece
    sent[:, dim + 3 * cols :] = proj.astype(bf16)
    copies += mover.start(sent, sent_out)

    half = count // 2
    wide = jnp.where(first, points[:half].astype(f32), points[half:].astype(f32))
    rest = to_row(-0.5 * jnp.sum(wide * wide, axis=1, keepdims=True))
    near[:half] = wide.astype(bf16)
    pieces = []
    for _ in range(3):
        piece = rest.astype(bf16).astype(f32)
        pieces += [piece[:, k : k + dim] for k in range(0, half, dim)]
        rest = rest - piece
    pieces.append(jnp.zeros((16 - len(pieces), dim), f32))
    near[half:] = jnp.concatenate(pieces, axis=0).astype(bf16)
    arrive(copies)


def prepare(ids, pivots, points, mine, other, targets):
    size, count, dim = pivots.shape[1], *points.shape
    width = dim + 3 * mine.shape[1] + 128
    full = (count, 2 * mine.shape[1])
    return pl.pallas_call(
        prepare_kernel,
        out_shape=(
            jax.ShapeDtypeStruct((size, width), bf16),
            jax.ShapeDtypeStruct(full, f32),
            jax.ShapeDtypeStruct((count // 2 + 16, dim), bf16),
        ),
        in_specs=[scalar, whole, far, far, far, whole],
        out_specs=(far, far, whole),
        scratch_shapes=[
            pltpu.VMEM(points.shape, bf16),
            pltpu.VMEM(mine.shape, f32),
            pltpu.VMEM(mine.shape, f32),
            pltpu.VMEM((size, width), bf16),
            pltpu.VMEM(full, f32),
            pltpu.SemaphoreType.DMA((20,)),
        ],
        compiler_params=params,
        name="prepare",
    )(ids, pivots, points, mine, other, targets)


def to_column(row):
    blocks = [
        jnp.transpose(jnp.broadcast_to(row[:, k : k + 128], (128, 128)))
        for k in range(0, row.shape[1], 128)
    ]
    return jnp.concatenate(blocks, axis=0)


def to_row(column):
    blocks = [
        jnp.transpose(jnp.broadcast_to(column[k : k + 128], (128, 128)))[:1]
        for k in range(0, column.shape[0], 128)
    ]
    return jnp.concatenate(blocks, axis=1)


def columns_kernel(
    ids, points_in, came_in, swapped_in, old_in, targets,
    columns_out, block_out, gram_out, old_core_out, old_proj,
    points, came, swapped, old_full, columns, block, gram, old_core, sems,
):
    mover = Mover(sems)
    early = mover.start(points_in, points) + mover.start(came_in, came)
    late = mover.start(swapped_in, swapped) + mover.start(old_in, old_full)
    arrive(early)
    first = ids[1] == 0
    dim = points.shape[1]
    size = came.shape[0]
    cols = size // 2
    rate = -2.0 / dim
    pivot_points = came[:, :dim]
    wide = points[...].astype(f32)
    pivot_wide = pivot_points.astype(f32)
    squares = pivot_wide * pivot_wide
    norms = jnp.sum(wide * wide, axis=1, keepdims=True)
    pivot_column = jnp.sum(squares, axis=1, keepdims=True)
    pivot_row = dot(jnp.ones((8, dim), f32), squares, ((1,), (1,)))[:1]
    inner = narrow_dot(points[...], pivot_points)
    values = jnp.exp(rate * jnp.maximum(norms + pivot_row - 2.0 * inner, 0.0))
    arrive(late)
    mine, other = came[:, dim : dim + cols], swapped[:, dim : dim + cols]
    pivot_old = jnp.concatenate(
        [jnp.where(first, mine, other), jnp.where(first, other, mine)], axis=1
    )
    high = old_full[...].astype(bf16)
    low = (old_full[...] - high.astype(f32)).astype(bf16)
    values = values - (narrow_dot(high, pivot_old) + narrow_dot(low, pivot_old))
    columns[...] = values
    copies = mover.start(columns, columns_out)
    inner = narrow_dot(pivot_points, pivot_points)
    square = jnp.exp(rate * jnp.maximum(pivot_column + pivot_row - 2.0 * inner, 0.0))
    square = square - narrow_dot(pivot_old, pivot_old)
    eye = lax.broadcasted_iota(jnp.int32, (size, size), 0) == lax.broadcasted_iota(jnp.int32, (size, size), 1)
    shift = jnp.where(eye, ridge_shift, 0.0)
    block[...] = square + shift

    copies += mover.start(block, block_out)

    def old_half(ref):
        start = dim + cols
        return ref[:, start : start + cols].astype(f32) + ref[:, start + cols : start + 2 * cols].astype(f32)

    mine, other = old_half(came), old_half(swapped)
    old_core[:, :cols] = jnp.where(first, mine, other) + shift[:, :cols]
    old_core[:, cols:] = jnp.where(first, other, mine) + shift[:, cols:]
    pieces = came[:, dim + 3 * cols :].astype(f32)
    old_proj[...] = to_row(pieces[:, 0:1] + pieces[:, 1:2] + pieces[:, 2:3])
    copies += mover.start(old_core, old_core_out)

    @pl.when(first)
    def _():
        gram[...] = dot(old_full[...], columns[...], ((0,), (0,)))

    @pl.when(ids[1] == 1)
    def _():
        gram[...] = dot(columns[...], columns[...], ((0,), (0,)))
        proj = dot(jnp.broadcast_to(targets[...], (8, targets.shape[1])), columns[...], ((1,), (0,)))
        gram[size - 2 : size - 1, :cols] = proj[:1, :cols]
        gram[size - 1 : size, :cols] = proj[:1, cols:]

    copies += mover.start(gram, gram_out)
    arrive(copies)


def pivot_columns(ids, points, came, swapped, old_full, targets):
    count, size = points.shape[0], came.shape[0]
    square = jax.ShapeDtypeStruct((size, size), f32)
    return pl.pallas_call(
        columns_kernel,
        out_shape=(
            jax.ShapeDtypeStruct((count, size), f32), square, square, square,
            jax.ShapeDtypeStruct((1, size), f32),
        ),
        in_specs=[scalar] + [far] * 4 + [whole],
        out_specs=(far, far, far, far, whole),
        scratch_shapes=[
            pltpu.VMEM(points.shape, bf16),
            pltpu.VMEM(came.shape, bf16),
            pltpu.VMEM(came.shape, bf16),
            pltpu.VMEM(old_full.shape, f32),
            pltpu.VMEM((count, size), f32),
        ]
        + [pltpu.VMEM((size, size), f32)] * 3
        + [pltpu.SemaphoreType.DMA((32,))],
        compiler_params=params,
        name="pivot_columns",
    )(ids, points, came, swapped, old_full, targets)


def across(matrix, row):
    return jnp.sum(matrix * row, axis=1, keepdims=True)


def down(matrix, column):
    return jnp.sum(matrix * column, axis=0, keepdims=True)


def solve(old_inverse, cross_low, schur_inverse, old_side, new_side):
    up = across(old_inverse[...], old_side)
    middle = across(schur_inverse[...], new_side - down(cross_low[...], up))
    new_coef = down(schur_inverse[...], middle)
    old_coef = down(old_inverse[...], up - across(cross_low[...], new_coef))
    return old_coef, new_coef


def fit(coefs, old_full, columns):
    return across(old_full[...], coefs[0]) + across(columns[...], coefs[1])


def core_kernel(
    ids, old_inverse_in, block_in, mine_in, other_in, old_proj, old_in, columns_in, targets,
    cross_out, schur_out, new_proj, direction, weights,
    old_inverse, block, mine, other, cross_low, schur_inverse, old_full, columns,
    left, part, inverse, sems,
):
    mover = Mover(sems)
    both_parts = mover.start(mine_in, mine) + mover.start(other_in, other)
    first_copy = mover.start(old_inverse_in, old_inverse)
    second_copy = mover.start(block_in, block)
    late = mover.start(old_in, old_full) + mover.start(columns_in, columns)
    arrive(both_parts)
    size = block.shape[0]
    mid = size // 2
    first = ids[1] == 0
    cross = jnp.where(first, mine[...], other[...])
    schur_inverse[...] = jnp.where(first, other[...], mine[...])
    new_proj[:, :mid] = schur_inverse[size - 2 : size - 1, :mid]
    new_proj[:, mid:] = schur_inverse[size - 1 : size, :mid]
    for start in range(0, mid, 128):
        turned = jnp.transpose(schur_inverse[start : start + 128, size - 128 :])
        schur_inverse[size - 2 :, start : start + 128] = turned[126:]
    arrive(first_copy)
    cross_low[...] = dot(old_inverse[...], cross, ((1,), (0,)))
    copies = mover.start(cross_low, cross_out)
    arrive(second_copy)
    schur_inverse[...] = (
        ridge_shift * block[...]
        + schur_inverse[...]
        - dot(cross_low[...], cross_low[...], ((0,), (0,)))
    )
    chol_inverse(schur_inverse, left, part, inverse)
    copies += mover.start(schur_inverse, schur_out)
    arrive(late)
    coefs = solve(old_inverse, cross_low, schur_inverse, old_proj[...], new_proj[...])
    value = (targets[...] - to_row(fit(coefs, old_full, columns))) * (1.0 / ridge_shift)
    direction[...] = value
    half = value.shape[1] // 2
    mine_half = jnp.where(first, value[:, :half], value[:, half:])
    weights[...] = jnp.broadcast_to(mine_half[None], weights.shape)
    arrive(copies)


def core_solve(ids, old_inverse, block, mine, other, old_proj, old_full, columns, targets, parts):
    size, count = block.shape[0], columns.shape[0]
    square = jax.ShapeDtypeStruct((size, size), f32)
    return pl.pallas_call(
        core_kernel,
        out_shape=(
            square,
            square,
            jax.ShapeDtypeStruct((1, size), f32),
            jax.ShapeDtypeStruct((1, count), f32),
            jax.ShapeDtypeStruct((parts, 1, count // 2), f32),
        ),
        in_specs=[scalar] + [far] * 4 + [whole] + [far] * 2 + [whole],
        out_specs=(far, far, whole, whole, whole),
        scratch_shapes=[pltpu.VMEM((size, size), f32)] * 6
        + [pltpu.VMEM((count, size), f32)] * 2
        + factor_scratch(size)
        + [pltpu.SemaphoreType.DMA((32,))],
        compiler_params=params,
        name="core_solve",
    )(ids, old_inverse, block, mine, other, old_proj, old_full, columns, targets)


def rows_kernel(
    scale, stride, half, ids, points, others, weights, old_in, columns_in, direction, targets,
    rows, sums, left, acc, old_full, columns, sems,
):
    count, dim = points.shape
    step = pl.program_id(0)

    @pl.when(step == 0)
    def _():
        mover = Mover(sems)
        mover.start(old_in, old_full)
        mover.start(columns_in, columns)
        acc[...] = jnp.zeros_like(acc)
        wide = points[...].astype(f32)
        rest = -0.5 * jnp.sum(wide * wide, axis=1, keepdims=True)
        lane = lax.broadcasted_iota(jnp.int32, (count, dim), 1)
        extra = jnp.zeros((count, dim), f32)
        for k in range(3):
            piece = rest.astype(bf16).astype(f32)
            extra = jnp.where(lane == k, piece, extra)
            rest = rest - piece
        left[:, :dim] = points[...]
        left[:, dim:] = extra.astype(bf16)

    lane = lax.broadcasted_iota(jnp.int32, (256, dim), 1)
    ones = jnp.where(lane < 3, 1.0, 0.0).astype(bf16)
    groups = half // 128
    chips = others.shape[0] // stride
    total = acc[...]
    for pair in range(chips // 2):
        tiles = []
        for chip in (2 * pair, 2 * pair + 1):
            base = chip * stride
            pieces = others[base + half : base + half + 16, :].astype(f32)
            shift = scale * (pieces[:groups] + pieces[groups : 2 * groups] + pieces[2 * groups : 3 * groups])
            weight = weights[2 * chip + ids[1]]
            for g in range(groups):
                tiles.append(
                    (
                        others[base + 128 * g : base + 128 * g + 128, :],
                        shift[g : g + 1],
                        weight[:, 128 * g : 128 * g + 128],
                    )
                )
        for k in range(0, len(tiles), 2):
            one, two = tiles[k], tiles[k + 1]
            right = jnp.concatenate([jnp.concatenate([one[0], two[0]], axis=0), ones], axis=1)
            inner = narrow_dot(left[...], right) * scale
            one_value = jnp.exp2(jnp.minimum(inner[:, :128] + one[1], 0.0)) * one[2]
            two_value = jnp.exp2(jnp.minimum(inner[:, 128:] + two[1], 0.0)) * two[2]
            total = total + (one_value + two_value)
    acc[...] = total

    @pl.when(step == pl.num_programs(0) - 1)
    def _():
        mover = Mover(sems)
        arrive(mover.plan(old_in, old_full) + mover.plan(columns_in, columns))
        mine = jnp.sum(acc[...], axis=1, keepdims=True)
        rows[...] = to_row(mine)
        image = mine + (0.5 * ridge_shift) * to_column(direction[...])[:, :1]
        size = old_full.shape[1]
        flat = (sums.shape[0], 1)
        sums[:, :, :size] = jnp.broadcast_to(down(old_full[...], image)[None], flat + (size,))
        sums[:, :, size : 2 * size] = jnp.broadcast_to(down(columns[...], image)[None], flat + (size,))
        along_image = jnp.sum(to_row(image) * direction[...], axis=1, keepdims=True)
        along_targets = 0.5 * jnp.sum(targets[...] * direction[...], axis=1, keepdims=True)
        place = lax.broadcasted_iota(jnp.int32, (1, 128), 1)
        last = jnp.where(place == 0, along_image, jnp.where(place == 1, along_targets, 0.0))
        sums[:, :, 2 * size :] = jnp.broadcast_to(last[None], flat + (128,))


def kernel_rows(ids, points, others, stride, weights, old_full, columns, direction, targets):
    count, dim = points.shape
    parts = weights.shape[0]
    chips = parts // 2
    scale = 2.0 * (2.0 / dim) * math.log2(math.e)
    steps = 8
    size = others.shape[0] // steps
    width = old_full.shape[1] + columns.shape[1] + 128

    def fixed(array):
        return pl.BlockSpec(array.shape, lambda i: (0,) * array.ndim)

    return pl.pallas_call(
        lambda *refs: rows_kernel(scale, stride, weights.shape[2], *refs),
        grid=(steps,),
        in_specs=[
            scalar,
            fixed(points),
            pl.BlockSpec((size, dim), lambda i: (i, 0)),
            pl.BlockSpec((parts // steps, 1, weights.shape[2]), lambda i: (i, 0, 0)),
            far,
            far,
            fixed(direction),
            fixed(targets),
        ],
        out_specs=(
            pl.BlockSpec((1, count), lambda i: (0, 0)),
            pl.BlockSpec((parts, 1, width), lambda i: (0, 0, 0)),
        ),
        out_shape=(
            jax.ShapeDtypeStruct((1, count), f32),
            jax.ShapeDtypeStruct((parts, 1, width), f32),
        ),
        scratch_shapes=[
            pltpu.VMEM((count, 2 * dim), bf16),
            pltpu.VMEM((count, 128), f32),
            pltpu.VMEM(old_full.shape, f32),
            pltpu.VMEM(columns.shape, f32),
            pltpu.SemaphoreType.DMA((8,)),
        ],
        compiler_params=params,
        name="kernel_rows",
    )(ids, points, others, weights, old_full, columns, direction, targets)


def tail_kernel(
    sums_in, mine, other, old_inverse_in, cross_in, schur_in, old_proj, new_proj,
    old_in, columns_in, direction, targets, answer, residual, preconditioned,
    sums, old_inverse, cross_low, schur_inverse, old_full, columns, sems,
):
    mover = Mover(sems)
    early = mover.start(sums_in, sums)
    copies = mover.start(old_inverse_in, old_inverse)
    copies += mover.start(cross_in, cross_low)
    copies += mover.start(schur_in, schur_inverse)
    late = mover.start(old_in, old_full) + mover.start(columns_in, columns)
    arrive(early)
    size = old_proj.shape[1]
    total = jnp.sum(sums[...], axis=0)
    alpha = total[:, 2 * size + 1 : 2 * size + 2] / total[:, 2 * size : 2 * size + 1]
    step = alpha * direction[...]
    answer[...] = step[0]
    left = targets[...] - alpha * (mine[...] + other[...]) - ridge_shift * step
    residual[...] = left[0]
    arrive(copies)
    coefs = solve(
        old_inverse, cross_low, schur_inverse,
        old_proj[...] - alpha * total[:, :size], new_proj[...] - alpha * total[:, size : 2 * size],
    )
    arrive(late)
    preconditioned[...] = ((left - to_row(fit(coefs, old_full, columns))) * (1.0 / ridge_shift))[0]


def tail(*args):
    row = jax.ShapeDtypeStruct(args[1].shape[1:], f32)
    size = args[3].shape[0]
    tall = args[8].shape
    return pl.pallas_call(
        tail_kernel,
        out_shape=(row,) * 3,
        in_specs=[far] + [whole] * 2 + [far] * 3 + [whole] * 2 + [far] * 2 + [whole] * 2,
        out_specs=(whole,) * 3,
        scratch_shapes=[pltpu.VMEM(args[0].shape, f32)]
        + [pltpu.VMEM((size, size), f32)] * 3
        + [pltpu.VMEM(tall, f32)] * 2
        + [pltpu.SemaphoreType.DMA((24,))],
        compiler_params=params,
        name="tail",
    )(*args)


def exchange(pieces, axes):
    return lax.all_to_all(pieces, axes, 0, 0, tiled=True)


def spread(piece, count, axes):
    return exchange(jnp.broadcast_to(piece[None], (count,) + piece.shape), axes)


def split(rest, count):
    pieces = []
    for _ in range(count):
        piece = lax.reduce_precision(rest, 8, 7)
        pieces.append(piece.astype(bf16))
        rest = rest - piece
    return pieces


def swap(value):
    return lax.ppermute(value, "sub", [(0, 1), (1, 0)])


def local(points, old_factor, targets, pivots):
    count, dim = points.shape
    size = pivots.shape[0]
    part = lax.axis_index("sub")
    chips = lax.axis_size("rows")
    parts = 2 * chips
    each = size // chips
    cols = old_factor.shape[1]
    first = lax.axis_index("rows") * count
    ids = jnp.stack([first, part]).astype(jnp.int32)
    row = targets.reshape(1, count)

    sent, old_full, near = prepare(ids, pivots.reshape(1, size), points, old_factor, swap(old_factor), row)
    others = lax.all_gather(near, "rows", axis=0, tiled=True)
    width = sent.shape[1]
    came = exchange(sent.reshape(chips, each, width), "rows")
    kept = jnp.sum(came.astype(f32), axis=0)
    start = dim + cols
    gram = kept[:, start : start + cols] + kept[:, start + cols : start + 2 * cols]
    proj = jnp.sum(kept[:, start + 2 * cols : start + 2 * cols + 3], axis=1, keepdims=True)
    kept = jnp.concatenate(
        [kept[:, :start].astype(bf16)]
        + split(gram, 2)
        + [jnp.pad(jnp.concatenate(split(proj, 3), axis=1), ((0, 0), (0, 125)))],
        axis=1,
    )
    came = spread(kept, chips, "rows").reshape(size, width)
    swapped = swap(came)

    columns, block, gram, old_core, old_proj = pivot_columns(
        ids, points, came, swapped, old_full, row
    )
    came = exchange(gram.reshape(chips, each, size), "rows")
    block_inverse = factor(block)
    came, block_inverse = lax.optimization_barrier((came, block_inverse))
    mine = exchange(sum_spread(came), "rows").reshape(size, size)
    old_inverse = factor(old_core)
    mine, old_inverse = lax.optimization_barrier((mine, old_inverse))
    other = swap(mine)

    cross_low, schur_inverse, new_proj, direction, weights = core_solve(
        ids, old_inverse, block, mine, other, old_proj, old_full, columns, row, parts
    )
    weights = exchange(weights, everyone)
    chosen = lax.dynamic_slice_in_dim(block_inverse, part * cols, cols, 0)
    new_part = dot(columns, chosen, ((1,), (1,)))
    rows, sums = kernel_rows(
        ids, points, others, near.shape[0], weights, old_full, columns, direction, row
    )
    sums = exchange(sums, everyone)
    answer, residual, preconditioned = tail(
        sums, rows, swap(rows), old_inverse, cross_low, schur_inverse, old_proj, new_proj,
        old_full, columns, direction, row,
    )
    return new_part, answer, residual, preconditioned


def solution(mesh):
    in_specs = (P("rows", None), P("rows", "sub"), P("rows"), P())
    out_specs = (P("rows", "sub"), P("rows"), P("rows"), P("rows"))
    return jax.shard_map(local, mesh=mesh, in_specs=in_specs, out_specs=out_specs, check_vma=False)
```

```python
import math

import jax
import jax.numpy as jnp
from jax import lax
from jax.experimental import pallas as pl
from jax.experimental.pallas import tpu as pltpu
from jax.sharding import PartitionSpec as P

ridge_shift = 0.5
precise = lax.Precision.HIGHEST
everyone = ("rows", "sub")
f32, bf16 = jnp.float32, jnp.bfloat16
whole = pl.BlockSpec(memory_space=pltpu.VMEM)
far = pl.BlockSpec(memory_space=pltpu.HBM)
scalar = pl.BlockSpec(memory_space=pltpu.SMEM)


def grant(megabytes):
    return pltpu.CompilerParams(vmem_limit_bytes=megabytes << 20)


def dot(left, right, contract):
    return lax.dot_general(left, right, (contract, ((), ())), precision=precise, preferred_element_type=f32)


def pieces_of(value):
    high = value.astype(bf16)
    return high, (value - high.astype(f32)).astype(bf16)


def three_dot(left, right, contract):
    left_high, left_low = pieces_of(left)
    right_high, right_low = pieces_of(right)

    def one(a, b):
        return lax.dot_general(a, b, (contract, ((), ())), preferred_element_type=f32)

    return one(left_high, right_high) + (one(left_high, right_low) + one(left_low, right_high))


def narrow_dot(left, right):
    return lax.dot_general(left, right, (((1,), (1,)), ((), ())), preferred_element_type=f32)


def total(terms):
    while len(terms) > 1:
        terms = [terms[i] + terms[i + 1] if i + 1 < len(terms) else terms[i] for i in range(0, len(terms), 2)]
    return terms[0]

def factor_block(a, hook):
    lane = lax.broadcasted_iota(jnp.int32, (8, 128), 1)
    sub = lax.broadcasted_iota(jnp.int32, (8, 128), 0)
    full = lambda v: jnp.broadcast_to(v, (8, 128))
    rows = [a[8 * i:8 * i + 8] for i in range(16)]
    outs, pending = [], []
    def drain(n):
        for _ in range(min(n, len(pending))):
            pending.pop(0)()
    for panel in range(16):
        lo = 8 * panel
        inside = (lane >= lo) & (lane < lo + 8)
        head = rows[panel]
        cols = [full(head[:, lo + j:lo + j + 1]) for j in range(8)]
        e = {(i, j): full(cols[j][i:i + 1]) for j in range(8) for i in range(j, 8)}
        head = jnp.where(inside, (lane == lo + sub).astype(f32), head)
        base = [full(head[j:j + 1]) for j in range(8)]
        per = -(-len(pending) // 5)
        m, pieces = {}, {}
        for j in (0, 2, 4, 6):
            p, q, s = e[j, j], e[j + 1, j], e[j + 1, j + 1]
            rdet = 1.0 / (p * s - q * q)
            pieces[j] = (p, q, s, rdet)
            g = {}
            for i in range(j + 2, 8):
                x, y = e[i, j], e[i, j + 1]
                g[i] = (x * s - y * q, y * p - x * q)
            for i in range(j + 2, 8):
                for k in range(j + 2, i + 1):
                    e[i, k] = e[i, k] - (g[i][0] * e[k, j] + g[i][1] * e[k, j + 1]) * rdet
            for i in range(j + 2, 8):
                f0, f1 = g[i][0] * rdet, g[i][1] * rdet
                for k in range(j):
                    m[i, k] = m[i, k] - (f0 * m[j, k] + f1 * m[j + 1, k])
                m[i, j], m[i, j + 1] = -f0, -f1
            drain(per)
            if j == 2:
                hook(panel)
        h = [total([base[i]] + [m[i, k] * base[k] for k in range(i - i % 2)]) for i in range(8)]
        y = []
        for j in (0, 2, 4, 6):
            p, q, s, rdet = pieces[j]
            y.append((s * h[j] - q * h[j + 1]) * rdet)
            y.append((p * h[j + 1] - q * h[j]) * rdet)
        G = [total([y[l]] + [m[i, l] * y[i] for i in range(l - l % 2 + 2, 8)]) for l in range(8)]
        drain(len(pending))
        if panel < 15:
            r = rows[panel + 1]
            c = total([full(r[:, lo + j:lo + j + 1]) * G[j] for j in range(8)])
            rows[panel + 1] = jnp.where(inside, 0.0, r) - c
        if panel < 14:
            g = G[7]
            for l in range(7):
                g = jnp.where(sub == l, G[l], g)
            parts = ([jnp.zeros((lo, 128), f32)] if panel else []) + [g, jnp.zeros((120 - lo, 128), f32)]
            upd = dot(jnp.concatenate(rows[panel + 2:], 0), jnp.concatenate(parts, 0), ((1,), (0,)))

            def use(i, upd=upd, first=panel + 2, inside=inside):
                rows[i] = jnp.where(inside, 0.0, rows[i]) - upd[8 * (i - first):8 * (i - first) + 8]

            for i in range(panel + 2, 16):
                pending.append(lambda i=i, u=use: u(i))
        out = jnp.zeros((8, 128), f32)
        for j in (0, 2, 4, 6):
            p, q, s, rdet = pieces[j]
            rp = 1.0 / p
            out = jnp.where(sub == j, h[j] * lax.rsqrt(p), out)
            out = jnp.where(sub == j + 1, (h[j + 1] - (q * rp) * h[j]) * lax.rsqrt(s - q * (q * rp)), out)
        outs.append(out)
    low = lax.broadcasted_iota(jnp.int32, (128, 128), 0) >= lax.broadcasted_iota(jnp.int32, (128, 128), 1)
    return jnp.where(low, jnp.concatenate(outs, 0), 0.0)

def chol_inverse(ref, left, block, inverse):
    size = ref.shape[0]
    blocks = size // 128
    row = lax.broadcasted_iota(jnp.int32, (size, 128), 0)
    lane = lax.broadcasted_iota(jnp.int32, (128, size), 1)
    block[...] = ref[:128, :128]
    inverse[...] = jnp.zeros_like(inverse)

    def finish(here, off):
        inside = (lane >= off) & (lane < off + 128)
        return dot(inverse[...], jnp.where(inside, 0.0, ref[here, :]), ((1,), (0,)))

    def step(k, carry):
        off = pl.multiple_of(k * 128, 128)
        prev = pl.multiple_of(jnp.maximum(off - 128, 0), 128)
        here, before = pl.ds(off, 128), pl.ds(prev, 128)

        def hook(panel):
            if panel == 0:
                value = dot(ref[:, before], inverse[...], ((1,), (1,)))
                left[...] = jnp.where((row >= off) & (off > 0), value, 0.0)
            elif panel == 2:
                ref[before, :] = jnp.where(off > 0, finish(before, prev), ref[before, :])
                ref[before, before] = jnp.where(off > 0, inverse[...], ref[before, before])
            elif panel % 3 == 1 and panel // 3 - 1 in range(blocks):
                c = panel // 3 - 1
                lanes = slice(128 * c, 128 * c + 128)
                gone = (off > 0) & (prev == 128 * c)
                old = ref[:, lanes]
                upd = dot(left[...], ref[before, lanes], ((1,), (0,)))
                ref[:, lanes] = jnp.where(row >= off, jnp.where(gone, 0.0, old) - upd, old)

        value = factor_block(block[...], hook)
        after = pl.multiple_of(jnp.minimum(off + 128, size - 128), 128)
        after = pl.ds(after, 128)
        part = dot(ref[after, here], value, ((1,), (1,)))
        block[...] = ref[after, after] - dot(part, part, ((1,), (1,)))
        inverse[...] = value
        return carry

    lax.fori_loop(0, blocks, step, 0)
    last = slice(size - 128, size)
    ref[last, :] = finish(last, size - 128)
    ref[last, last] = inverse[...]
    rows = lax.broadcasted_iota(jnp.int32, (size, size), 0)
    lanes = lax.broadcasted_iota(jnp.int32, (size, size), 1)
    ref[...] = jnp.where(rows >= lanes, ref[...], 0.0)


def factor_scratch(size):
    return [pltpu.VMEM((size, 128), f32), pltpu.VMEM((128, 128), f32), pltpu.VMEM((128, 128), f32)]


class Mover:
    def __init__(self, sems):
        self.sems, self.used = sems, 0

    def plan(self, source, target, pieces=4):
        rows = source.shape[0] // pieces
        copies = []
        for k in range(pieces):
            here = pl.ds(k * rows, rows)
            copies.append(pltpu.make_async_copy(source.at[here], target.at[here], self.sems.at[self.used]))
            self.used += 1
        return copies

    def start(self, source, target):
        copies = self.plan(source, target)
        for copy in copies:
            copy.start()
        return copies


def arrive(copies):
    for copy in copies:
        copy.wait()


def factor_kernel(matrix, out, work, left, block, inverse, sems):
    mover = Mover(sems)
    arrive(mover.start(matrix, work))
    chol_inverse(work, left, block, inverse)
    arrive(mover.start(work, out))


def factor(matrix):
    size = matrix.shape[0]
    return pl.pallas_call(
        factor_kernel,
        out_shape=jax.ShapeDtypeStruct(matrix.shape, f32),
        in_specs=[far],
        out_specs=far,
        scratch_shapes=[pltpu.VMEM((size, size), f32)] + factor_scratch(size) + [pltpu.SemaphoreType.DMA((8,))],
        compiler_params=grant(57),
        cost_estimate=pl.CostEstimate(flops=120 * size**3, bytes_accessed=8 * size**2, transcendentals=0),
        name="factor",
    )(matrix)


def sum_kernel(came, out, work, sems):
    work[...] = jnp.broadcast_to(jnp.sum(came[...], axis=0)[None], work.shape)
    arrive(Mover(sems).start(work, out))


def sum_spread(came):
    return pl.pallas_call(
        sum_kernel,
        out_shape=jax.ShapeDtypeStruct(came.shape, f32),
        in_specs=[whole],
        out_specs=far,
        scratch_shapes=[pltpu.VMEM(came.shape, f32), pltpu.SemaphoreType.DMA((4,))],
        compiler_params=grant(24),
        name="sum_spread",
    )(came)


def prepare_kernel(
    ids, pivots, points, mine, other, targets, sent, old_full, near,
):
    size, count = pivots.shape[1], points.shape[0]
    dim, cols = points.shape[1], mine.shape[1]
    first = ids[1] == 0
    places = ids[0] + lax.broadcasted_iota(jnp.int32, (size, count), 1)
    wanted_ids = jnp.concatenate([to_column(pivots[...].astype(f32))] * (count // 128), axis=1)
    picks = jnp.where(wanted_ids == places.astype(f32), 1.0, 0.0).astype(bf16)
    wanted = jnp.concatenate([points[...], mine[...].astype(bf16)], axis=1)
    picked = lax.dot_general(picks, wanted, (((1,), (0,)), ((), ())), preferred_element_type=f32)
    sent[:, dim : dim + cols] = picked[:, dim:].astype(bf16)
    old_full[:, :cols] = jnp.where(first, mine[...], other[...])
    old_full[:, cols:] = jnp.where(first, other[...], mine[...])
    wide = jnp.concatenate([mine[...], to_column(targets[...])], axis=1)
    gram = dot(old_full[...], wide, ((0,), (0,)))
    rest = gram[:, :cols]
    for k in range(2):
        piece = rest.astype(bf16)
        start = dim + cols + k * cols
        sent[:, start : start + cols] = piece
        rest = rest - piece.astype(f32)
    rest = gram[:, cols:]
    lane = lax.broadcasted_iota(jnp.int32, (size, 128), 1)
    proj = jnp.zeros((size, 128), f32)
    for k in range(3):
        piece = rest.astype(bf16).astype(f32)
        proj = jnp.where(lane == k, piece, proj)
        rest = rest - piece
    sent[:, :dim] = jnp.where(first, picked[:, :dim], proj).astype(bf16)

    half = count // 2
    wide = jnp.where(first, points[:half].astype(f32), points[half:].astype(f32))
    rest = to_row(-0.5 * jnp.sum(wide * wide, axis=1, keepdims=True))
    near[:half] = wide.astype(bf16)
    pieces = []
    for _ in range(3):
        piece = rest.astype(bf16).astype(f32)
        pieces += [piece[:, k : k + dim] for k in range(0, half, dim)]
        rest = rest - piece
    pieces.append(jnp.zeros((16 - len(pieces), dim), f32))
    near[half:] = jnp.concatenate(pieces, axis=0).astype(bf16)


def prepare(ids, pivots, points, mine, other, targets):
    size, count, dim = pivots.shape[1], *points.shape
    width = dim + 3 * mine.shape[1]
    return pl.pallas_call(
        prepare_kernel,
        out_shape=(
            jax.ShapeDtypeStruct((size, width), bf16),
            jax.ShapeDtypeStruct((count, 2 * mine.shape[1]), f32),
            jax.ShapeDtypeStruct((count // 2 + 16, dim), bf16),
        ),
        in_specs=[scalar] + [whole] * 5,
        out_specs=(whole,) * 3,
        compiler_params=grant(24),
        name="prepare",
    )(ids, pivots, points, mine, other, targets)


def to_column(row):
    blocks = [
        jnp.transpose(jnp.broadcast_to(row[:, k : k + 128], (128, 128)))
        for k in range(0, row.shape[1], 128)
    ]
    return jnp.concatenate(blocks, axis=0)


def to_row(column):
    blocks = [
        jnp.transpose(jnp.broadcast_to(column[k : k + 128], (128, 128)))[:1]
        for k in range(0, column.shape[0], 128)
    ]
    return jnp.concatenate(blocks, axis=1)


def columns_kernel(
    ids, points_in, came_in, swapped, old_full, targets,
    columns, block_out, gram_out, old_core_out, old_proj,
    points, came, block, gram, old_core, sems,
):
    mover = Mover(sems)
    early = mover.start(points_in, points) + mover.start(came_in, came)
    arrive(early)
    first = ids[1] == 0
    dim = points.shape[1]
    size = came.shape[0]
    cols = size // 2
    rate = -2.0 / dim
    pivot_points = jnp.where(first, came[:, :dim], swapped[:, :dim])
    wide = points[...].astype(f32)
    pivot_wide = pivot_points.astype(f32)
    squares = pivot_wide * pivot_wide
    norms = jnp.sum(wide * wide, axis=1, keepdims=True)
    pivot_column = jnp.sum(squares, axis=1, keepdims=True)
    pivot_row = dot(jnp.ones((8, dim), f32), squares, ((1,), (1,)))[:1]
    inner = narrow_dot(points[...], pivot_points)
    values = jnp.exp(rate * jnp.maximum(norms + pivot_row - 2.0 * inner, 0.0))
    mine, other = came[:, dim : dim + cols], swapped[:, dim : dim + cols]
    pivot_old = jnp.concatenate(
        [jnp.where(first, mine, other), jnp.where(first, other, mine)], axis=1
    )
    high = old_full[...].astype(bf16)
    low = (old_full[...] - high.astype(f32)).astype(bf16)
    values = values - (narrow_dot(high, pivot_old) + narrow_dot(low, pivot_old))
    columns[...] = values
    inner = narrow_dot(pivot_points, pivot_points)
    square = jnp.exp(rate * jnp.maximum(pivot_column + pivot_row - 2.0 * inner, 0.0))
    square = square - narrow_dot(pivot_old, pivot_old)
    eye = lax.broadcasted_iota(jnp.int32, (size, size), 0) == lax.broadcasted_iota(jnp.int32, (size, size), 1)
    shift = jnp.where(eye, ridge_shift, 0.0)
    block[...] = square + shift

    copies = mover.start(block, block_out)

    def old_half(ref):
        start = dim + cols
        return ref[:, start : start + cols].astype(f32) + ref[:, start + cols : start + 2 * cols].astype(f32)

    mine, other = old_half(came), old_half(swapped)
    old_core[:, :cols] = jnp.where(first, mine, other) + shift[:, :cols]
    old_core[:, cols:] = jnp.where(first, other, mine) + shift[:, cols:]
    pieces = jnp.where(first, swapped[:, :dim], came[:, :dim]).astype(f32)
    old_proj[...] = to_row(pieces[:, 0:1] + pieces[:, 1:2] + pieces[:, 2:3])
    copies += mover.start(old_core, old_core_out)

    @pl.when(first)
    def _():
        gram[...] = dot(old_full[...], columns[...], ((0,), (0,)))

    @pl.when(ids[1] == 1)
    def _():
        gram[...] = dot(columns[...], columns[...], ((0,), (0,)))
        proj = dot(jnp.broadcast_to(targets[...], (8, targets.shape[1])), columns[...], ((1,), (0,)))
        gram[size - 2 : size - 1, :cols] = proj[:1, :cols]
        gram[size - 1 : size, :cols] = proj[:1, cols:]

    copies += mover.start(gram, gram_out)
    arrive(copies)


def pivot_columns(ids, points, came, swapped, old_full, targets):
    count, size = points.shape[0], came.shape[0]
    square = jax.ShapeDtypeStruct((size, size), f32)
    return pl.pallas_call(
        columns_kernel,
        out_shape=(
            jax.ShapeDtypeStruct((count, size), f32), square, square, square,
            jax.ShapeDtypeStruct((1, size), f32),
        ),
        in_specs=[scalar, far, far] + [whole] * 3,
        out_specs=(whole, far, far, far, whole),
        scratch_shapes=[pltpu.VMEM(points.shape, bf16), pltpu.VMEM(came.shape, bf16)]
        + [pltpu.VMEM((size, size), f32)] * 3
        + [pltpu.SemaphoreType.DMA((20,))],
        compiler_params=grant(55),
        name="pivot_columns",
    )(ids, points, came, swapped, old_full, targets)


def across(matrix, row):
    return jnp.sum(matrix * row, axis=1, keepdims=True)


def down(matrix, column):
    return jnp.sum(matrix * column, axis=0, keepdims=True)


def solve(old_inverse, cross_low, schur_inverse, old_side, new_side):
    up = across(old_inverse[...], old_side)
    middle = across(schur_inverse[...], new_side - down(cross_low[...], up))
    new_coef = down(schur_inverse[...], middle)
    old_coef = down(old_inverse[...], up - across(cross_low[...], new_coef))
    return old_coef, new_coef


def fit(coefs, old_full, columns):
    return across(old_full[...], coefs[0]) + across(columns[...], coefs[1])


def core_kernel(
    ids, old_inverse_in, block_in, mine, other, old_proj, old_full, columns, targets,
    cross_out, schur_out, new_proj, direction, weights,
    old_inverse, block, cross_low, schur_inverse, left, part, inverse, sems,
):
    mover = Mover(sems)
    first_copy = mover.start(old_inverse_in, old_inverse)
    second_copy = mover.start(block_in, block)
    size = block.shape[0]
    mid = size // 2
    first = ids[1] == 0
    cross = jnp.where(first, mine[...], other[...])
    schur_inverse[...] = jnp.where(first, other[...], mine[...])
    new_proj[:, :mid] = schur_inverse[size - 2 : size - 1, :mid]
    new_proj[:, mid:] = schur_inverse[size - 1 : size, :mid]
    for start in range(0, mid, 128):
        turned = jnp.transpose(schur_inverse[start : start + 128, size - 128 :])
        schur_inverse[size - 2 :, start : start + 128] = turned[126:]
    arrive(first_copy)
    cross_low[...] = three_dot(old_inverse[...], cross, ((1,), (0,)))
    copies = mover.start(cross_low, cross_out)
    arrive(second_copy)
    schur_inverse[...] = (
        ridge_shift * block[...]
        + schur_inverse[...]
        - three_dot(cross_low[...], cross_low[...], ((0,), (0,)))
    )
    chol_inverse(schur_inverse, left, part, inverse)
    copies += mover.start(schur_inverse, schur_out)
    coefs = solve(old_inverse, cross_low, schur_inverse, old_proj[...], new_proj[...])
    value = (targets[...] - to_row(fit(coefs, old_full, columns))) * (1.0 / ridge_shift)
    direction[...] = value
    half = value.shape[1] // 2
    mine_half = jnp.where(first, value[:, :half], value[:, half:])
    weights[...] = jnp.broadcast_to(mine_half[None], weights.shape)
    arrive(copies)


def core_solve(ids, old_inverse, block, mine, other, old_proj, old_full, columns, targets, parts):
    size, count = block.shape[0], columns.shape[0]
    square = jax.ShapeDtypeStruct((size, size), f32)
    return pl.pallas_call(
        core_kernel,
        out_shape=(
            square,
            square,
            jax.ShapeDtypeStruct((1, size), f32),
            jax.ShapeDtypeStruct((1, count), f32),
            jax.ShapeDtypeStruct((parts, 1, count // 2), f32),
        ),
        in_specs=[scalar, far, far] + [whole] * 6,
        out_specs=(far, far, whole, whole, whole),
        scratch_shapes=[pltpu.VMEM((size, size), f32)] * 4
        + factor_scratch(size)
        + [pltpu.SemaphoreType.DMA((16,))],
        compiler_params=grant(54),
        name="core_solve",
    )(ids, old_inverse, block, mine, other, old_proj, old_full, columns, targets)


def rows_kernel(
    scale, stride, half, ids, points, others, weights, old_full, columns, direction, targets,
    rows, sums, left, acc,
):
    count, dim = points.shape
    step = pl.program_id(0)

    @pl.when(step == 0)
    def _():
        acc[...] = jnp.zeros_like(acc)
        wide = points[...].astype(f32)
        rest = -0.5 * jnp.sum(wide * wide, axis=1, keepdims=True)
        lane = lax.broadcasted_iota(jnp.int32, (count, dim), 1)
        extra = jnp.zeros((count, dim), f32)
        for k in range(3):
            piece = rest.astype(bf16).astype(f32)
            extra = jnp.where(lane == k, piece, extra)
            rest = rest - piece
        left[:, :dim] = points[...]
        left[:, dim:] = extra.astype(bf16)

    lane = lax.broadcasted_iota(jnp.int32, (256, dim), 1)
    ones = jnp.where(lane < 3, 1.0, 0.0).astype(bf16)
    groups = half // 128
    chips = others.shape[0] // stride
    total = acc[...]
    for pair in range(chips // 2):
        tiles = []
        for chip in (2 * pair, 2 * pair + 1):
            base = chip * stride
            pieces = others[base + half : base + half + 16, :].astype(f32)
            shift = scale * (pieces[:groups] + pieces[groups : 2 * groups] + pieces[2 * groups : 3 * groups])
            weight = weights[2 * chip + ids[1]]
            for g in range(groups):
                tiles.append(
                    (
                        others[base + 128 * g : base + 128 * g + 128, :],
                        shift[g : g + 1],
                        weight[:, 128 * g : 128 * g + 128],
                    )
                )
        for k in range(0, len(tiles), 2):
            one, two = tiles[k], tiles[k + 1]
            right = jnp.concatenate([jnp.concatenate([one[0], two[0]], axis=0), ones], axis=1)
            inner = narrow_dot(left[...], right) * scale
            one_value = jnp.exp2(jnp.minimum(inner[:, :128] + one[1], 0.0)) * one[2]
            two_value = jnp.exp2(jnp.minimum(inner[:, 128:] + two[1], 0.0)) * two[2]
            total = total + (one_value + two_value)
    acc[...] = total

    @pl.when(step == pl.num_programs(0) - 1)
    def _():
        mine = jnp.sum(acc[...], axis=1, keepdims=True)
        rows[...] = to_row(mine)
        image = mine + (0.5 * ridge_shift) * to_column(direction[...])[:, :1]
        size = old_full.shape[1]
        flat = (sums.shape[0], 1)
        sums[:, :, :size] = jnp.broadcast_to(down(old_full[...], image)[None], flat + (size,))
        sums[:, :, size : 2 * size] = jnp.broadcast_to(down(columns[...], image)[None], flat + (size,))
        along_image = jnp.sum(to_row(image) * direction[...], axis=1, keepdims=True)
        along_targets = 0.5 * jnp.sum(targets[...] * direction[...], axis=1, keepdims=True)
        place = lax.broadcasted_iota(jnp.int32, (1, 128), 1)
        last = jnp.where(place == 0, along_image, jnp.where(place == 1, along_targets, 0.0))
        sums[:, :, 2 * size :] = jnp.broadcast_to(last[None], flat + (128,))


def kernel_rows(ids, points, others, stride, weights, old_full, columns, direction, targets):
    count, dim = points.shape
    parts = weights.shape[0]
    chips = parts // 2
    scale = 2.0 * (2.0 / dim) * math.log2(math.e)
    steps = 8
    size = others.shape[0] // steps
    width = old_full.shape[1] + columns.shape[1] + 128

    def fixed(array):
        return pl.BlockSpec(array.shape, lambda i: (0,) * array.ndim)

    return pl.pallas_call(
        lambda *refs: rows_kernel(scale, stride, weights.shape[2], *refs),
        grid=(steps,),
        in_specs=[
            scalar,
            fixed(points),
            pl.BlockSpec((size, dim), lambda i: (i, 0)),
            pl.BlockSpec((parts // steps, 1, weights.shape[2]), lambda i: (i, 0, 0)),
            whole,
            whole,
            fixed(direction),
            fixed(targets),
        ],
        out_specs=(
            pl.BlockSpec((1, count), lambda i: (0, 0)),
            pl.BlockSpec((parts, 1, width), lambda i: (0, 0, 0)),
        ),
        out_shape=(
            jax.ShapeDtypeStruct((1, count), f32),
            jax.ShapeDtypeStruct((parts, 1, width), f32),
        ),
        scratch_shapes=[pltpu.VMEM((count, 2 * dim), bf16), pltpu.VMEM((count, 128), f32)],
        compiler_params=grant(55),
        name="kernel_rows",
    )(ids, points, others, weights, old_full, columns, direction, targets)


def tail_kernel(
    sums, mine, other, old_inverse_in, cross_in, schur_in, old_proj, new_proj,
    old_full, columns, direction, targets, answer, residual, preconditioned,
    old_inverse, cross_low, schur_inverse, sems,
):
    mover = Mover(sems)
    copies = mover.start(old_inverse_in, old_inverse)
    copies += mover.start(cross_in, cross_low)
    copies += mover.start(schur_in, schur_inverse)
    size = old_proj.shape[1]
    total = jnp.sum(sums[...], axis=0)
    alpha = total[:, 2 * size + 1 : 2 * size + 2] / total[:, 2 * size : 2 * size + 1]
    step = alpha * direction[...]
    answer[...] = step[0]
    left = targets[...] - alpha * (mine[...] + other[...]) - ridge_shift * step
    residual[...] = left[0]
    arrive(copies)
    coefs = solve(
        old_inverse, cross_low, schur_inverse,
        old_proj[...] - alpha * total[:, :size], new_proj[...] - alpha * total[:, size : 2 * size],
    )
    preconditioned[...] = ((left - to_row(fit(coefs, old_full, columns))) * (1.0 / ridge_shift))[0]


def tail(*args):
    row = jax.ShapeDtypeStruct(args[1].shape[1:], f32)
    size = args[3].shape[0]
    return pl.pallas_call(
        tail_kernel,
        out_shape=(row,) * 3,
        in_specs=[whole] * 3 + [far] * 3 + [whole] * (len(args) - 6),
        out_specs=(whole,) * 3,
        scratch_shapes=[pltpu.VMEM((size, size), f32)] * 3 + [pltpu.SemaphoreType.DMA((12,))],
        compiler_params=grant(55),
        name="tail",
    )(*args)


def exchange(pieces, axes):
    return lax.all_to_all(pieces, axes, 0, 0, tiled=True)


def spread(piece, count, axes):
    return exchange(jnp.broadcast_to(piece[None], (count,) + piece.shape), axes)


def split(rest, count):
    pieces = []
    for _ in range(count):
        piece = lax.reduce_precision(rest, 8, 7)
        pieces.append(piece.astype(bf16))
        rest = rest - piece
    return pieces


def swap(value):
    return lax.ppermute(value, "sub", [(0, 1), (1, 0)])


def local(points, old_factor, targets, pivots):
    count, dim = points.shape
    size = pivots.shape[0]
    part = lax.axis_index("sub")
    chips = lax.axis_size("rows")
    parts = 2 * chips
    each = size // chips
    cols = old_factor.shape[1]
    first = lax.axis_index("rows") * count
    ids = jnp.stack([first, part]).astype(jnp.int32)
    row = targets.reshape(1, count)

    sent, old_full, near = prepare(ids, pivots.reshape(1, size), points, old_factor, swap(old_factor), row)
    others = lax.all_gather(near, "rows", axis=0, tiled=True)
    width = sent.shape[1]
    came = exchange(sent.reshape(chips, each, width), "rows")
    kept = jnp.sum(came.astype(f32), axis=0)
    start = dim + cols
    gram = kept[:, start : start + cols] + kept[:, start + cols : start + 2 * cols]
    proj = jnp.sum(kept[:, :3], axis=1, keepdims=True)
    proj = jnp.pad(jnp.concatenate(split(proj, 3), axis=1), ((0, 0), (0, dim - 3)))
    kept = jnp.concatenate(
        [jnp.where(part == 0, kept[:, :dim].astype(bf16), proj), kept[:, dim:start].astype(bf16)]
        + split(gram, 2),
        axis=1,
    )
    came = spread(kept, chips, "rows").reshape(size, width)
    swapped = swap(came)

    columns, block, gram, old_core, old_proj = pivot_columns(
        ids, points, came, swapped, old_full, row
    )
    came = exchange(gram.reshape(chips, each, size), "rows")
    block_inverse = factor(block)
    came, block_inverse = lax.optimization_barrier((came, block_inverse))
    mine = exchange(sum_spread(came), "rows").reshape(size, size)
    old_inverse = factor(old_core)
    mine, old_inverse = lax.optimization_barrier((mine, old_inverse))
    other = swap(mine)

    cross_low, schur_inverse, new_proj, direction, weights = core_solve(
        ids, old_inverse, block, mine, other, old_proj, old_full, columns, row, parts
    )
    weights = exchange(weights, everyone)
    chosen = lax.dynamic_slice_in_dim(block_inverse, part * cols, cols, 0)
    new_part = dot(columns, chosen, ((1,), (1,)))
    rows, sums = kernel_rows(
        ids, points, others, near.shape[0], weights, old_full, columns, direction, row
    )
    sums = exchange(sums, everyone)
    answer, residual, preconditioned = tail(
        sums, rows, swap(rows), old_inverse, cross_low, schur_inverse, old_proj, new_proj,
        old_full, columns, direction, row,
    )
    return new_part, answer, residual, preconditioned


def solution(mesh):
    in_specs = (P("rows", None), P("rows", "sub"), P("rows"), P())
    out_specs = (P("rows", "sub"), P("rows"), P("rows"), P("rows"))
    return jax.shard_map(local, mesh=mesh, in_specs=in_specs, out_specs=out_specs, check_vma=False)
```

```python
import math

import jax
import jax.numpy as jnp
from jax import lax
from jax.experimental import pallas as pl
from jax.experimental.pallas import tpu as pltpu
from jax.sharding import PartitionSpec as P

ridge_shift = 0.5
precise = lax.Precision.HIGHEST
everyone = ("rows", "sub")
f32, bf16 = jnp.float32, jnp.bfloat16
whole = pl.BlockSpec(memory_space=pltpu.VMEM)
far = pl.BlockSpec(memory_space=pltpu.HBM)
scalar = pl.BlockSpec(memory_space=pltpu.SMEM)


def grant(megabytes):
    return pltpu.CompilerParams(vmem_limit_bytes=megabytes << 20)


def dot(left, right, contract):
    return lax.dot_general(left, right, (contract, ((), ())), precision=precise, preferred_element_type=f32)


def pieces_of(value):
    high = value.astype(bf16)
    return high, (value - high.astype(f32)).astype(bf16)


def three_dot(left, right, contract):
    left_high, left_low = pieces_of(left)
    right_high, right_low = pieces_of(right)

    def one(a, b):
        return lax.dot_general(a, b, (contract, ((), ())), preferred_element_type=f32)

    return one(left_high, right_high) + (one(left_high, right_low) + one(left_low, right_high))


def narrow_dot(left, right):
    return lax.dot_general(left, right, (((1,), (1,)), ((), ())), preferred_element_type=f32)


def total(terms):
    while len(terms) > 1:
        terms = [terms[i] + terms[i + 1] if i + 1 < len(terms) else terms[i] for i in range(0, len(terms), 2)]
    return terms[0]

def factor_block(a, hook):
    lane = lax.broadcasted_iota(jnp.int32, (8, 128), 1)
    sub = lax.broadcasted_iota(jnp.int32, (8, 128), 0)
    full = lambda v: jnp.broadcast_to(v, (8, 128))
    rows = [a[8 * i:8 * i + 8] for i in range(16)]
    outs, pending = [], []
    def drain(n):
        for _ in range(min(n, len(pending))):
            pending.pop(0)()
    for panel in range(16):
        lo = 8 * panel
        inside = (lane >= lo) & (lane < lo + 8)
        head = rows[panel]
        cols = [full(head[:, lo + j:lo + j + 1]) for j in range(8)]
        e = {(i, j): full(cols[j][i:i + 1]) for j in range(8) for i in range(j, 8)}
        head = jnp.where(inside, (lane == lo + sub).astype(f32), head)
        base = [full(head[j:j + 1]) for j in range(8)]
        per = -(-len(pending) // 5)
        m, pieces = {}, {}
        for j in (0, 2, 4, 6):
            p, q, s = e[j, j], e[j + 1, j], e[j + 1, j + 1]
            rdet = 1.0 / (p * s - q * q)
            pieces[j] = (p, q, s, rdet)
            g = {}
            for i in range(j + 2, 8):
                x, y = e[i, j], e[i, j + 1]
                g[i] = (x * s - y * q, y * p - x * q)
            for i in range(j + 2, 8):
                for k in range(j + 2, i + 1):
                    e[i, k] = e[i, k] - (g[i][0] * e[k, j] + g[i][1] * e[k, j + 1]) * rdet
            for i in range(j + 2, 8):
                f0, f1 = g[i][0] * rdet, g[i][1] * rdet
                for k in range(j):
                    m[i, k] = m[i, k] - (f0 * m[j, k] + f1 * m[j + 1, k])
                m[i, j], m[i, j + 1] = -f0, -f1
            drain(per)
            if j == 2:
                hook(panel)
        h = [total([base[i]] + [m[i, k] * base[k] for k in range(i - i % 2)]) for i in range(8)]
        y = []
        for j in (0, 2, 4, 6):
            p, q, s, rdet = pieces[j]
            y.append((s * h[j] - q * h[j + 1]) * rdet)
            y.append((p * h[j + 1] - q * h[j]) * rdet)
        G = [total([y[l]] + [m[i, l] * y[i] for i in range(l - l % 2 + 2, 8)]) for l in range(8)]
        drain(len(pending))
        if panel < 15:
            r = rows[panel + 1]
            c = total([full(r[:, lo + j:lo + j + 1]) * G[j] for j in range(8)])
            rows[panel + 1] = jnp.where(inside, 0.0, r) - c
        if panel < 14:
            g = G[7]
            for l in range(7):
                g = jnp.where(sub == l, G[l], g)
            parts = ([jnp.zeros((lo, 128), f32)] if panel else []) + [g, jnp.zeros((120 - lo, 128), f32)]
            upd = dot(jnp.concatenate(rows[panel + 2:], 0), jnp.concatenate(parts, 0), ((1,), (0,)))

            def use(i, upd=upd, first=panel + 2, inside=inside):
                rows[i] = jnp.where(inside, 0.0, rows[i]) - upd[8 * (i - first):8 * (i - first) + 8]

            for i in range(panel + 2, 16):
                pending.append(lambda i=i, u=use: u(i))
        out = jnp.zeros((8, 128), f32)
        for j in (0, 2, 4, 6):
            p, q, s, rdet = pieces[j]
            rp = 1.0 / p
            out = jnp.where(sub == j, h[j] * lax.rsqrt(p), out)
            out = jnp.where(sub == j + 1, (h[j + 1] - (q * rp) * h[j]) * lax.rsqrt(s - q * (q * rp)), out)
        outs.append(out)
    low = lax.broadcasted_iota(jnp.int32, (128, 128), 0) >= lax.broadcasted_iota(jnp.int32, (128, 128), 1)
    return jnp.where(low, jnp.concatenate(outs, 0), 0.0)

def chol_inverse(ref, left, block, inverse):
    size = ref.shape[0]
    blocks = size // 128
    row = lax.broadcasted_iota(jnp.int32, (size, 128), 0)
    lane = lax.broadcasted_iota(jnp.int32, (128, size), 1)
    block[...] = ref[:128, :128]
    inverse[...] = jnp.zeros_like(inverse)

    def finish(here, off):
        inside = (lane >= off) & (lane < off + 128)
        return dot(inverse[...], jnp.where(inside, 0.0, ref[here, :]), ((1,), (0,)))

    def step(k, carry):
        off = pl.multiple_of(k * 128, 128)
        prev = pl.multiple_of(jnp.maximum(off - 128, 0), 128)
        here, before = pl.ds(off, 128), pl.ds(prev, 128)

        def hook(panel):
            if panel == 0:
                value = dot(ref[:, before], inverse[...], ((1,), (1,)))
                left[...] = jnp.where((row >= off) & (off > 0), value, 0.0)
            elif panel == 2:
                ref[before, :] = jnp.where(off > 0, finish(before, prev), ref[before, :])
                ref[before, before] = jnp.where(off > 0, inverse[...], ref[before, before])
            elif panel % 3 == 1 and panel // 3 - 1 in range(blocks):
                c = panel // 3 - 1
                lanes = slice(128 * c, 128 * c + 128)
                gone = (off > 0) & (prev == 128 * c)
                old = ref[:, lanes]
                upd = dot(left[...], ref[before, lanes], ((1,), (0,)))
                ref[:, lanes] = jnp.where(row >= off, jnp.where(gone, 0.0, old) - upd, old)

        value = factor_block(block[...], hook)
        after = pl.multiple_of(jnp.minimum(off + 128, size - 128), 128)
        after = pl.ds(after, 128)
        part = dot(ref[after, here], value, ((1,), (1,)))
        block[...] = ref[after, after] - dot(part, part, ((1,), (1,)))
        inverse[...] = value
        return carry

    lax.fori_loop(0, blocks, step, 0)
    last = slice(size - 128, size)
    ref[last, :] = finish(last, size - 128)
    ref[last, last] = inverse[...]
    rows = lax.broadcasted_iota(jnp.int32, (size, size), 0)
    lanes = lax.broadcasted_iota(jnp.int32, (size, size), 1)
    ref[...] = jnp.where(rows >= lanes, ref[...], 0.0)


def factor_scratch(size):
    return [pltpu.VMEM((size, 128), f32), pltpu.VMEM((128, 128), f32), pltpu.VMEM((128, 128), f32)]


class Mover:
    def __init__(self, sems):
        self.sems, self.used = sems, 0

    def plan(self, source, target, pieces=4):
        rows = source.shape[0] // pieces
        copies = []
        for k in range(pieces):
            here = pl.ds(k * rows, rows)
            copies.append(pltpu.make_async_copy(source.at[here], target.at[here], self.sems.at[self.used]))
            self.used += 1
        return copies

    def start(self, source, target, pieces=4):
        copies = self.plan(source, target, pieces)
        for copy in copies:
            copy.start()
        return copies


def arrive(copies):
    for copy in copies:
        copy.wait()


def factor_kernel(matrix, out, work, left, block, inverse, sems):
    mover = Mover(sems)
    arrive(mover.start(matrix, work))
    chol_inverse(work, left, block, inverse)
    arrive(mover.start(work, out))


def factor(matrix):
    size = matrix.shape[0]
    return pl.pallas_call(
        factor_kernel,
        out_shape=jax.ShapeDtypeStruct(matrix.shape, f32),
        in_specs=[far],
        out_specs=far,
        scratch_shapes=[pltpu.VMEM((size, size), f32)] + factor_scratch(size) + [pltpu.SemaphoreType.DMA((8,))],
        compiler_params=grant(57),
        cost_estimate=pl.CostEstimate(flops=120 * size**3, bytes_accessed=8 * size**2, transcendentals=0),
        name="factor",
    )(matrix)


def old_factor_kernel(ids, mine, other, out, work, left, block, inverse, sems):
    size, cols = work.shape[0], mine.shape[1]
    first = ids[1] == 0
    work[:, :cols] = jnp.where(first, mine[...], other[...])
    work[:, cols:] = jnp.where(first, other[...], mine[...])
    work[...] = work[...] + ridge(size)
    chol_inverse(work, left, block, inverse)
    arrive(Mover(sems).start(work, out))


def old_factor_inverse(ids, mine, other):
    size = mine.shape[0]
    return pl.pallas_call(
        old_factor_kernel,
        out_shape=jax.ShapeDtypeStruct((size, size), f32),
        in_specs=[scalar, whole, whole],
        out_specs=far,
        scratch_shapes=[pltpu.VMEM((size, size), f32)] + factor_scratch(size) + [pltpu.SemaphoreType.DMA((4,))],
        compiler_params=grant(55),
        cost_estimate=pl.CostEstimate(flops=120 * size**3, bytes_accessed=8 * size**2, transcendentals=0),
        name="old_factor",
    )(ids, mine, other)


def ridge(size):
    eye = lax.broadcasted_iota(jnp.int32, (size, size), 0) == lax.broadcasted_iota(jnp.int32, (size, size), 1)
    return jnp.where(eye, ridge_shift, 0.0)


def sum_kernel(came, out, half, work, sems):
    width = work.shape[2]
    work[...] = jnp.broadcast_to(jnp.sum(came[:, :, :width], axis=0)[None], work.shape)
    copies = Mover(sems).start(work, out)
    half[...] = came[:, :, width:].reshape(half.shape)
    arrive(copies)


def sum_spread(came, size):
    chips, each, width = came.shape
    square = (chips, each, size)
    return pl.pallas_call(
        sum_kernel,
        out_shape=(
            jax.ShapeDtypeStruct(square, f32),
            jax.ShapeDtypeStruct((chips * each, width - size), f32),
        ),
        in_specs=[whole],
        out_specs=(far, whole),
        scratch_shapes=[pltpu.VMEM(square, f32), pltpu.SemaphoreType.DMA((4,))],
        compiler_params=grant(24),
        name="sum_spread",
    )(came)


def pick_kernel(ids, pivots, points_in, mine_in, picked, near, points, mine, sems):
    mover = Mover(sems)
    copies = mover.start(points_in, points) + mover.start(mine_in, mine)
    size, count = pivots.shape[1], points.shape[0]
    dim = points.shape[1]
    first = ids[1] == 0
    places = ids[0] + lax.broadcasted_iota(jnp.int32, (size, count), 1)
    wanted_ids = jnp.concatenate([to_column(pivots[...].astype(f32))] * (count // 128), axis=1)
    picks = jnp.where(wanted_ids == places.astype(f32), 1.0, 0.0).astype(bf16)
    arrive(copies)
    wanted = jnp.concatenate([points[...], mine[...].astype(bf16)], axis=1)
    rows = lax.dot_general(picks, wanted, (((1,), (0,)), ((), ())), preferred_element_type=f32)
    picked[...] = rows.astype(bf16)

    half = count // 2
    wide = jnp.where(first, points[:half].astype(f32), points[half:].astype(f32))
    rest = to_row(-0.5 * jnp.sum(wide * wide, axis=1, keepdims=True))
    near[:half] = wide.astype(bf16)
    pieces = []
    for _ in range(3):
        piece = rest.astype(bf16).astype(f32)
        pieces += [piece[:, k : k + dim] for k in range(0, half, dim)]
        rest = rest - piece
    pieces.append(jnp.zeros((16 - len(pieces), dim), f32))
    near[half:] = jnp.concatenate(pieces, axis=0).astype(bf16)


def pick(ids, pivots, points, mine):
    size, count, dim = pivots.shape[1], *points.shape
    return pl.pallas_call(
        pick_kernel,
        out_shape=(
            jax.ShapeDtypeStruct((size, dim + mine.shape[1]), bf16),
            jax.ShapeDtypeStruct((count // 2 + 16, dim), bf16),
        ),
        in_specs=[scalar, whole, far, far],
        out_specs=(whole,) * 2,
        scratch_shapes=[
            pltpu.VMEM(points.shape, bf16),
            pltpu.VMEM(mine.shape, f32),
            pltpu.SemaphoreType.DMA((8,)),
        ],
        compiler_params=grant(56),
        name="pick",
    )(ids, pivots, points, mine)


def prepare_kernel(ids, mine, other, pieces, old_full):
    cols = mine.shape[1]
    first = ids[1] == 0
    old_full[:, :cols] = jnp.where(first, mine[...], other[...])
    old_full[:, cols:] = jnp.where(first, other[...], mine[...])
    high, low = pieces_of(dot(old_full[...], mine[...], ((0,), (0,))))
    pieces[:, :cols] = high
    pieces[:, cols:] = low


def prepare(ids, mine, other):
    count, cols = mine.shape
    return pl.pallas_call(
        prepare_kernel,
        out_shape=(
            jax.ShapeDtypeStruct((2 * cols, 2 * cols), bf16),
            jax.ShapeDtypeStruct((count, 2 * cols), f32),
        ),
        in_specs=[scalar] + [whole] * 2,
        out_specs=(whole, whole),
        compiler_params=grant(24),
        cost_estimate=pl.CostEstimate(flops=24 * count * cols**2, bytes_accessed=16 * count * cols, transcendentals=0),
        name="prepare",
    )(ids, mine, other)


def to_column(row):
    blocks = [
        jnp.transpose(jnp.broadcast_to(row[:, k : k + 128], (128, 128)))
        for k in range(0, row.shape[1], 128)
    ]
    return jnp.concatenate(blocks, axis=0)


def to_row(column):
    blocks = [
        jnp.transpose(jnp.broadcast_to(column[k : k + 128], (128, 128)))[:1]
        for k in range(0, column.shape[0], 128)
    ]
    return jnp.concatenate(blocks, axis=1)


def columns_kernel(
    ids, points, came, swapped, old_full, targets, columns, block_out, gram_out, block, gram, sems
):
    mover = Mover(sems)
    first = ids[1] == 0
    dim = points.shape[1]
    size = came.shape[0]
    cols = size // 2
    rate = -2.0 / dim
    pivot_points = came[:, :dim]
    wide = points[...].astype(f32)
    pivot_wide = pivot_points.astype(f32)
    squares = pivot_wide * pivot_wide
    norms = jnp.sum(wide * wide, axis=1, keepdims=True)
    pivot_column = jnp.sum(squares, axis=1, keepdims=True)
    pivot_row = dot(jnp.ones((8, dim), f32), squares, ((1,), (1,)))[:1]
    inner = narrow_dot(points[...], pivot_points)
    values = jnp.exp(rate * jnp.maximum(norms + pivot_row - 2.0 * inner, 0.0))
    mine, other = came[:, dim : dim + cols], swapped[...]
    pivot_old = jnp.concatenate(
        [jnp.where(first, mine, other), jnp.where(first, other, mine)], axis=1
    )
    high, low = pieces_of(old_full[...])
    values = values - (narrow_dot(high, pivot_old) + narrow_dot(low, pivot_old))
    columns[...] = values
    inner = narrow_dot(pivot_points, pivot_points)
    square = jnp.exp(rate * jnp.maximum(pivot_column + pivot_row - 2.0 * inner, 0.0))
    square = square - narrow_dot(pivot_old, pivot_old)
    block[...] = square + ridge(size)
    copies = mover.start(block, block_out)

    kept = jnp.sum(came[:, dim + cols :].astype(f32).reshape(size // 8, 8, size), axis=0)
    kept = kept[:, :cols] + kept[:, cols:]
    gram[:, size:] = jnp.broadcast_to(kept[None], (size // 8, 8, cols)).reshape(size, cols)

    row = jnp.broadcast_to(targets[...], (8, targets.shape[1]))
    old_proj = dot(row, old_full[...], ((1,), (0,)))
    new_proj = dot(row, columns[...], ((1,), (0,)))
    side = jnp.where(first, old_full[...], columns[...])
    for k in range(0, size, 128):
        here = slice(k, k + 128)
        gram[here, :size] = dot(side[:, here], columns[...], ((0,), (0,)))
        if k + 128 == size:
            for at, value in ((size - 4, old_proj), (size - 2, new_proj)):
                for place, lanes in ((at, slice(0, cols)), (at + 1, slice(cols, size))):
                    kept = gram[place : place + 1, :cols]
                    gram[place : place + 1, :cols] = jnp.where(first, kept, value[:1, lanes])
        copies += mover.start(gram.at[here], gram_out.at[here], 1)
    arrive(copies)


def pivot_columns(ids, points, came, swapped, old_full, targets):
    count, size = points.shape[0], came.shape[0]
    square = jax.ShapeDtypeStruct((size, size), f32)
    wide = jax.ShapeDtypeStruct((size, size + size // 2), f32)
    return pl.pallas_call(
        columns_kernel,
        out_shape=(jax.ShapeDtypeStruct((count, size), f32), square, wide),
        in_specs=[scalar] + [whole] * 5,
        out_specs=(whole, far, far),
        scratch_shapes=[
            pltpu.VMEM(square.shape, f32),
            pltpu.VMEM(wide.shape, f32),
            pltpu.SemaphoreType.DMA((8,)),
        ],
        compiler_params=grant(53),
        name="pivot_columns",
    )(ids, points, came, swapped, old_full, targets)


def across(matrix, row):
    return jnp.sum(matrix * row, axis=1, keepdims=True)


def down(matrix, column):
    return jnp.sum(matrix * column, axis=0, keepdims=True)


def solve(old_inverse, cross_low, schur_inverse, old_side, new_side):
    up = across(old_inverse[...], old_side)
    middle = across(schur_inverse[...], new_side - down(cross_low[...], up))
    new_coef = down(schur_inverse[...], middle)
    old_coef = down(old_inverse[...], up - across(cross_low[...], new_coef))
    return old_coef, new_coef


def fit(coefs, old_full, columns):
    return across(old_full[...], coefs[0]) + across(columns[...], coefs[1])


def core_kernel(
    ids, old_inverse_in, block_in, mine, other, old_full, columns, targets,
    cross_out, schur_out, old_proj, new_proj, direction, weights,
    old_inverse, block, cross_low, schur_inverse, left, part, inverse, sems,
):
    mover = Mover(sems)
    first_copy = mover.start(old_inverse_in, old_inverse)
    second_copy = mover.start(block_in, block)
    size = block.shape[0]
    mid = size // 2
    first = ids[1] == 0
    cross = jnp.where(first, mine[...], other[...])
    schur_inverse[...] = jnp.where(first, other[...], mine[...])
    for at, value in ((size - 4, old_proj), (size - 2, new_proj)):
        value[:, :mid] = schur_inverse[at : at + 1, :mid]
        value[:, mid:] = schur_inverse[at + 1 : at + 2, :mid]
    for start in range(0, mid, 128):
        turned = jnp.transpose(schur_inverse[start : start + 128, size - 128 :])
        schur_inverse[size - 4 :, start : start + 128] = turned[124:]
    arrive(first_copy)
    cross_low[...] = dot(old_inverse[...], cross, ((1,), (0,)))
    copies = mover.start(cross_low, cross_out)
    arrive(second_copy)
    schur_inverse[...] = (
        ridge_shift * block[...]
        + schur_inverse[...]
        - dot(cross_low[...], cross_low[...], ((0,), (0,)))
    )
    chol_inverse(schur_inverse, left, part, inverse)
    copies += mover.start(schur_inverse, schur_out)
    coefs = solve(old_inverse, cross_low, schur_inverse, old_proj[...], new_proj[...])
    value = (targets[...] - to_row(fit(coefs, old_full, columns))) * (1.0 / ridge_shift)
    direction[...] = value
    half = value.shape[1] // 2
    mine_half = jnp.where(first, value[:, :half], value[:, half:])
    weights[...] = jnp.broadcast_to(mine_half[None], weights.shape)
    arrive(copies)


def core_solve(ids, old_inverse, block, mine, other, old_full, columns, targets, parts):
    size, count = block.shape[0], columns.shape[0]
    square = jax.ShapeDtypeStruct((size, size), f32)
    return pl.pallas_call(
        core_kernel,
        out_shape=(
            square,
            square,
            jax.ShapeDtypeStruct((1, size), f32),
            jax.ShapeDtypeStruct((1, size), f32),
            jax.ShapeDtypeStruct((1, count), f32),
            jax.ShapeDtypeStruct((parts, 1, count // 2), f32),
        ),
        in_specs=[scalar, far, far] + [whole] * 5,
        out_specs=(far, far) + (whole,) * 4,
        scratch_shapes=[pltpu.VMEM((size, size), f32)] * 4
        + factor_scratch(size)
        + [pltpu.SemaphoreType.DMA((16,))],
        compiler_params=grant(54),
        name="core_solve",
    )(ids, old_inverse, block, mine, other, old_full, columns, targets)


def rows_kernel(
    scale, stride, half, ids, points, others, weights, old_full, columns, direction, targets,
    rows, sums, left, acc,
):
    count, dim = points.shape
    step = pl.program_id(0)

    @pl.when(step == 0)
    def _():
        acc[...] = jnp.zeros_like(acc)
        wide = points[...].astype(f32)
        rest = -0.5 * jnp.sum(wide * wide, axis=1, keepdims=True)
        lane = lax.broadcasted_iota(jnp.int32, (count, dim), 1)
        extra = jnp.zeros((count, dim), f32)
        for k in range(3):
            piece = rest.astype(bf16).astype(f32)
            extra = jnp.where(lane == k, piece, extra)
            rest = rest - piece
        left[:, :dim] = points[...]
        left[:, dim:] = extra.astype(bf16)

    lane = lax.broadcasted_iota(jnp.int32, (256, dim), 1)
    ones = jnp.where(lane < 3, 1.0, 0.0).astype(bf16)
    groups = half // 128
    chips = others.shape[0] // stride
    total = acc[...]
    for pair in range(chips // 2):
        tiles = []
        for chip in (2 * pair, 2 * pair + 1):
            base = chip * stride
            pieces = others[base + half : base + half + 16, :].astype(f32)
            shift = scale * (pieces[:groups] + pieces[groups : 2 * groups] + pieces[2 * groups : 3 * groups])
            weight = weights[2 * chip + ids[1]]
            for g in range(groups):
                tiles.append(
                    (
                        others[base + 128 * g : base + 128 * g + 128, :],
                        shift[g : g + 1],
                        weight[:, 128 * g : 128 * g + 128],
                    )
                )
        for k in range(0, len(tiles), 2):
            one, two = tiles[k], tiles[k + 1]
            right = jnp.concatenate([jnp.concatenate([one[0], two[0]], axis=0), ones], axis=1)
            inner = narrow_dot(left[...], right) * scale
            one_value = jnp.exp2(jnp.minimum(inner[:, :128] + one[1], 0.0)) * one[2]
            two_value = jnp.exp2(jnp.minimum(inner[:, 128:] + two[1], 0.0)) * two[2]
            total = total + (one_value + two_value)
    acc[...] = total

    @pl.when(step == pl.num_programs(0) - 1)
    def _():
        mine = jnp.sum(acc[...], axis=1, keepdims=True)
        rows[...] = to_row(mine)
        image = mine + (0.5 * ridge_shift) * to_column(direction[...])[:, :1]
        size = old_full.shape[1]
        flat = (sums.shape[0], 1)
        sums[:, :, :size] = jnp.broadcast_to(down(old_full[...], image)[None], flat + (size,))
        sums[:, :, size : 2 * size] = jnp.broadcast_to(down(columns[...], image)[None], flat + (size,))
        along_image = jnp.sum(to_row(image) * direction[...], axis=1, keepdims=True)
        along_targets = 0.5 * jnp.sum(targets[...] * direction[...], axis=1, keepdims=True)
        place = lax.broadcasted_iota(jnp.int32, (1, 128), 1)
        last = jnp.where(place == 0, along_image, jnp.where(place == 1, along_targets, 0.0))
        sums[:, :, 2 * size :] = jnp.broadcast_to(last[None], flat + (128,))


def kernel_rows(ids, points, others, stride, weights, old_full, columns, direction, targets):
    count, dim = points.shape
    parts = weights.shape[0]
    chips = parts // 2
    scale = 2.0 * (2.0 / dim) * math.log2(math.e)
    steps = 8
    size = others.shape[0] // steps
    width = old_full.shape[1] + columns.shape[1] + 128

    def fixed(array):
        return pl.BlockSpec(array.shape, lambda i: (0,) * array.ndim)

    return pl.pallas_call(
        lambda *refs: rows_kernel(scale, stride, weights.shape[2], *refs),
        grid=(steps,),
        in_specs=[
            scalar,
            fixed(points),
            pl.BlockSpec((size, dim), lambda i: (i, 0)),
            pl.BlockSpec((parts // steps, 1, weights.shape[2]), lambda i: (i, 0, 0)),
            whole,
            whole,
            fixed(direction),
            fixed(targets),
        ],
        out_specs=(
            pl.BlockSpec((1, count), lambda i: (0, 0)),
            pl.BlockSpec((parts, 1, width), lambda i: (0, 0, 0)),
        ),
        out_shape=(
            jax.ShapeDtypeStruct((1, count), f32),
            jax.ShapeDtypeStruct((parts, 1, width), f32),
        ),
        scratch_shapes=[pltpu.VMEM((count, 2 * dim), bf16), pltpu.VMEM((count, 128), f32)],
        compiler_params=grant(55),
        name="kernel_rows",
    )(ids, points, others, weights, old_full, columns, direction, targets)


def gain_kernel(
    old_inverse_in, cross_in, schur_in, old_full, columns, gain, old_inverse, cross_low, schur_inverse, sems
):
    mover = Mover(sems)
    copies = [
        mover.start(old_inverse_in, old_inverse),
        mover.start(cross_in, cross_low),
        mover.start(schur_in, schur_inverse),
    ]
    size = cross_low.shape[0]
    arrive(copies[0])
    up = three_dot(old_full[...], old_inverse[...], ((1,), (1,)))
    arrive(copies[1])
    rest = columns[...] - three_dot(up, cross_low[...], ((1,), (0,)))
    arrive(copies[2])
    middle = three_dot(rest, schur_inverse[...], ((1,), (1,)))
    gain[:, size:] = three_dot(middle, schur_inverse[...], ((1,), (0,)))
    rest = up - three_dot(gain[:, size:], cross_low[...], ((1,), (1,)))
    gain[:, :size] = three_dot(rest, old_inverse[...], ((1,), (0,)))


def gain_of(old_inverse, cross_low, schur_inverse, old_full, columns):
    size, count = cross_low.shape[0], columns.shape[0]
    return pl.pallas_call(
        gain_kernel,
        out_shape=jax.ShapeDtypeStruct((count, 2 * size), f32),
        in_specs=[far] * 3 + [whole] * 2,
        out_specs=whole,
        scratch_shapes=[pltpu.VMEM((size, size), f32)] * 3 + [pltpu.SemaphoreType.DMA((12,))],
        compiler_params=grant(52),
        cost_estimate=pl.CostEstimate(flops=72 * count * size**2, bytes_accessed=12 * size**2, transcendentals=0),
        name="gain",
    )(old_inverse, cross_low, schur_inverse, old_full, columns)


def tail_kernel(
    sums, mine, other, old_proj, new_proj, gain, direction, targets, answer, residual, preconditioned
):
    size = old_proj.shape[1]
    total = jnp.sum(sums[...], axis=0)
    alpha = total[:, 2 * size + 1 : 2 * size + 2] / total[:, 2 * size : 2 * size + 1]
    step = alpha * direction[...]
    answer[...] = step[0]
    left = targets[...] - alpha * (mine[...] + other[...]) - ridge_shift * step
    residual[...] = left[0]
    proj = jnp.concatenate([old_proj[...], new_proj[...]], axis=1) - alpha * total[:, : 2 * size]
    fitted = to_row(across(gain[...], proj))
    preconditioned[...] = ((left - fitted) * (1.0 / ridge_shift))[0]


def tail(*args):
    row = jax.ShapeDtypeStruct(args[1].shape[1:], f32)
    return pl.pallas_call(
        tail_kernel,
        out_shape=(row,) * 3,
        in_specs=[whole] * len(args),
        out_specs=(whole,) * 3,
        compiler_params=grant(52),
        name="tail",
    )(*args)


def exchange(pieces, axes):
    return lax.all_to_all(pieces, axes, 0, 0, tiled=True)


def swap(value):
    return lax.ppermute(value, "sub", [(0, 1), (1, 0)])


def local(points, old_factor, targets, pivots):
    count, dim = points.shape
    size = pivots.shape[0]
    part = lax.axis_index("sub")
    chips = lax.axis_size("rows")
    parts = 2 * chips
    each = size // chips
    cols = old_factor.shape[1]
    first = lax.axis_index("rows") * count
    ids = jnp.stack([first, part]).astype(jnp.int32)
    row = targets.reshape(1, count)

    picked, near = pick(ids, pivots.reshape(1, size), points, old_factor)
    picked, old_factor = lax.optimization_barrier((picked, old_factor))
    width = picked.shape[1]
    came = exchange(picked.reshape(chips, each, width), "rows")
    pieces, old_full = prepare(ids, old_factor, swap(old_factor))
    kept = jnp.sum(came.astype(f32), axis=0).astype(bf16)
    sent = [jnp.broadcast_to(kept[None], (chips, each, width)), pieces.reshape(chips, each, size)]
    came = exchange(jnp.concatenate(sent, axis=2), "rows").reshape(size, width + size)
    swapped = swap(came[:, dim:width])

    columns, block, gram = pivot_columns(ids, points, came, swapped, old_full, row)
    came = exchange(gram.reshape(chips, each, size + cols), "rows")
    block_inverse = factor(block)
    came, block_inverse, near = lax.optimization_barrier((came, block_inverse, near))
    others = lax.all_gather(near, "rows", axis=0, tiled=True)
    spread_gram, mine = sum_spread(came, size)
    other = swap(mine)
    mine_gram = exchange(spread_gram, "rows").reshape(size, size)
    old_inverse = old_factor_inverse(ids, mine, other)
    mine_gram, old_inverse = lax.optimization_barrier((mine_gram, old_inverse))
    other_gram = swap(mine_gram)

    cross_low, schur_inverse, old_proj, new_proj, direction, weights = core_solve(
        ids, old_inverse, block, mine_gram, other_gram, old_full, columns, row, parts
    )
    weights = exchange(weights, everyone)
    chosen = lax.dynamic_slice_in_dim(block_inverse, part * cols, cols, 0)
    new_part = dot(columns, chosen, ((1,), (1,)))
    rows, sums = kernel_rows(
        ids, points, others, near.shape[0], weights, old_full, columns, direction, row
    )
    rows, cross_low = lax.optimization_barrier((rows, cross_low))
    sums = exchange(sums, everyone)
    gain = gain_of(old_inverse, cross_low, schur_inverse, old_full, columns)
    answer, residual, preconditioned = tail(
        sums, rows, swap(rows), old_proj, new_proj, gain, direction, row
    )
    return new_part, answer, residual, preconditioned


def solution(mesh):
    in_specs = (P("rows", None), P("rows", "sub"), P("rows"), P())
    out_specs = (P("rows", "sub"), P("rows"), P("rows"), P("rows"))
    return jax.shard_map(local, mesh=mesh, in_specs=in_specs, out_specs=out_specs, check_vma=False)
```

```python
import math

import jax
import jax.numpy as jnp
from jax import lax
from jax.experimental import pallas as pl
from jax.experimental.pallas import tpu as pltpu
from jax.sharding import PartitionSpec as P

ridge_shift = 0.5
precise = lax.Precision.HIGHEST
everyone = ("rows", "sub")
f32, bf16 = jnp.float32, jnp.bfloat16
whole = pl.BlockSpec(memory_space=pltpu.VMEM)
far = pl.BlockSpec(memory_space=pltpu.HBM)
scalar = pl.BlockSpec(memory_space=pltpu.SMEM)


def grant(megabytes):
    return pltpu.CompilerParams(vmem_limit_bytes=megabytes << 20)


def dot(left, right, contract):
    return lax.dot_general(left, right, (contract, ((), ())), precision=precise, preferred_element_type=f32)


def pieces_of(value):
    high = value.astype(bf16)
    return high, (value - high.astype(f32)).astype(bf16)


def three_dot(left, right, contract):
    left_high, left_low = pieces_of(left)
    right_high, right_low = pieces_of(right)

    def one(a, b):
        return lax.dot_general(a, b, (contract, ((), ())), preferred_element_type=f32)

    return one(left_high, right_high) + (one(left_high, right_low) + one(left_low, right_high))


def narrow_dot(left, right):
    return lax.dot_general(left, right, (((1,), (1,)), ((), ())), preferred_element_type=f32)


def total(terms):
    while len(terms) > 1:
        terms = [terms[i] + terms[i + 1] if i + 1 < len(terms) else terms[i] for i in range(0, len(terms), 2)]
    return terms[0]

def factor_block(a, hook):
    lane = lax.broadcasted_iota(jnp.int32, (8, 128), 1)
    sub = lax.broadcasted_iota(jnp.int32, (8, 128), 0)
    full = lambda v: jnp.broadcast_to(v, (8, 128))
    rows = [a[8 * i:8 * i + 8] for i in range(16)]
    outs, pending = [], []
    def drain(n):
        for _ in range(min(n, len(pending))):
            pending.pop(0)()
    for panel in range(16):
        lo = 8 * panel
        inside = (lane >= lo) & (lane < lo + 8)
        head = rows[panel]
        cols = [full(head[:, lo + j:lo + j + 1]) for j in range(8)]
        e = {(i, j): full(cols[j][i:i + 1]) for j in range(8) for i in range(j, 8)}
        head = jnp.where(inside, (lane == lo + sub).astype(f32), head)
        base = [full(head[j:j + 1]) for j in range(8)]
        per = -(-len(pending) // 5)
        m, pieces = {}, {}
        for j in (0, 2, 4, 6):
            p, q, s = e[j, j], e[j + 1, j], e[j + 1, j + 1]
            rdet = 1.0 / (p * s - q * q)
            pieces[j] = (p, q, s, rdet)
            g = {}
            for i in range(j + 2, 8):
                x, y = e[i, j], e[i, j + 1]
                g[i] = (x * s - y * q, y * p - x * q)
            for i in range(j + 2, 8):
                for k in range(j + 2, i + 1):
                    e[i, k] = e[i, k] - (g[i][0] * e[k, j] + g[i][1] * e[k, j + 1]) * rdet
            for i in range(j + 2, 8):
                f0, f1 = g[i][0] * rdet, g[i][1] * rdet
                for k in range(j):
                    m[i, k] = m[i, k] - (f0 * m[j, k] + f1 * m[j + 1, k])
                m[i, j], m[i, j + 1] = -f0, -f1
            drain(per)
            if j == 2:
                hook(panel)
        h = [total([base[i]] + [m[i, k] * base[k] for k in range(i - i % 2)]) for i in range(8)]
        y = []
        for j in (0, 2, 4, 6):
            p, q, s, rdet = pieces[j]
            y.append((s * h[j] - q * h[j + 1]) * rdet)
            y.append((p * h[j + 1] - q * h[j]) * rdet)
        G = [total([y[l]] + [m[i, l] * y[i] for i in range(l - l % 2 + 2, 8)]) for l in range(8)]
        drain(len(pending))
        if panel < 15:
            r = rows[panel + 1]
            c = total([full(r[:, lo + j:lo + j + 1]) * G[j] for j in range(8)])
            rows[panel + 1] = jnp.where(inside, 0.0, r) - c
        if panel < 14:
            g = G[7]
            for l in range(7):
                g = jnp.where(sub == l, G[l], g)
            parts = ([jnp.zeros((lo, 128), f32)] if panel else []) + [g, jnp.zeros((120 - lo, 128), f32)]
            upd = dot(jnp.concatenate(rows[panel + 2:], 0), jnp.concatenate(parts, 0), ((1,), (0,)))

            def use(i, upd=upd, first=panel + 2, inside=inside):
                rows[i] = jnp.where(inside, 0.0, rows[i]) - upd[8 * (i - first):8 * (i - first) + 8]

            for i in range(panel + 2, 16):
                pending.append(lambda i=i, u=use: u(i))
        out = jnp.zeros((8, 128), f32)
        for j in (0, 2, 4, 6):
            p, q, s, rdet = pieces[j]
            rp = 1.0 / p
            out = jnp.where(sub == j, h[j] * lax.rsqrt(p), out)
            out = jnp.where(sub == j + 1, (h[j + 1] - (q * rp) * h[j]) * lax.rsqrt(s - q * (q * rp)), out)
        outs.append(out)
    low = lax.broadcasted_iota(jnp.int32, (128, 128), 0) >= lax.broadcasted_iota(jnp.int32, (128, 128), 1)
    return jnp.where(low, jnp.concatenate(outs, 0), 0.0)

def chol_inverse(ref, left, block, inverse):
    size = ref.shape[0]
    blocks = size // 128
    row = lax.broadcasted_iota(jnp.int32, (size, 128), 0)
    lane = lax.broadcasted_iota(jnp.int32, (128, size), 1)
    block[...] = ref[:128, :128]
    inverse[...] = jnp.zeros_like(inverse)

    def finish(here, off):
        inside = (lane >= off) & (lane < off + 128)
        return dot(inverse[...], jnp.where(inside, 0.0, ref[here, :]), ((1,), (0,)))

    def step(k, carry):
        off = pl.multiple_of(k * 128, 128)
        prev = pl.multiple_of(jnp.maximum(off - 128, 0), 128)
        here, before = pl.ds(off, 128), pl.ds(prev, 128)

        def hook(panel):
            if panel == 0:
                value = dot(ref[:, before], inverse[...], ((1,), (1,)))
                left[...] = jnp.where((row >= off) & (off > 0), value, 0.0)
            elif panel == 2:
                ref[before, :] = jnp.where(off > 0, finish(before, prev), ref[before, :])
                ref[before, before] = jnp.where(off > 0, inverse[...], ref[before, before])
            elif panel % 3 == 1 and panel // 3 - 1 in range(blocks):
                c = panel // 3 - 1
                lanes = slice(128 * c, 128 * c + 128)
                gone = (off > 0) & (prev == 128 * c)
                old = ref[:, lanes]
                upd = dot(left[...], ref[before, lanes], ((1,), (0,)))
                ref[:, lanes] = jnp.where(row >= off, jnp.where(gone, 0.0, old) - upd, old)

        value = factor_block(block[...], hook)
        after = pl.multiple_of(jnp.minimum(off + 128, size - 128), 128)
        after = pl.ds(after, 128)
        part = dot(ref[after, here], value, ((1,), (1,)))
        block[...] = ref[after, after] - dot(part, part, ((1,), (1,)))
        inverse[...] = value
        return carry

    lax.fori_loop(0, blocks, step, 0)
    last = slice(size - 128, size)
    ref[last, :] = finish(last, size - 128)
    ref[last, last] = inverse[...]
    rows = lax.broadcasted_iota(jnp.int32, (size, size), 0)
    lanes = lax.broadcasted_iota(jnp.int32, (size, size), 1)
    ref[...] = jnp.where(rows >= lanes, ref[...], 0.0)


def factor_scratch(size):
    return [pltpu.VMEM((size, 128), f32), pltpu.VMEM((128, 128), f32), pltpu.VMEM((128, 128), f32)]


class Mover:
    def __init__(self, sems):
        self.sems, self.used = sems, 0

    def plan(self, source, target, pieces=4):
        rows = source.shape[0] // pieces
        copies = []
        for k in range(pieces):
            here = pl.ds(k * rows, rows)
            copies.append(pltpu.make_async_copy(source.at[here], target.at[here], self.sems.at[self.used]))
            self.used += 1
        return copies

    def start(self, source, target, pieces=4):
        copies = self.plan(source, target, pieces)
        for copy in copies:
            copy.start()
        return copies


def arrive(copies):
    for copy in copies:
        copy.wait()


def factor_kernel(matrix, out, work, left, block, inverse, sems):
    mover = Mover(sems)
    arrive(mover.start(matrix, work))
    chol_inverse(work, left, block, inverse)
    arrive(mover.start(work, out))


def factor(matrix):
    size = matrix.shape[0]
    return pl.pallas_call(
        factor_kernel,
        out_shape=jax.ShapeDtypeStruct(matrix.shape, f32),
        in_specs=[far],
        out_specs=far,
        scratch_shapes=[pltpu.VMEM((size, size), f32)] + factor_scratch(size) + [pltpu.SemaphoreType.DMA((8,))],
        compiler_params=grant(57),
        cost_estimate=pl.CostEstimate(flops=120 * size**3, bytes_accessed=8 * size**2, transcendentals=0),
        name="factor",
    )(matrix)


def old_factor_kernel(ids, mine, other, out, work, left, block, inverse, sems):
    size, cols = work.shape[0], mine.shape[1]
    first = ids[1] == 0
    work[:, :cols] = jnp.where(first, mine[...], other[...])
    work[:, cols:] = jnp.where(first, other[...], mine[...])
    work[...] = work[...] + ridge(size)
    chol_inverse(work, left, block, inverse)
    arrive(Mover(sems).start(work, out))


def old_factor_inverse(ids, mine, other):
    size = mine.shape[0]
    return pl.pallas_call(
        old_factor_kernel,
        out_shape=jax.ShapeDtypeStruct((size, size), f32),
        in_specs=[scalar, whole, whole],
        out_specs=far,
        scratch_shapes=[pltpu.VMEM((size, size), f32)] + factor_scratch(size) + [pltpu.SemaphoreType.DMA((4,))],
        compiler_params=grant(55),
        cost_estimate=pl.CostEstimate(flops=120 * size**3, bytes_accessed=8 * size**2, transcendentals=0),
        name="old_factor",
    )(ids, mine, other)


def ridge(size):
    eye = lax.broadcasted_iota(jnp.int32, (size, size), 0) == lax.broadcasted_iota(jnp.int32, (size, size), 1)
    return jnp.where(eye, ridge_shift, 0.0)


def sum_kernel(came, out, half, work, sems):
    width = work.shape[2]
    work[...] = jnp.broadcast_to(jnp.sum(came[:, :, :width], axis=0)[None], work.shape)
    copies = Mover(sems).start(work, out)
    half[...] = came[:, :, width:].reshape(half.shape)
    arrive(copies)


def sum_spread(came, size):
    chips, each, width = came.shape
    square = (chips, each, size)
    return pl.pallas_call(
        sum_kernel,
        out_shape=(
            jax.ShapeDtypeStruct(square, f32),
            jax.ShapeDtypeStruct((chips * each, width - size), f32),
        ),
        in_specs=[whole],
        out_specs=(far, whole),
        scratch_shapes=[pltpu.VMEM(square, f32), pltpu.SemaphoreType.DMA((4,))],
        compiler_params=grant(24),
        name="sum_spread",
    )(came)


def pick_kernel(ids, pivots, points_in, mine_in, picked, near, points, mine, sems):
    mover = Mover(sems)
    copies = mover.start(points_in, points) + mover.start(mine_in, mine)
    size, count = pivots.shape[1], points.shape[0]
    dim = points.shape[1]
    first = ids[1] == 0
    places = ids[0] + lax.broadcasted_iota(jnp.int32, (size, count), 1)
    wanted_ids = jnp.concatenate([to_column(pivots[...].astype(f32))] * (count // 128), axis=1)
    picks = jnp.where(wanted_ids == places.astype(f32), 1.0, 0.0).astype(bf16)
    arrive(copies)
    wanted = jnp.concatenate([points[...], mine[...].astype(bf16)], axis=1)
    rows = lax.dot_general(picks, wanted, (((1,), (0,)), ((), ())), preferred_element_type=f32)
    picked[...] = rows.astype(bf16)

    half = count // 2
    wide = jnp.where(first, points[:half].astype(f32), points[half:].astype(f32))
    rest = to_row(-0.5 * jnp.sum(wide * wide, axis=1, keepdims=True))
    near[:half] = wide.astype(bf16)
    pieces = []
    for _ in range(3):
        piece = rest.astype(bf16).astype(f32)
        pieces += [piece[:, k : k + dim] for k in range(0, half, dim)]
        rest = rest - piece
    pieces.append(jnp.zeros((16 - len(pieces), dim), f32))
    near[half:] = jnp.concatenate(pieces, axis=0).astype(bf16)


def pick(ids, pivots, points, mine):
    size, count, dim = pivots.shape[1], *points.shape
    return pl.pallas_call(
        pick_kernel,
        out_shape=(
            jax.ShapeDtypeStruct((size, dim + mine.shape[1]), bf16),
            jax.ShapeDtypeStruct((count // 2 + 16, dim), bf16),
        ),
        in_specs=[scalar, whole, far, far],
        out_specs=(whole,) * 2,
        scratch_shapes=[
            pltpu.VMEM(points.shape, bf16),
            pltpu.VMEM(mine.shape, f32),
            pltpu.SemaphoreType.DMA((8,)),
        ],
        compiler_params=grant(56),
        name="pick",
    )(ids, pivots, points, mine)


def prepare_kernel(ids, mine, other, pieces, old_full):
    cols = mine.shape[1]
    first = ids[1] == 0
    old_full[:, :cols] = jnp.where(first, mine[...], other[...])
    old_full[:, cols:] = jnp.where(first, other[...], mine[...])
    high, low = pieces_of(dot(old_full[...], mine[...], ((0,), (0,))))
    pieces[:, :cols] = high
    pieces[:, cols:] = low


def prepare(ids, mine, other):
    count, cols = mine.shape
    return pl.pallas_call(
        prepare_kernel,
        out_shape=(
            jax.ShapeDtypeStruct((2 * cols, 2 * cols), bf16),
            jax.ShapeDtypeStruct((count, 2 * cols), f32),
        ),
        in_specs=[scalar] + [whole] * 2,
        out_specs=(whole, whole),
        compiler_params=grant(24),
        cost_estimate=pl.CostEstimate(flops=300 * count * cols**2, bytes_accessed=16 * count * cols, transcendentals=0),
        name="prepare",
    )(ids, mine, other)


def to_column(row):
    blocks = [
        jnp.transpose(jnp.broadcast_to(row[:, k : k + 128], (128, 128)))
        for k in range(0, row.shape[1], 128)
    ]
    return jnp.concatenate(blocks, axis=0)


def to_row(column):
    blocks = [
        jnp.transpose(jnp.broadcast_to(column[k : k + 128], (128, 128)))[:1]
        for k in range(0, column.shape[0], 128)
    ]
    return jnp.concatenate(blocks, axis=1)


def columns_kernel(
    ids, points, came, swapped, old_full, targets, columns, block_out, gram_out, block, gram, sems
):
    mover = Mover(sems)
    first = ids[1] == 0
    dim = points.shape[1]
    size = came.shape[0]
    cols = size // 2
    rate = -2.0 / dim
    pivot_points = came[:, :dim]
    wide = points[...].astype(f32)
    pivot_wide = pivot_points.astype(f32)
    squares = pivot_wide * pivot_wide
    norms = jnp.sum(wide * wide, axis=1, keepdims=True)
    pivot_column = jnp.sum(squares, axis=1, keepdims=True)
    pivot_row = dot(jnp.ones((8, dim), f32), squares, ((1,), (1,)))[:1]
    inner = narrow_dot(points[...], pivot_points)
    values = jnp.exp(rate * jnp.maximum(norms + pivot_row - 2.0 * inner, 0.0))
    mine, other = came[:, dim : dim + cols], swapped[...]
    pivot_old = jnp.concatenate(
        [jnp.where(first, mine, other), jnp.where(first, other, mine)], axis=1
    )
    high, low = pieces_of(old_full[...])
    values = values - (narrow_dot(high, pivot_old) + narrow_dot(low, pivot_old))
    columns[...] = values
    inner = narrow_dot(pivot_points, pivot_points)
    square = jnp.exp(rate * jnp.maximum(pivot_column + pivot_row - 2.0 * inner, 0.0))
    square = square - narrow_dot(pivot_old, pivot_old)
    block[...] = square + ridge(size)
    copies = mover.start(block, block_out)

    kept = jnp.sum(came[:, dim + cols :].astype(f32).reshape(size // 8, 8, size), axis=0)
    kept = kept[:, :cols] + kept[:, cols:]
    gram[:, size:] = jnp.broadcast_to(kept[None], (size // 8, 8, cols)).reshape(size, cols)

    row = jnp.broadcast_to(targets[...], (8, targets.shape[1]))
    old_proj = dot(row, old_full[...], ((1,), (0,)))
    new_proj = dot(row, columns[...], ((1,), (0,)))
    side = jnp.where(first, old_full[...], columns[...])
    for k in range(0, size, 128):
        here = slice(k, k + 128)
        gram[here, :size] = dot(side[:, here], columns[...], ((0,), (0,)))
        if k + 128 == size:
            for at, value in ((size - 4, old_proj), (size - 2, new_proj)):
                for place, lanes in ((at, slice(0, cols)), (at + 1, slice(cols, size))):
                    kept = gram[place : place + 1, :cols]
                    gram[place : place + 1, :cols] = jnp.where(first, kept, value[:1, lanes])
        copies += mover.start(gram.at[here], gram_out.at[here], 1)
    arrive(copies)


def pivot_columns(ids, points, came, swapped, old_full, targets):
    count, size = points.shape[0], came.shape[0]
    square = jax.ShapeDtypeStruct((size, size), f32)
    wide = jax.ShapeDtypeStruct((size, size + size // 2), f32)
    return pl.pallas_call(
        columns_kernel,
        out_shape=(jax.ShapeDtypeStruct((count, size), f32), square, wide),
        in_specs=[scalar] + [whole] * 5,
        out_specs=(whole, far, far),
        scratch_shapes=[
            pltpu.VMEM(square.shape, f32),
            pltpu.VMEM(wide.shape, f32),
            pltpu.SemaphoreType.DMA((8,)),
        ],
        compiler_params=grant(53),
        name="pivot_columns",
    )(ids, points, came, swapped, old_full, targets)


def across(matrix, row):
    return jnp.sum(matrix * row, axis=1, keepdims=True)


def down(matrix, column):
    return jnp.sum(matrix * column, axis=0, keepdims=True)


def solve(old_inverse, cross_low, schur_inverse, old_side, new_side):
    up = across(old_inverse[...], old_side)
    middle = across(schur_inverse[...], new_side - down(cross_low[...], up))
    new_coef = down(schur_inverse[...], middle)
    old_coef = down(old_inverse[...], up - across(cross_low[...], new_coef))
    return old_coef, new_coef


def fit(coefs, old_full, columns):
    return across(old_full[...], coefs[0]) + across(columns[...], coefs[1])


def core_kernel(
    ids, old_inverse_in, block_in, mine, other, old_full, columns, targets,
    cross_out, schur_out, old_proj, new_proj, direction, weights,
    old_inverse, block, cross_low, schur_inverse, left, part, inverse, sems,
):
    mover = Mover(sems)
    first_copy = mover.start(old_inverse_in, old_inverse)
    second_copy = mover.start(block_in, block)
    size = block.shape[0]
    mid = size // 2
    first = ids[1] == 0
    cross = jnp.where(first, mine[...], other[...])
    schur_inverse[...] = jnp.where(first, other[...], mine[...])
    for at, value in ((size - 4, old_proj), (size - 2, new_proj)):
        value[:, :mid] = schur_inverse[at : at + 1, :mid]
        value[:, mid:] = schur_inverse[at + 1 : at + 2, :mid]
    for start in range(0, mid, 128):
        turned = jnp.transpose(schur_inverse[start : start + 128, size - 128 :])
        schur_inverse[size - 4 :, start : start + 128] = turned[124:]
    arrive(first_copy)
    cross_low[...] = dot(old_inverse[...], cross, ((1,), (0,)))
    copies = mover.start(cross_low, cross_out)
    arrive(second_copy)
    schur_inverse[...] = (
        ridge_shift * block[...]
        + schur_inverse[...]
        - dot(cross_low[...], cross_low[...], ((0,), (0,)))
    )
    chol_inverse(schur_inverse, left, part, inverse)
    copies += mover.start(schur_inverse, schur_out)
    coefs = solve(old_inverse, cross_low, schur_inverse, old_proj[...], new_proj[...])
    value = (targets[...] - to_row(fit(coefs, old_full, columns))) * (1.0 / ridge_shift)
    direction[...] = value
    half = value.shape[1] // 2
    mine_half = jnp.where(first, value[:, :half], value[:, half:])
    weights[...] = jnp.broadcast_to(mine_half[None], weights.shape)
    arrive(copies)


def core_solve(ids, old_inverse, block, mine, other, old_full, columns, targets, parts):
    size, count = block.shape[0], columns.shape[0]
    square = jax.ShapeDtypeStruct((size, size), f32)
    return pl.pallas_call(
        core_kernel,
        out_shape=(
            square,
            square,
            jax.ShapeDtypeStruct((1, size), f32),
            jax.ShapeDtypeStruct((1, size), f32),
            jax.ShapeDtypeStruct((1, count), f32),
            jax.ShapeDtypeStruct((parts, 1, count // 2), f32),
        ),
        in_specs=[scalar, far, far] + [whole] * 5,
        out_specs=(far, far) + (whole,) * 4,
        scratch_shapes=[pltpu.VMEM((size, size), f32)] * 4
        + factor_scratch(size)
        + [pltpu.SemaphoreType.DMA((16,))],
        compiler_params=grant(54),
        name="core_solve",
    )(ids, old_inverse, block, mine, other, old_full, columns, targets)


def rows_kernel(
    scale, stride, half, ids, points, others, weights, old_full, columns, direction, targets,
    rows, sums, left, acc,
):
    count, dim = points.shape
    step = pl.program_id(0)

    @pl.when(step == 0)
    def _():
        acc[...] = jnp.zeros_like(acc)
        wide = points[...].astype(f32)
        rest = -0.5 * jnp.sum(wide * wide, axis=1, keepdims=True)
        lane = lax.broadcasted_iota(jnp.int32, (count, dim), 1)
        extra = jnp.zeros((count, dim), f32)
        for k in range(3):
            piece = rest.astype(bf16).astype(f32)
            extra = jnp.where(lane == k, piece, extra)
            rest = rest - piece
        left[:, :dim] = points[...]
        left[:, dim:] = extra.astype(bf16)

    lane = lax.broadcasted_iota(jnp.int32, (256, dim), 1)
    ones = jnp.where(lane < 3, 1.0, 0.0).astype(bf16)
    groups = half // 128
    chips = others.shape[0] // stride
    total = acc[...]
    for pair in range(chips // 2):
        tiles = []
        for chip in (2 * pair, 2 * pair + 1):
            base = chip * stride
            pieces = others[base + half : base + half + 16, :].astype(f32)
            shift = scale * (pieces[:groups] + pieces[groups : 2 * groups] + pieces[2 * groups : 3 * groups])
            weight = weights[2 * chip + ids[1]]
            for g in range(groups):
                tiles.append(
                    (
                        others[base + 128 * g : base + 128 * g + 128, :],
                        shift[g : g + 1],
                        weight[:, 128 * g : 128 * g + 128],
                    )
                )
        for k in range(0, len(tiles), 2):
            one, two = tiles[k], tiles[k + 1]
            right = jnp.concatenate([jnp.concatenate([one[0], two[0]], axis=0), ones], axis=1)
            inner = narrow_dot(left[...], right) * scale
            one_value = jnp.exp2(jnp.minimum(inner[:, :128] + one[1], 0.0)) * one[2]
            two_value = jnp.exp2(jnp.minimum(inner[:, 128:] + two[1], 0.0)) * two[2]
            total = total + (one_value + two_value)
    acc[...] = total

    @pl.when(step == pl.num_programs(0) - 1)
    def _():
        mine = jnp.sum(acc[...], axis=1, keepdims=True)
        rows[...] = to_row(mine)
        image = mine + (0.5 * ridge_shift) * to_column(direction[...])[:, :1]
        size = old_full.shape[1]
        flat = (sums.shape[0], 1)
        sums[:, :, :size] = jnp.broadcast_to(down(old_full[...], image)[None], flat + (size,))
        sums[:, :, size : 2 * size] = jnp.broadcast_to(down(columns[...], image)[None], flat + (size,))
        along_image = jnp.sum(to_row(image) * direction[...], axis=1, keepdims=True)
        along_targets = 0.5 * jnp.sum(targets[...] * direction[...], axis=1, keepdims=True)
        place = lax.broadcasted_iota(jnp.int32, (1, 128), 1)
        last = jnp.where(place == 0, along_image, jnp.where(place == 1, along_targets, 0.0))
        sums[:, :, 2 * size :] = jnp.broadcast_to(last[None], flat + (128,))


def kernel_rows(ids, points, others, stride, weights, old_full, columns, direction, targets):
    count, dim = points.shape
    parts = weights.shape[0]
    chips = parts // 2
    scale = 2.0 * (2.0 / dim) * math.log2(math.e)
    steps = 8
    size = others.shape[0] // steps
    width = old_full.shape[1] + columns.shape[1] + 128

    def fixed(array):
        return pl.BlockSpec(array.shape, lambda i: (0,) * array.ndim)

    return pl.pallas_call(
        lambda *refs: rows_kernel(scale, stride, weights.shape[2], *refs),
        grid=(steps,),
        in_specs=[
            scalar,
            fixed(points),
            pl.BlockSpec((size, dim), lambda i: (i, 0)),
            pl.BlockSpec((parts // steps, 1, weights.shape[2]), lambda i: (i, 0, 0)),
            whole,
            whole,
            fixed(direction),
            fixed(targets),
        ],
        out_specs=(
            pl.BlockSpec((1, count), lambda i: (0, 0)),
            pl.BlockSpec((parts, 1, width), lambda i: (0, 0, 0)),
        ),
        out_shape=(
            jax.ShapeDtypeStruct((1, count), f32),
            jax.ShapeDtypeStruct((parts, 1, width), f32),
        ),
        scratch_shapes=[pltpu.VMEM((count, 2 * dim), bf16), pltpu.VMEM((count, 128), f32)],
        compiler_params=grant(55),
        name="kernel_rows",
    )(ids, points, others, weights, old_full, columns, direction, targets)


def gain_kernel(
    old_inverse_in, cross_in, schur_in, old_full, columns, gain, old_inverse, cross_low, schur_inverse, sems
):
    mover = Mover(sems)
    copies = [
        mover.start(old_inverse_in, old_inverse),
        mover.start(cross_in, cross_low),
        mover.start(schur_in, schur_inverse),
    ]
    size = cross_low.shape[0]
    arrive(copies[0])
    up = three_dot(old_full[...], old_inverse[...], ((1,), (1,)))
    arrive(copies[1])
    rest = columns[...] - three_dot(up, cross_low[...], ((1,), (0,)))
    arrive(copies[2])
    middle = three_dot(rest, schur_inverse[...], ((1,), (1,)))
    gain[:, size:] = three_dot(middle, schur_inverse[...], ((1,), (0,)))
    rest = up - three_dot(gain[:, size:], cross_low[...], ((1,), (1,)))
    gain[:, :size] = three_dot(rest, old_inverse[...], ((1,), (0,)))


def gain_of(old_inverse, cross_low, schur_inverse, old_full, columns):
    size, count = cross_low.shape[0], columns.shape[0]
    return pl.pallas_call(
        gain_kernel,
        out_shape=jax.ShapeDtypeStruct((count, 2 * size), f32),
        in_specs=[far] * 3 + [whole] * 2,
        out_specs=whole,
        scratch_shapes=[pltpu.VMEM((size, size), f32)] * 3 + [pltpu.SemaphoreType.DMA((12,))],
        compiler_params=grant(52),
        cost_estimate=pl.CostEstimate(flops=72 * count * size**2, bytes_accessed=12 * size**2, transcendentals=0),
        name="gain",
    )(old_inverse, cross_low, schur_inverse, old_full, columns)


def tail_kernel(
    sums, mine, other, old_proj, new_proj, gain, direction, targets, answer, residual, preconditioned
):
    size = old_proj.shape[1]
    total = jnp.sum(sums[...], axis=0)
    alpha = total[:, 2 * size + 1 : 2 * size + 2] / total[:, 2 * size : 2 * size + 1]
    step = alpha * direction[...]
    answer[...] = step[0]
    left = targets[...] - alpha * (mine[...] + other[...]) - ridge_shift * step
    residual[...] = left[0]
    proj = jnp.concatenate([old_proj[...], new_proj[...]], axis=1) - alpha * total[:, : 2 * size]
    fitted = to_row(across(gain[...], proj))
    preconditioned[...] = ((left - fitted) * (1.0 / ridge_shift))[0]


def tail(*args):
    row = jax.ShapeDtypeStruct(args[1].shape[1:], f32)
    return pl.pallas_call(
        tail_kernel,
        out_shape=(row,) * 3,
        in_specs=[whole] * len(args),
        out_specs=(whole,) * 3,
        compiler_params=grant(52),
        name="tail",
    )(*args)


def exchange(pieces, axes):
    return lax.all_to_all(pieces, axes, 0, 0, tiled=True)


def swap(value):
    return lax.ppermute(value, "sub", [(0, 1), (1, 0)])


def local(points, old_factor, targets, pivots):
    count, dim = points.shape
    size = pivots.shape[0]
    part = lax.axis_index("sub")
    chips = lax.axis_size("rows")
    parts = 2 * chips
    each = size // chips
    cols = old_factor.shape[1]
    first = lax.axis_index("rows") * count
    ids = jnp.stack([first, part]).astype(jnp.int32)
    row = targets.reshape(1, count)

    picked, near = pick(ids, pivots.reshape(1, size), points, old_factor)
    picked, old_factor = lax.optimization_barrier((picked, old_factor))
    width = picked.shape[1]
    came = exchange(picked.reshape(chips, each, width), "rows")
    pieces, old_full = prepare(ids, old_factor, swap(old_factor))
    kept = jnp.sum(came.astype(f32), axis=0).astype(bf16)
    sent = [jnp.broadcast_to(kept[None], (chips, each, width)), pieces.reshape(chips, each, size)]
    came = exchange(jnp.concatenate(sent, axis=2), "rows").reshape(size, width + size)
    swapped = swap(came[:, dim:width])

    columns, block, gram = pivot_columns(ids, points, came, swapped, old_full, row)
    came = exchange(gram.reshape(chips, each, size + cols), "rows")
    block_inverse = factor(block)
    came, block_inverse, near = lax.optimization_barrier((came, block_inverse, near))
    others = lax.all_gather(near, "rows", axis=0, tiled=True)
    spread_gram, mine = sum_spread(came, size)
    other = swap(mine)
    mine_gram = exchange(spread_gram, "rows").reshape(size, size)
    old_inverse = old_factor_inverse(ids, mine, other)
    mine_gram, old_inverse = lax.optimization_barrier((mine_gram, old_inverse))
    other_gram = swap(mine_gram)

    cross_low, schur_inverse, old_proj, new_proj, direction, weights = core_solve(
        ids, old_inverse, block, mine_gram, other_gram, old_full, columns, row, parts
    )
    weights = exchange(weights, everyone)
    chosen = lax.dynamic_slice_in_dim(block_inverse, part * cols, cols, 0)
    new_part = dot(columns, chosen, ((1,), (1,)))
    rows, sums = kernel_rows(
        ids, points, others, near.shape[0], weights, old_full, columns, direction, row
    )
    rows, cross_low = lax.optimization_barrier((rows, cross_low))
    sums = exchange(sums, everyone)
    gain = gain_of(old_inverse, cross_low, schur_inverse, old_full, columns)
    answer, residual, preconditioned = tail(
        sums, rows, swap(rows), old_proj, new_proj, gain, direction, row
    )
    return new_part, answer, residual, preconditioned


def solution(mesh):
    in_specs = (P("rows", None), P("rows", "sub"), P("rows"), P())
    out_specs = (P("rows", "sub"), P("rows"), P("rows"), P("rows"))
    return jax.shard_map(local, mesh=mesh, in_specs=in_specs, out_specs=out_specs, check_vma=False)
```

```python
import math

import jax
import jax.numpy as jnp
from jax import lax
from jax.experimental import pallas as pl
from jax.experimental.pallas import tpu as pltpu
from jax.sharding import PartitionSpec as P

ridge_shift = 0.5
precise = lax.Precision.HIGHEST
everyone = ("rows", "sub")
f32, bf16 = jnp.float32, jnp.bfloat16
whole = pl.BlockSpec(memory_space=pltpu.VMEM)
far = pl.BlockSpec(memory_space=pltpu.HBM)
scalar = pl.BlockSpec(memory_space=pltpu.SMEM)


def grant(megabytes):
    return pltpu.CompilerParams(vmem_limit_bytes=megabytes << 20)


def dot(left, right, contract):
    return lax.dot_general(left, right, (contract, ((), ())), precision=precise, preferred_element_type=f32)


def pieces_of(value):
    high = value.astype(bf16)
    return high, (value - high.astype(f32)).astype(bf16)


def three_dot(left, right, contract):
    left_high, left_low = pieces_of(left)
    right_high, right_low = pieces_of(right)

    def one(a, b):
        return lax.dot_general(a, b, (contract, ((), ())), preferred_element_type=f32)

    return one(left_high, right_high) + (one(left_high, right_low) + one(left_low, right_high))


def narrow_dot(left, right):
    return lax.dot_general(left, right, (((1,), (1,)), ((), ())), preferred_element_type=f32)


def total(terms):
    while len(terms) > 1:
        terms = [terms[i] + terms[i + 1] if i + 1 < len(terms) else terms[i] for i in range(0, len(terms), 2)]
    return terms[0]

def factor_block(a, hook):
    lane = lax.broadcasted_iota(jnp.int32, (8, 128), 1)
    sub = lax.broadcasted_iota(jnp.int32, (8, 128), 0)
    full = lambda v: jnp.broadcast_to(v, (8, 128))
    rows = [a[8 * i:8 * i + 8] for i in range(16)]
    outs, pending = [], []
    def drain(n):
        for _ in range(min(n, len(pending))):
            pending.pop(0)()
    for panel in range(16):
        lo = 8 * panel
        inside = (lane >= lo) & (lane < lo + 8)
        head = rows[panel]
        cols = [full(head[:, lo + j:lo + j + 1]) for j in range(8)]
        e = {(i, j): full(cols[j][i:i + 1]) for j in range(8) for i in range(j, 8)}
        head = jnp.where(inside, (lane == lo + sub).astype(f32), head)
        base = [full(head[j:j + 1]) for j in range(8)]
        per = -(-len(pending) // 5)
        m, pieces = {}, {}
        for j in (0, 2, 4, 6):
            p, q, s = e[j, j], e[j + 1, j], e[j + 1, j + 1]
            rdet = 1.0 / (p * s - q * q)
            pieces[j] = (p, q, s, rdet)
            g = {}
            for i in range(j + 2, 8):
                x, y = e[i, j], e[i, j + 1]
                g[i] = (x * s - y * q, y * p - x * q)
            for i in range(j + 2, 8):
                for k in range(j + 2, i + 1):
                    e[i, k] = e[i, k] - (g[i][0] * e[k, j] + g[i][1] * e[k, j + 1]) * rdet
            for i in range(j + 2, 8):
                f0, f1 = g[i][0] * rdet, g[i][1] * rdet
                for k in range(j):
                    m[i, k] = m[i, k] - (f0 * m[j, k] + f1 * m[j + 1, k])
                m[i, j], m[i, j + 1] = -f0, -f1
            drain(per)
            if j == 2:
                hook(panel)
        h = [total([base[i]] + [m[i, k] * base[k] for k in range(i - i % 2)]) for i in range(8)]
        y = []
        for j in (0, 2, 4, 6):
            p, q, s, rdet = pieces[j]
            y.append((s * h[j] - q * h[j + 1]) * rdet)
            y.append((p * h[j + 1] - q * h[j]) * rdet)
        G = [total([y[l]] + [m[i, l] * y[i] for i in range(l - l % 2 + 2, 8)]) for l in range(8)]
        drain(len(pending))
        if panel < 15:
            r = rows[panel + 1]
            c = total([full(r[:, lo + j:lo + j + 1]) * G[j] for j in range(8)])
            rows[panel + 1] = jnp.where(inside, 0.0, r) - c
        if panel < 14:
            g = G[7]
            for l in range(7):
                g = jnp.where(sub == l, G[l], g)
            parts = ([jnp.zeros((lo, 128), f32)] if panel else []) + [g, jnp.zeros((120 - lo, 128), f32)]
            upd = dot(jnp.concatenate(rows[panel + 2:], 0), jnp.concatenate(parts, 0), ((1,), (0,)))

            def use(i, upd=upd, first=panel + 2, inside=inside):
                rows[i] = jnp.where(inside, 0.0, rows[i]) - upd[8 * (i - first):8 * (i - first) + 8]

            for i in range(panel + 2, 16):
                pending.append(lambda i=i, u=use: u(i))
        out = jnp.zeros((8, 128), f32)
        for j in (0, 2, 4, 6):
            p, q, s, rdet = pieces[j]
            rp = 1.0 / p
            out = jnp.where(sub == j, h[j] * lax.rsqrt(p), out)
            out = jnp.where(sub == j + 1, (h[j + 1] - (q * rp) * h[j]) * lax.rsqrt(s - q * (q * rp)), out)
        outs.append(out)
    low = lax.broadcasted_iota(jnp.int32, (128, 128), 0) >= lax.broadcasted_iota(jnp.int32, (128, 128), 1)
    return jnp.where(low, jnp.concatenate(outs, 0), 0.0)

def chol_inverse(ref, left, block, inverse):
    size = ref.shape[0]
    blocks = size // 128
    row = lax.broadcasted_iota(jnp.int32, (size, 128), 0)
    lane = lax.broadcasted_iota(jnp.int32, (128, size), 1)
    block[...] = ref[:128, :128]
    inverse[...] = jnp.zeros_like(inverse)

    def finish(here, off):
        inside = (lane >= off) & (lane < off + 128)
        return dot(inverse[...], jnp.where(inside, 0.0, ref[here, :]), ((1,), (0,)))

    def step(k, carry):
        off = pl.multiple_of(k * 128, 128)
        prev = pl.multiple_of(jnp.maximum(off - 128, 0), 128)
        here, before = pl.ds(off, 128), pl.ds(prev, 128)

        def hook(panel):
            if panel == 0:
                value = dot(ref[:, before], inverse[...], ((1,), (1,)))
                left[...] = jnp.where((row >= off) & (off > 0), value, 0.0)
            elif panel == 2:
                ref[before, :] = jnp.where(off > 0, finish(before, prev), ref[before, :])
                ref[before, before] = jnp.where(off > 0, inverse[...], ref[before, before])
            elif panel % 3 == 1 and panel // 3 - 1 in range(blocks):
                c = panel // 3 - 1
                lanes = slice(128 * c, 128 * c + 128)
                gone = (off > 0) & (prev == 128 * c)
                old = ref[:, lanes]
                upd = dot(left[...], ref[before, lanes], ((1,), (0,)))
                ref[:, lanes] = jnp.where(row >= off, jnp.where(gone, 0.0, old) - upd, old)

        value = factor_block(block[...], hook)
        after = pl.multiple_of(jnp.minimum(off + 128, size - 128), 128)
        after = pl.ds(after, 128)
        part = dot(ref[after, here], value, ((1,), (1,)))
        block[...] = ref[after, after] - dot(part, part, ((1,), (1,)))
        inverse[...] = value
        return carry

    lax.fori_loop(0, blocks, step, 0)
    last = slice(size - 128, size)
    ref[last, :] = finish(last, size - 128)
    ref[last, last] = inverse[...]
    rows = lax.broadcasted_iota(jnp.int32, (size, size), 0)
    lanes = lax.broadcasted_iota(jnp.int32, (size, size), 1)
    ref[...] = jnp.where(rows >= lanes, ref[...], 0.0)


def factor_scratch(size):
    return [pltpu.VMEM((size, 128), f32), pltpu.VMEM((128, 128), f32), pltpu.VMEM((128, 128), f32)]


class Mover:
    def __init__(self, sems):
        self.sems, self.used = sems, 0

    def plan(self, source, target, pieces=4):
        rows = source.shape[0] // pieces
        copies = []
        for k in range(pieces):
            here = pl.ds(k * rows, rows)
            copies.append(pltpu.make_async_copy(source.at[here], target.at[here], self.sems.at[self.used]))
            self.used += 1
        return copies

    def start(self, source, target, pieces=4):
        copies = self.plan(source, target, pieces)
        for copy in copies:
            copy.start()
        return copies


def arrive(copies):
    for copy in copies:
        copy.wait()


def factor_kernel(matrix, out, work, left, block, inverse, sems):
    mover = Mover(sems)
    arrive(mover.start(matrix, work))
    chol_inverse(work, left, block, inverse)
    arrive(mover.start(work, out))


def factor(matrix):
    size = matrix.shape[0]
    return pl.pallas_call(
        factor_kernel,
        out_shape=jax.ShapeDtypeStruct(matrix.shape, f32),
        in_specs=[far],
        out_specs=far,
        scratch_shapes=[pltpu.VMEM((size, size), f32)] + factor_scratch(size) + [pltpu.SemaphoreType.DMA((8,))],
        compiler_params=grant(57),
        cost_estimate=pl.CostEstimate(flops=120 * size**3, bytes_accessed=8 * size**2, transcendentals=0),
        name="factor",
    )(matrix)


def old_factor_kernel(ids, mine, other, out, work, left, block, inverse, sems):
    size, cols = work.shape[0], mine.shape[1]
    first = ids[1] == 0
    work[:, :cols] = jnp.where(first, mine[...], other[...])
    work[:, cols:] = jnp.where(first, other[...], mine[...])
    work[...] = work[...] + ridge(size)
    chol_inverse(work, left, block, inverse)
    arrive(Mover(sems).start(work, out))


def old_factor_inverse(ids, mine, other):
    size = mine.shape[0]
    return pl.pallas_call(
        old_factor_kernel,
        out_shape=jax.ShapeDtypeStruct((size, size), f32),
        in_specs=[scalar, whole, whole],
        out_specs=far,
        scratch_shapes=[pltpu.VMEM((size, size), f32)] + factor_scratch(size) + [pltpu.SemaphoreType.DMA((4,))],
        compiler_params=grant(55),
        cost_estimate=pl.CostEstimate(flops=120 * size**3, bytes_accessed=8 * size**2, transcendentals=0),
        name="old_factor",
    )(ids, mine, other)


def ridge(size):
    eye = lax.broadcasted_iota(jnp.int32, (size, size), 0) == lax.broadcasted_iota(jnp.int32, (size, size), 1)
    return jnp.where(eye, ridge_shift, 0.0)


def sum_kernel(came, out, half, work, sems):
    width = work.shape[2]
    work[...] = jnp.broadcast_to(jnp.sum(came[:, :, :width], axis=0)[None], work.shape)
    copies = Mover(sems).start(work, out)
    half[...] = came[:, :, width:].reshape(half.shape)
    arrive(copies)


def sum_spread(came, size):
    chips, each, width = came.shape
    square = (chips, each, size)
    return pl.pallas_call(
        sum_kernel,
        out_shape=(
            jax.ShapeDtypeStruct(square, f32),
            jax.ShapeDtypeStruct((chips * each, width - size), f32),
        ),
        in_specs=[whole],
        out_specs=(far, whole),
        scratch_shapes=[pltpu.VMEM(square, f32), pltpu.SemaphoreType.DMA((4,))],
        compiler_params=grant(24),
        name="sum_spread",
    )(came)


def pick_kernel(ids, pivots, points_in, mine_in, picked, near, points, mine, sems):
    mover = Mover(sems)
    copies = mover.start(points_in, points) + mover.start(mine_in, mine)
    size, count = pivots.shape[1], points.shape[0]
    dim = points.shape[1]
    first = ids[1] == 0
    places = ids[0] + lax.broadcasted_iota(jnp.int32, (size, count), 1)
    wanted_ids = jnp.concatenate([to_column(pivots[...].astype(f32))] * (count // 128), axis=1)
    picks = jnp.where(wanted_ids == places.astype(f32), 1.0, 0.0).astype(bf16)
    arrive(copies)
    wanted = jnp.concatenate([points[...], mine[...].astype(bf16)], axis=1)
    rows = lax.dot_general(picks, wanted, (((1,), (0,)), ((), ())), preferred_element_type=f32)
    picked[...] = rows.astype(bf16)

    half = count // 2
    wide = jnp.where(first, points[:half].astype(f32), points[half:].astype(f32))
    rest = to_row(-0.5 * jnp.sum(wide * wide, axis=1, keepdims=True))
    near[:half] = wide.astype(bf16)
    pieces = []
    for _ in range(3):
        piece = rest.astype(bf16).astype(f32)
        pieces += [piece[:, k : k + dim] for k in range(0, half, dim)]
        rest = rest - piece
    pieces.append(jnp.zeros((16 - len(pieces), dim), f32))
    near[half:] = jnp.concatenate(pieces, axis=0).astype(bf16)


def pick(ids, pivots, points, mine):
    size, count, dim = pivots.shape[1], *points.shape
    return pl.pallas_call(
        pick_kernel,
        out_shape=(
            jax.ShapeDtypeStruct((size, dim + mine.shape[1]), bf16),
            jax.ShapeDtypeStruct((count // 2 + 16, dim), bf16),
        ),
        in_specs=[scalar, whole, far, far],
        out_specs=(whole,) * 2,
        scratch_shapes=[
            pltpu.VMEM(points.shape, bf16),
            pltpu.VMEM(mine.shape, f32),
            pltpu.SemaphoreType.DMA((8,)),
        ],
        compiler_params=grant(56),
        name="pick",
    )(ids, pivots, points, mine)


def prepare_kernel(ids, mine, other, pieces, old_full):
    cols = mine.shape[1]
    first = ids[1] == 0
    old_full[:, :cols] = jnp.where(first, mine[...], other[...])
    old_full[:, cols:] = jnp.where(first, other[...], mine[...])
    high, low = pieces_of(dot(old_full[...], mine[...], ((0,), (0,))))
    pieces[:, :cols] = high
    pieces[:, cols:] = low


def prepare(ids, mine, other):
    count, cols = mine.shape
    return pl.pallas_call(
        prepare_kernel,
        out_shape=(
            jax.ShapeDtypeStruct((2 * cols, 2 * cols), bf16),
            jax.ShapeDtypeStruct((count, 2 * cols), f32),
        ),
        in_specs=[scalar] + [whole] * 2,
        out_specs=(whole, whole),
        compiler_params=grant(24),
        cost_estimate=pl.CostEstimate(flops=24 * count * cols**2, bytes_accessed=16 * count * cols, transcendentals=0),
        name="prepare",
    )(ids, mine, other)


def to_column(row):
    blocks = [
        jnp.transpose(jnp.broadcast_to(row[:, k : k + 128], (128, 128)))
        for k in range(0, row.shape[1], 128)
    ]
    return jnp.concatenate(blocks, axis=0)


def to_row(column):
    blocks = [
        jnp.transpose(jnp.broadcast_to(column[k : k + 128], (128, 128)))[:1]
        for k in range(0, column.shape[0], 128)
    ]
    return jnp.concatenate(blocks, axis=1)


def columns_kernel(
    ids, points, came, swapped, old_full, targets, columns, block_out, gram_out, block, gram, sems
):
    mover = Mover(sems)
    first = ids[1] == 0
    dim = points.shape[1]
    size = came.shape[0]
    cols = size // 2
    rate = -2.0 / dim
    pivot_points = came[:, :dim]
    wide = points[...].astype(f32)
    pivot_wide = pivot_points.astype(f32)
    squares = pivot_wide * pivot_wide
    norms = jnp.sum(wide * wide, axis=1, keepdims=True)
    pivot_column = jnp.sum(squares, axis=1, keepdims=True)
    pivot_row = dot(jnp.ones((8, dim), f32), squares, ((1,), (1,)))[:1]
    inner = narrow_dot(points[...], pivot_points)
    values = jnp.exp(rate * jnp.maximum(norms + pivot_row - 2.0 * inner, 0.0))
    mine, other = came[:, dim : dim + cols], swapped[...]
    pivot_old = jnp.concatenate(
        [jnp.where(first, mine, other), jnp.where(first, other, mine)], axis=1
    )
    high, low = pieces_of(old_full[...])
    values = values - (narrow_dot(high, pivot_old) + narrow_dot(low, pivot_old))
    columns[...] = values
    inner = narrow_dot(pivot_points, pivot_points)
    square = jnp.exp(rate * jnp.maximum(pivot_column + pivot_row - 2.0 * inner, 0.0))
    square = square - narrow_dot(pivot_old, pivot_old)
    block[...] = square + ridge(size)
    copies = mover.start(block, block_out)

    kept = jnp.sum(came[:, dim + cols :].astype(f32).reshape(size // 8, 8, size), axis=0)
    kept = kept[:, :cols] + kept[:, cols:]
    gram[:, size:] = jnp.broadcast_to(kept[None], (size // 8, 8, cols)).reshape(size, cols)

    row = jnp.broadcast_to(targets[...], (8, targets.shape[1]))
    old_proj = dot(row, old_full[...], ((1,), (0,)))
    new_proj = dot(row, columns[...], ((1,), (0,)))
    side = jnp.where(first, old_full[...], columns[...])
    for k in range(0, size, 128):
        here = slice(k, k + 128)
        gram[here, :size] = dot(side[:, here], columns[...], ((0,), (0,)))
        if k + 128 == size:
            for at, value in ((size - 4, old_proj), (size - 2, new_proj)):
                for place, lanes in ((at, slice(0, cols)), (at + 1, slice(cols, size))):
                    kept = gram[place : place + 1, :cols]
                    gram[place : place + 1, :cols] = jnp.where(first, kept, value[:1, lanes])
        copies += mover.start(gram.at[here], gram_out.at[here], 1)
    arrive(copies)


def pivot_columns(ids, points, came, swapped, old_full, targets):
    count, size = points.shape[0], came.shape[0]
    square = jax.ShapeDtypeStruct((size, size), f32)
    wide = jax.ShapeDtypeStruct((size, size + size // 2), f32)
    return pl.pallas_call(
        columns_kernel,
        out_shape=(jax.ShapeDtypeStruct((count, size), f32), square, wide),
        in_specs=[scalar] + [whole] * 5,
        out_specs=(whole, far, far),
        scratch_shapes=[
            pltpu.VMEM(square.shape, f32),
            pltpu.VMEM(wide.shape, f32),
            pltpu.SemaphoreType.DMA((8,)),
        ],
        compiler_params=grant(53),
        name="pivot_columns",
    )(ids, points, came, swapped, old_full, targets)


def across(matrix, row):
    return jnp.sum(matrix * row, axis=1, keepdims=True)


def down(matrix, column):
    return jnp.sum(matrix * column, axis=0, keepdims=True)


def solve(old_inverse, cross_low, schur_inverse, old_side, new_side):
    up = across(old_inverse[...], old_side)
    middle = across(schur_inverse[...], new_side - down(cross_low[...], up))
    new_coef = down(schur_inverse[...], middle)
    old_coef = down(old_inverse[...], up - across(cross_low[...], new_coef))
    return old_coef, new_coef


def fit(coefs, old_full, columns):
    return across(old_full[...], coefs[0]) + across(columns[...], coefs[1])


def core_kernel(
    ids, old_inverse_in, block_in, mine, other, old_full, columns, targets,
    cross_out, schur_out, old_proj, new_proj, direction, weights,
    old_inverse, block, cross_low, schur_inverse, left, part, inverse, sems,
):
    mover = Mover(sems)
    first_copy = mover.start(old_inverse_in, old_inverse)
    second_copy = mover.start(block_in, block)
    size = block.shape[0]
    mid = size // 2
    first = ids[1] == 0
    cross = jnp.where(first, mine[...], other[...])
    schur_inverse[...] = jnp.where(first, other[...], mine[...])
    for at, value in ((size - 4, old_proj), (size - 2, new_proj)):
        value[:, :mid] = schur_inverse[at : at + 1, :mid]
        value[:, mid:] = schur_inverse[at + 1 : at + 2, :mid]
    for start in range(0, mid, 128):
        turned = jnp.transpose(schur_inverse[start : start + 128, size - 128 :])
        schur_inverse[size - 4 :, start : start + 128] = turned[124:]
    arrive(first_copy)
    cross_low[...] = dot(old_inverse[...], cross, ((1,), (0,)))
    copies = mover.start(cross_low, cross_out)
    arrive(second_copy)
    schur_inverse[...] = (
        ridge_shift * block[...]
        + schur_inverse[...]
        - dot(cross_low[...], cross_low[...], ((0,), (0,)))
    )
    chol_inverse(schur_inverse, left, part, inverse)
    copies += mover.start(schur_inverse, schur_out)
    coefs = solve(old_inverse, cross_low, schur_inverse, old_proj[...], new_proj[...])
    value = (targets[...] - to_row(fit(coefs, old_full, columns))) * (1.0 / ridge_shift)
    direction[...] = value
    half = value.shape[1] // 2
    mine_half = jnp.where(first, value[:, :half], value[:, half:])
    weights[...] = jnp.broadcast_to(mine_half[None], weights.shape)
    arrive(copies)


def core_solve(ids, old_inverse, block, mine, other, old_full, columns, targets, parts):
    size, count = block.shape[0], columns.shape[0]
    square = jax.ShapeDtypeStruct((size, size), f32)
    return pl.pallas_call(
        core_kernel,
        out_shape=(
            square,
            square,
            jax.ShapeDtypeStruct((1, size), f32),
            jax.ShapeDtypeStruct((1, size), f32),
            jax.ShapeDtypeStruct((1, count), f32),
            jax.ShapeDtypeStruct((parts, 1, count // 2), f32),
        ),
        in_specs=[scalar, far, far] + [whole] * 5,
        out_specs=(far, far) + (whole,) * 4,
        scratch_shapes=[pltpu.VMEM((size, size), f32)] * 4
        + factor_scratch(size)
        + [pltpu.SemaphoreType.DMA((16,))],
        compiler_params=grant(54),
        name="core_solve",
    )(ids, old_inverse, block, mine, other, old_full, columns, targets)


def rows_kernel(
    scale, stride, half, ids, points, others, weights, old_full, columns, direction, targets,
    rows, sums, left, acc,
):
    count, dim = points.shape
    step = pl.program_id(0)

    @pl.when(step == 0)
    def _():
        acc[...] = jnp.zeros_like(acc)
        wide = points[...].astype(f32)
        rest = -0.5 * jnp.sum(wide * wide, axis=1, keepdims=True)
        lane = lax.broadcasted_iota(jnp.int32, (count, dim), 1)
        extra = jnp.zeros((count, dim), f32)
        for k in range(3):
            piece = rest.astype(bf16).astype(f32)
            extra = jnp.where(lane == k, piece, extra)
            rest = rest - piece
        left[:, :dim] = points[...]
        left[:, dim:] = extra.astype(bf16)

    lane = lax.broadcasted_iota(jnp.int32, (256, dim), 1)
    ones = jnp.where(lane < 3, 1.0, 0.0).astype(bf16)
    groups = half // 128
    chips = others.shape[0] // stride
    total = acc[...]
    for pair in range(chips // 2):
        tiles = []
        for chip in (2 * pair, 2 * pair + 1):
            base = chip * stride
            pieces = others[base + half : base + half + 16, :].astype(f32)
            shift = scale * (pieces[:groups] + pieces[groups : 2 * groups] + pieces[2 * groups : 3 * groups])
            weight = weights[2 * chip + ids[1]]
            for g in range(groups):
                tiles.append(
                    (
                        others[base + 128 * g : base + 128 * g + 128, :],
                        shift[g : g + 1],
                        weight[:, 128 * g : 128 * g + 128],
                    )
                )
        for k in range(0, len(tiles), 2):
            one, two = tiles[k], tiles[k + 1]
            right = jnp.concatenate([jnp.concatenate([one[0], two[0]], axis=0), ones], axis=1)
            inner = narrow_dot(left[...], right) * scale
            one_value = jnp.exp2(jnp.minimum(inner[:, :128] + one[1], 0.0)) * one[2]
            two_value = jnp.exp2(jnp.minimum(inner[:, 128:] + two[1], 0.0)) * two[2]
            total = total + (one_value + two_value)
    acc[...] = total

    @pl.when(step == pl.num_programs(0) - 1)
    def _():
        mine = jnp.sum(acc[...], axis=1, keepdims=True)
        rows[...] = to_row(mine)
        image = mine + (0.5 * ridge_shift) * to_column(direction[...])[:, :1]
        size = old_full.shape[1]
        flat = (sums.shape[0], 1)
        sums[:, :, :size] = jnp.broadcast_to(down(old_full[...], image)[None], flat + (size,))
        sums[:, :, size : 2 * size] = jnp.broadcast_to(down(columns[...], image)[None], flat + (size,))
        along_image = jnp.sum(to_row(image) * direction[...], axis=1, keepdims=True)
        along_targets = 0.5 * jnp.sum(targets[...] * direction[...], axis=1, keepdims=True)
        place = lax.broadcasted_iota(jnp.int32, (1, 128), 1)
        last = jnp.where(place == 0, along_image, jnp.where(place == 1, along_targets, 0.0))
        sums[:, :, 2 * size :] = jnp.broadcast_to(last[None], flat + (128,))


def kernel_rows(ids, points, others, stride, weights, old_full, columns, direction, targets):
    count, dim = points.shape
    parts = weights.shape[0]
    chips = parts // 2
    scale = 2.0 * (2.0 / dim) * math.log2(math.e)
    steps = 8
    size = others.shape[0] // steps
    width = old_full.shape[1] + columns.shape[1] + 128

    def fixed(array):
        return pl.BlockSpec(array.shape, lambda i: (0,) * array.ndim)

    return pl.pallas_call(
        lambda *refs: rows_kernel(scale, stride, weights.shape[2], *refs),
        grid=(steps,),
        in_specs=[
            scalar,
            fixed(points),
            pl.BlockSpec((size, dim), lambda i: (i, 0)),
            pl.BlockSpec((parts // steps, 1, weights.shape[2]), lambda i: (i, 0, 0)),
            whole,
            whole,
            fixed(direction),
            fixed(targets),
        ],
        out_specs=(
            pl.BlockSpec((1, count), lambda i: (0, 0)),
            pl.BlockSpec((parts, 1, width), lambda i: (0, 0, 0)),
        ),
        out_shape=(
            jax.ShapeDtypeStruct((1, count), f32),
            jax.ShapeDtypeStruct((parts, 1, width), f32),
        ),
        scratch_shapes=[pltpu.VMEM((count, 2 * dim), bf16), pltpu.VMEM((count, 128), f32)],
        compiler_params=grant(55),
        name="kernel_rows",
    )(ids, points, others, weights, old_full, columns, direction, targets)


def gain_kernel(
    old_inverse_in, cross_in, schur_in, old_full, columns, gain, old_inverse, cross_low, schur_inverse, sems
):
    mover = Mover(sems)
    copies = [
        mover.start(old_inverse_in, old_inverse),
        mover.start(cross_in, cross_low),
        mover.start(schur_in, schur_inverse),
    ]
    size = cross_low.shape[0]
    arrive(copies[0])
    up = three_dot(old_full[...], old_inverse[...], ((1,), (1,)))
    arrive(copies[1])
    rest = columns[...] - three_dot(up, cross_low[...], ((1,), (0,)))
    arrive(copies[2])
    middle = three_dot(rest, schur_inverse[...], ((1,), (1,)))
    gain[:, size:] = three_dot(middle, schur_inverse[...], ((1,), (0,)))
    rest = up - three_dot(gain[:, size:], cross_low[...], ((1,), (1,)))
    gain[:, :size] = three_dot(rest, old_inverse[...], ((1,), (0,)))


def gain_of(old_inverse, cross_low, schur_inverse, old_full, columns):
    size, count = cross_low.shape[0], columns.shape[0]
    return pl.pallas_call(
        gain_kernel,
        out_shape=jax.ShapeDtypeStruct((count, 2 * size), f32),
        in_specs=[far] * 3 + [whole] * 2,
        out_specs=whole,
        scratch_shapes=[pltpu.VMEM((size, size), f32)] * 3 + [pltpu.SemaphoreType.DMA((12,))],
        compiler_params=grant(52),
        cost_estimate=pl.CostEstimate(flops=72 * count * size**2, bytes_accessed=12 * size**2, transcendentals=0),
        name="gain",
    )(old_inverse, cross_low, schur_inverse, old_full, columns)


def tail_kernel(
    sums, mine, other, old_proj, new_proj, gain, direction, targets, answer, residual, preconditioned
):
    size = old_proj.shape[1]
    total = jnp.sum(sums[...], axis=0)
    alpha = total[:, 2 * size + 1 : 2 * size + 2] / total[:, 2 * size : 2 * size + 1]
    step = alpha * direction[...]
    answer[...] = step[0]
    left = targets[...] - alpha * (mine[...] + other[...]) - ridge_shift * step
    residual[...] = left[0]
    proj = jnp.concatenate([old_proj[...], new_proj[...]], axis=1) - alpha * total[:, : 2 * size]
    fitted = to_row(across(gain[...], proj))
    preconditioned[...] = ((left - fitted) * (1.0 / ridge_shift))[0]


def tail(*args):
    row = jax.ShapeDtypeStruct(args[1].shape[1:], f32)
    return pl.pallas_call(
        tail_kernel,
        out_shape=(row,) * 3,
        in_specs=[whole] * len(args),
        out_specs=(whole,) * 3,
        compiler_params=grant(52),
        name="tail",
    )(*args)


def exchange(pieces, axes):
    return lax.all_to_all(pieces, axes, 0, 0, tiled=True)


def swap(value):
    return lax.ppermute(value, "sub", [(0, 1), (1, 0)])


def local(points, old_factor, targets, pivots):
    count, dim = points.shape
    size = pivots.shape[0]
    part = lax.axis_index("sub")
    chips = lax.axis_size("rows")
    parts = 2 * chips
    each = size // chips
    cols = old_factor.shape[1]
    first = lax.axis_index("rows") * count
    ids = jnp.stack([first, part]).astype(jnp.int32)
    row = targets.reshape(1, count)

    picked, near = pick(ids, pivots.reshape(1, size), points, old_factor)
    picked, old_factor = lax.optimization_barrier((picked, old_factor))
    width = picked.shape[1]
    came = exchange(picked.reshape(chips, each, width), "rows")
    pieces, old_full = prepare(ids, old_factor, swap(old_factor))
    came, pieces, old_full = lax.optimization_barrier((came, pieces, old_full))
    kept = jnp.sum(came.astype(f32), axis=0).astype(bf16)
    sent = [jnp.broadcast_to(kept[None], (chips, each, width)), pieces.reshape(chips, each, size)]
    came = exchange(jnp.concatenate(sent, axis=2), "rows").reshape(size, width + size)
    swapped = swap(came[:, dim:width])

    columns, block, gram = pivot_columns(ids, points, came, swapped, old_full, row)
    came = exchange(gram.reshape(chips, each, size + cols), "rows")
    block_inverse = factor(block)
    came, block_inverse, near = lax.optimization_barrier((came, block_inverse, near))
    others = lax.all_gather(near, "rows", axis=0, tiled=True)
    spread_gram, mine = sum_spread(came, size)
    other = swap(mine)
    mine_gram = exchange(spread_gram, "rows").reshape(size, size)
    old_inverse = old_factor_inverse(ids, mine, other)
    mine_gram, old_inverse = lax.optimization_barrier((mine_gram, old_inverse))
    other_gram = swap(mine_gram)

    cross_low, schur_inverse, old_proj, new_proj, direction, weights = core_solve(
        ids, old_inverse, block, mine_gram, other_gram, old_full, columns, row, parts
    )
    weights = exchange(weights, everyone)
    chosen = lax.dynamic_slice_in_dim(block_inverse, part * cols, cols, 0)
    new_part = dot(columns, chosen, ((1,), (1,)))
    rows, sums = kernel_rows(
        ids, points, others, near.shape[0], weights, old_full, columns, direction, row
    )
    rows, cross_low = lax.optimization_barrier((rows, cross_low))
    sums = exchange(sums, everyone)
    gain = gain_of(old_inverse, cross_low, schur_inverse, old_full, columns)
    answer, residual, preconditioned = tail(
        sums, rows, swap(rows), old_proj, new_proj, gain, direction, row
    )
    return new_part, answer, residual, preconditioned


def solution(mesh):
    in_specs = (P("rows", None), P("rows", "sub"), P("rows"), P())
    out_specs = (P("rows", "sub"), P("rows"), P("rows"), P("rows"))
    return jax.shard_map(local, mesh=mesh, in_specs=in_specs, out_specs=out_specs, check_vma=False)
```
